128 devices in a mesh: dp: 16 (over z, y_lo, core), blk: 8 (over x, y_hi).
Axes of the slice: x: 4, y: 4 (y_hi: 2, y_lo: 2; y = y_hi * 2 + y_lo), z: 4, core: 2. Of those that a mesh axis runs over, the one named last changes fastest.
Arguments:
- image_rows: bfloat16 [32, 1024, 1024], P('dp', 'blk'), may hold values from -6 to 6
- text_states: bfloat16 [128, 1024], replicated, may hold values from -6 to 6
- text_segment: int32 [128], replicated, may hold values from 0 to 7, never falling along the last dimension, each value on 1 to 32 neighbouring positions
- item_segment: int32 [32], P('dp'), may hold values from 0 to 7
- norm_gain: float32 [3, 1024], replicated, may hold values from 0.5 to 1.5
- norm_shift: float32 [3, 1024], replicated, may hold values from -2 to 2
- triple_weight: bfloat16 [1024, 3072], replicated, may hold values from -0.1875 to 0.1875
- output_weight: bfloat16 [1024, 1024], replicated, may hold values from -0.75 to 0.75
- query_weight: bfloat16 [1024, 1024], replicated, may hold values from -0.1875 to 0.1875
- memory_weight: bfloat16 [1024, 2048], replicated, may hold values from -0.1875 to 0.1875
- return_weight: bfloat16 [1024, 1024], replicated, may hold values from -0.75 to 0.75
- up_weight: bfloat16 [1024, 4096], replicated, may hold values from -0.1875 to 0.1875
- inner_bias: float32 [4096], replicated, may hold values from -2 to 2
- down_weight: bfloat16 [4096, 1024], replicated, may hold values from -0.09375 to 0.09375
- outer_bias: float32 [1024], replicated, may hold values from -2 to 2
- cotangent: bfloat16 [32, 1024, 1024], P('dp', 'blk'), may hold values from -6 to 6
Outputs:
- layer_output: bfloat16 [32, 1024, 1024], P('dp', 'blk')
- input_grad: float32 [32, 1024, 1024], P('dp', 'blk')
- text_grad: float32 [128, 1024], P(None, ('dp', 'blk'))
- gain_grad: float32 [3, 1024], P(None, ('dp', 'blk'))
- shift_grad: float32 [3, 1024], P(None, ('dp', 'blk'))
- triple_grad: float32 [1024, 3072], P(('dp', 'blk'))
- output_grad: float32 [1024, 1024], P(('dp', 'blk'))
- query_grad: float32 [1024, 1024], P(('dp', 'blk'))
- memory_grad: float32 [1024, 2048], P(('dp', 'blk'))
- return_grad: float32 [1024, 1024], P(('dp', 'blk'))
- up_grad: float32 [1024, 4096], P(('dp', 'blk'))
- inner_grad: float32 [4096], P(('dp', 'blk'))
- down_grad: float32 [4096, 1024], P(('dp', 'blk'))
- outer_grad: float32 [1024], P(('dp', 'blk'))
The draws below stay inside these ranges and needn't reach their ends.
Inputs may be any that keep to these rules, and one draw needn't show every extreme that they name: `text_segment`: caption numbers never fall along the rows; each caption has 1 to 32 rows.
All inputs are finite; a program needn't handle non-finite values.
Results may differ from the reference program's by a relative error of at most 0.035.
Values may be sent and summed in bfloat16 or wider, within the bound.
No kernel may reach another device: no remote copies, remote signals or barrier semaphores. Data moves between devices by JAX's collectives and lax.ppermute only.
A program may use at most 256 MiB of HBM per device.

```python
import math
import jax
import jax.numpy as jnp
import numpy as np
from jax import lax

D = 1024
FF = 4096
H = 16
DH = 64
SEQ = 1024
TEXT = 128
SEGS = 8
ITEMS = 32


def touch_ends(entries, key, smallest, largest):
    spot = [jax.random.randint(jax.random.fold_in(key, axis), (), 0, length) for axis, length in enumerate(entries.shape)]
    longest = entries.shape.index(max(entries.shape))
    beside = spot[:longest] + [(spot[longest] + 1) % entries.shape[longest]] + spot[longest + 1:]
    return entries.at[tuple(spot)].set(smallest).at[tuple(beside)].set(largest)


def block_scale(stream_key, extent, split, least, largest):
    level, own = 1.0, jax.random.fold_in(stream_key, 6)
    for position, blocks in split:
        steps = jnp.exp(jax.random.uniform(jax.random.fold_in(own, position), (blocks,), jnp.float32, least / len(split), largest / len(split)))
        level = level * jnp.repeat(steps, extent[position] // blocks).reshape([-1 if axis == position else 1 for axis in range(len(extent))])
    return level


def split_up(amount, total, bound, slope):
    weights = [(1 << 20) // math.isqrt(standing ** slope) + 1 for standing in range(2, amount + 1)]
    surplus, holding = total - bound - (amount - 1), [1] * (amount - 1)
    while surplus > 0:
        movable = [i for i in range(amount - 1) if holding[i] < bound]
        pool, budget = sum([weights[i] for i in movable]), surplus
        for i in movable:
            extra = min(bound - holding[i], max(1, budget * weights[i] // pool), surplus)
            holding[i] = holding[i] + extra
            surplus = surplus - extra
    return np.array([bound] + holding)


def ragged(rng, count, total, reach, skew):
    if count == 2:
        one = jax.random.randint(rng, (), max(1, total - reach), min(reach, total - 1) + 1)
        return jnp.stack([one, total - one])
    sizes = jnp.asarray(split_up(count, total, reach, skew), jnp.int32)
    twos = (count - 1) // 2
    giver, receiver = sizes[1:1 + 2 * twos:2], sizes[2:2 + 2 * twos:2]
    margin = jnp.minimum(giver - 1, reach - receiver)
    moved = jax.random.randint(jax.random.fold_in(rng, 1), (twos,), 0, 1 << 20) % (margin + 1)
    sizes = sizes.at[1:1 + 2 * twos:2].set(giver - moved).at[2:2 + 2 * twos:2].set(receiver + moved)
    return sizes[jax.random.permutation(jax.random.fold_in(rng, 2), count)]


def gaussian(rng, extent, width, most, pieces=(), held_as=jnp.bfloat16):
    loudness = block_scale(rng, extent, pieces, -0.22, 0.18) if pieces else 1.0
    values = jax.random.normal(rng, extent, jnp.float32) * width * loudness
    return jnp.minimum(jnp.maximum(values, -most), most).astype(held_as)


def setup_inputs(seed: int = 0) -> dict:
    seeds = jax.random.split(jax.random.key(seed), 17)
    return {
        "image_rows": gaussian(seeds[0], (ITEMS, SEQ, D), 1.0, 6.0, ((0, 16), (1, 8))),
        "text_states": gaussian(seeds[1], (TEXT, D), 1.0, 6.0),
        "text_segment": jnp.searchsorted(jnp.cumsum(ragged(seeds[2], SEGS, TEXT, TEXT // 4, 1)), jnp.arange(TEXT), side="right").astype(jnp.int32),
        "item_segment": touch_ends(jax.random.randint(seeds[3], (ITEMS,), 0, SEGS), jax.random.fold_in(seeds[3], 1), 0, SEGS - 1).astype(jnp.int32),
        "norm_gain": jnp.clip(1.0 + 0.1 * jax.random.normal(seeds[4], (3, D), jnp.float32), 0.5, 1.5),
        "norm_shift": gaussian(seeds[5], (3, D), 0.3, 2.0, (), jnp.float32),
        "triple_weight": gaussian(seeds[6], (D, 3 * D), D ** -0.5, 0.1875),
        "output_weight": gaussian(seeds[7], (D, D), (D // 16) ** -0.5, 0.75),
        "query_weight": gaussian(seeds[8], (D, D), D ** -0.5, 0.1875),
        "memory_weight": gaussian(seeds[9], (D, 2 * D), D ** -0.5, 0.1875),
        "return_weight": gaussian(seeds[10], (D, D), (D // 16) ** -0.5, 0.75),
        "up_weight": gaussian(seeds[11], (D, FF), D ** -0.5, 0.1875),
        "inner_bias": gaussian(seeds[12], (FF,), 0.3, 2.0, (), jnp.float32),
        "down_weight": gaussian(seeds[13], (FF, D), FF ** -0.5, 0.09375),
        "outer_bias": gaussian(seeds[14], (D,), 0.3, 2.0, (), jnp.float32),
        "cotangent": gaussian(seeds[15], (ITEMS, SEQ, D), 1.0, 6.0, ((0, 16), (1, 8))),
    }


@jax.custom_vjp
def low(v):
    return lax.optimization_barrier(v.astype(jnp.bfloat16)).astype(jnp.float32)

@jax.custom_vjp
def low_back(v):
    return v

def low_keep(v):
    return (low(v), None)

def low_pass(kept, grad):
    return (grad,)

def back_keep(v):
    return (v, None)

def back_low(kept, grad):
    return (low(grad),)
low.defvjp(low_keep, low_pass)
low_back.defvjp(back_keep, back_low)
epsilon = 1e-05
score_scale = 0.125
masked_value = -1e+30

def layer_norm(values, gain_row, shift_row):
    average = lax.optimization_barrier(jnp.mean(values, axis=-1, keepdims=True))
    centred = values - average
    variance = lax.optimization_barrier(jnp.mean(centred * centred, axis=-1, keepdims=True))
    return centred * lax.rsqrt(variance + epsilon) * gain_row + shift_row

def product(left, right):
    return jnp.dot(left, right, precision=lax.Precision.HIGHEST)

def item_forward(image, text, text_segment, segment, weights):
    norm_gain, norm_shift, triple_weight, output_weight, query_weight, memory_weight, return_weight, up_weight, inner_bias, down_weight, outer_bias = weights
    positions = jnp.arange(SEQ)
    causal = positions[None, :] <= positions[:, None]
    hidden_one = low(layer_norm(image, norm_gain[0], norm_shift[0]))
    triple = low_back(low(product(hidden_one, triple_weight)))
    queries = triple[:, :D].reshape(SEQ, H, DH)
    keys_all = triple[:, D:2 * D].reshape(SEQ, H, DH)
    values_all = triple[:, 2 * D:].reshape(SEQ, H, DH)
    raw = jnp.einsum('qhd,khd->hqk', queries, keys_all, precision=lax.Precision.HIGHEST) * score_scale
    scores = low_back(jnp.where(causal[None], raw, masked_value))
    probs = jax.nn.softmax(scores, axis=-1)
    attended = jnp.einsum('hqk,khd->qhd', low(probs), values_all, precision=lax.Precision.HIGHEST)
    attended = low_back(low(attended.reshape(SEQ, D)))
    after_self = image + low_back(product(attended, output_weight))
    hidden_two = low(layer_norm(after_self, norm_gain[1], norm_shift[1]))
    cross_queries = low_back(low(product(hidden_two, query_weight))).reshape(SEQ, H, DH)
    memory = low_back(low(product(text, memory_weight)))
    memory_keys = memory[:, :D].reshape(TEXT, H, DH)
    memory_values = memory[:, D:].reshape(TEXT, H, DH)
    allowed = (text_segment == segment)[None, None, :]
    cross_raw = jnp.einsum('qhd,thd->hqt', cross_queries, memory_keys, precision=lax.Precision.HIGHEST) * score_scale
    cross_scores = low_back(jnp.where(allowed, cross_raw, masked_value))
    cross_probs = jax.nn.softmax(cross_scores, axis=-1)
    cross_attended = jnp.einsum('hqt,thd->qhd', low(cross_probs), memory_values, precision=lax.Precision.HIGHEST)
    cross_attended = low_back(low(cross_attended.reshape(SEQ, D)))
    after_cross = after_self + low_back(product(cross_attended, return_weight))
    hidden_three = low(layer_norm(after_cross, norm_gain[2], norm_shift[2]))
    lifted = low_back(product(hidden_three, up_weight) + inner_bias)
    activated = low_back(low(jax.nn.gelu(lifted)))
    return after_cross + low_back(product(activated, down_weight)) + outer_bias

def reference(image_rows, text_states, text_segment, item_segment, norm_gain, norm_shift, triple_weight, output_weight, query_weight, memory_weight, return_weight, up_weight, inner_bias, down_weight, outer_bias, cotangent):
    weights = (norm_gain.astype(jnp.float32), norm_shift.astype(jnp.float32), triple_weight.astype(jnp.float32), output_weight.astype(jnp.float32), query_weight.astype(jnp.float32), memory_weight.astype(jnp.float32), return_weight.astype(jnp.float32), up_weight.astype(jnp.float32), inner_bias.astype(jnp.float32), down_weight.astype(jnp.float32), outer_bias.astype(jnp.float32))
    text_full = text_states.astype(jnp.float32)

    def one_item(totals, inputs):
        image, grad_out, segment = inputs

        def forward(image_value, text_value, weight_values):
            return item_forward(image_value, text_value, text_segment, segment, weight_values)
        output, pull = jax.vjp(forward, image.astype(jnp.float32), text_full, weights)
        image_grad, text_part, weight_grads = pull(grad_out.astype(jnp.float32))
        totals = jax.tree.map(lambda left, right: left + right, totals, (text_part, weight_grads))
        return (totals, (output.astype(jnp.bfloat16), image_grad))
    zeros = jax.tree.map(jnp.zeros_like, (text_full, weights))
    totals, outputs = lax.scan(one_item, zeros, (image_rows, cotangent, item_segment))
    layer_output, input_grad = outputs
    text_grad, grads = totals
    return (layer_output, input_grad, text_grad, grads[0], grads[1], grads[2], grads[3], grads[4], grads[5], grads[6], grads[7], grads[8], grads[9], grads[10])
```

```python
import functools

import jax
import jax.numpy as jnp
from jax import lax
from jax.experimental import pallas as pl
from jax.experimental.pallas import tpu as pltpu
from jax.sharding import Mesh, PartitionSpec as P

DH = 64
EPS = 1e-05
SCALE = 0.125
MASKED = -1e30
BF = jnp.bfloat16
F32 = jnp.float32
MIB = 1 << 20

BLK = ("x", "yh")
ALL = ("z", "yl", "c", "x", "yh")


def dot(a, b, ca=1, cb=0):
    return lax.dot_general(a, b, (((ca,), (cb,)), ((), ())), preferred_element_type=F32)


def cost(flops, nbytes, trans=0):
    return pl.CostEstimate(flops=int(flops), bytes_accessed=int(nbytes), transcendentals=int(trans))


def params(mib):
    return pltpu.CompilerParams(vmem_limit_bytes=mib * MIB)


SMEM = pl.BlockSpec(memory_space=pltpu.SMEM)


def whole(shape):
    return pl.BlockSpec(shape, lambda *_: (0,) * len(shape))


def normalise(v):
    mean = jnp.mean(v, axis=-1, keepdims=True)
    centred = v - mean
    var = jnp.mean(centred * centred, axis=-1, keepdims=True)
    rstd = lax.rsqrt(var + EPS)
    return centred * rstd, rstd


def norm_back(dy, xhat, rstd, gain):
    dx = dy * gain
    m1 = jnp.mean(dx, axis=-1, keepdims=True)
    m2 = jnp.mean(dx * xhat, axis=-1, keepdims=True)
    back = rstd * (dx - m1 - xhat * m2)
    dgain = jnp.sum(dy * xhat, axis=0, keepdims=True)
    dshift = jnp.sum(dy, axis=0, keepdims=True)
    return back, dgain, dshift


def triple_body(x_ref, g_ref, s_ref, perm_ref, wq_ref, wk_ref, wv_ref, p_ref, hm_ref, ht_ref, h_scr):
    @pl.when(pl.program_id(0) == 0)
    def _():
        xhat, _ = normalise(x_ref[...].astype(F32))
        h = (xhat * g_ref[...] + s_ref[...]).astype(BF)
        h_scr[...] = h
        hp = dot(h, perm_ref[...]).astype(BF)
        half = hp.shape[1] // 2
        hm_ref[...] = hp[:, :half]
        ht_ref[...] = hp[:, half:]

    h = h_scr[...]
    for i, w in enumerate((wq_ref, wk_ref, wv_ref)):
        r = dot(h, w[...]).astype(BF)
        p_ref[0, :, i * 128 : (i + 1) * 128] = r[:, :128]
        p_ref[1, :, i * 128 : (i + 1) * 128] = r[:, 128:]


def triple_forward(x, gain, shift, perm, w):
    t, d = x.shape
    n = d // 256
    return pl.pallas_call(
        triple_body,
        grid=(n,),
        in_specs=[
            whole((t, d)),
            whole((1, d)),
            whole((1, d)),
            whole((d, d)),
            pl.BlockSpec((d, 256), lambda j: (0, j)),
            pl.BlockSpec((d, 256), lambda j: (0, n + j)),
            pl.BlockSpec((d, 256), lambda j: (0, 2 * n + j)),
        ],
        out_specs=[
            pl.BlockSpec((2, t, 384), lambda j: (j, 0, 0)),
            whole((t, d // 2)),
            whole((t, d // 2)),
        ],
        out_shape=[
            jax.ShapeDtypeStruct((d // 128, t, 384), BF),
            jax.ShapeDtypeStruct((t, d // 2), BF),
            jax.ShapeDtypeStruct((t, d // 2), BF),
        ],
        scratch_shapes=[pltpu.VMEM((t, d), BF)],
        compiler_params=params(32),
        cost_estimate=cost(2 * t * d * 4 * d, 10 * MIB),
        name="triple_forward",
    )(x, gain, shift, perm, w, w, w)


def head_lanes(shape, h):
    return (lax.broadcasted_iota(jnp.int32, shape, 1) // DH) == h


def masked_head(v, h):
    return jnp.where(head_lanes(v.shape, h), v, 0.0).astype(BF)


def probs_t(k, qh, qb):
    kv = 256 * (qb + 1)
    st = dot(k[:kv], qh, 1, 1)
    kpos = lax.broadcasted_iota(jnp.int32, (256, 256), 0)
    qpos = lax.broadcasted_iota(jnp.int32, (256, 256), 1)
    last = jnp.where(kpos <= qpos, st[kv - 256 :], MASKED)
    st = jnp.concatenate([st[: kv - 256], last], axis=0) if qb else last
    top = jnp.max(st, axis=0, keepdims=True)
    e = jnp.exp(st - top)
    return e * (1.0 / jnp.sum(e, axis=0, keepdims=True))


def attend_body(p_ref, o_ref):
    rows = p_ref.shape[0] * p_ref.shape[2]
    k = p_ref[:, 0, :, 128:256].reshape(rows, 128)
    v = p_ref[:, 0, :, 256:384].reshape(rows, 128)
    vt = v.T
    for qb in range(rows // 256):
        q = p_ref[2 * qb : 2 * qb + 2, 0, :, 0:128].reshape(256, 128).astype(F32) * SCALE
        kv = 256 * (qb + 1)
        parts = []
        for h in range(2):
            a = probs_t(k, masked_head(q, h), qb).astype(BF)
            parts.append(dot(vt[h * DH : (h + 1) * DH, :kv], a))
        o = jnp.concatenate(parts, axis=0).T.astype(BF)
        o_ref[2 * qb : 2 * qb + 2, 0] = o.reshape(2, 128, 128)


def attend(p):
    b, items, r, _ = p.shape
    return pl.pallas_call(
        attend_body,
        grid=(items,),
        in_specs=[pl.BlockSpec((b, 1, r, 384), lambda i: (0, i, 0, 0))],
        out_specs=pl.BlockSpec((b, 1, r, 128), lambda i: (0, i, 0, 0)),
        out_shape=jax.ShapeDtypeStruct((b, items, r, 128), BF),
        compiler_params=params(32),
        cost_estimate=cost(2 * items * 2 * 10 * 65536 * 128 * 2, 3 * MIB, 4 * 655360),
        name="attend",
    )(p)


def attend_back_body(p_ref, do_ref, dp_ref, dk_scr, dv_scr):
    rows = p_ref.shape[0] * p_ref.shape[2]
    blocks = p_ref.shape[0]
    k = p_ref[:, 0, :, 128:256].reshape(rows, 128)
    v = p_ref[:, 0, :, 256:384].reshape(rows, 128)
    kt = k.T
    dk_scr[...] = jnp.zeros_like(dk_scr)
    dv_scr[...] = jnp.zeros_like(dv_scr)
    for qb in range(rows // 256):
        q = p_ref[2 * qb : 2 * qb + 2, 0, :, 0:128].reshape(256, 128).astype(F32) * SCALE
        do = do_ref[2 * qb : 2 * qb + 2, 0].reshape(256, 128).astype(F32)
        kv = 256 * (qb + 1)
        parts = []
        for h in range(2):
            qh = masked_head(q, h)
            doh = masked_head(do, h)
            a = probs_t(k, qh, qb)
            da = dot(v[:kv], doh, 1, 1)
            dots = jnp.sum(a * da, axis=0, keepdims=True)
            ds = (a * (da - dots)).astype(BF)
            dv_scr[:kv] += dot(a.astype(BF), doh)
            dk_scr[:kv] += dot(ds, qh)
            parts.append(dot(kt[h * DH : (h + 1) * DH, :kv], ds))
        dq = (jnp.concatenate(parts, axis=0) * SCALE).T.astype(BF)
        dp_ref[2 * qb : 2 * qb + 2, 0, :, 0:128] = dq.reshape(2, 128, 128)
    dp_ref[:, 0, :, 128:256] = dk_scr[...].astype(BF).reshape(blocks, -1, 128)
    dp_ref[:, 0, :, 256:384] = dv_scr[...].astype(BF).reshape(blocks, -1, 128)


def attend_back(p, do):
    b, items, r, _ = p.shape
    return pl.pallas_call(
        attend_back_body,
        grid=(items,),
        in_specs=[
            pl.BlockSpec((b, 1, r, 384), lambda i: (0, i, 0, 0)),
            pl.BlockSpec((b, 1, r, 128), lambda i: (0, i, 0, 0)),
        ],
        out_specs=pl.BlockSpec((b, 1, r, 384), lambda i: (0, i, 0, 0)),
        out_shape=jax.ShapeDtypeStruct((b, items, r, 384), BF),
        scratch_shapes=[pltpu.VMEM((b * r, 128), F32), pltpu.VMEM((b * r, 128), F32)],
        compiler_params=params(40),
        cost_estimate=cost(2 * items * 5 * 10 * 65536 * 128 * 2, 5 * MIB, 4 * 655360),
        name="attend_back",
    )(p, do)


def stack_heads(v, items):
    r = v.shape[0] // items
    parts = []
    for i in range(items):
        for h in range(2):
            parts.append(masked_head(v[i * r : (i + 1) * r], h))
    return jnp.concatenate(parts, axis=0)


def unstack_heads(v, items):
    r = v.shape[0] // (2 * items)
    parts = []
    for i in range(items):
        first = v[(2 * i) * r : (2 * i + 1) * r]
        second = v[(2 * i + 1) * r : (2 * i + 2) * r]
        parts.append(jnp.where(head_lanes(first.shape, 0), first, second))
    return jnp.concatenate(parts, axis=0)


def cross_probs_t(mk, q4, allowed):
    st = jnp.where(allowed, dot(mk, q4, 1, 1), MASKED)
    top = jnp.max(st, axis=0, keepdims=True)
    e = jnp.exp(st - top)
    return e * (1.0 / jnp.sum(e, axis=0, keepdims=True))


def allowed_mask(tseg_ref, iseg_ref, items, r):
    seg = tseg_ref[...]
    return jnp.concatenate(
        [jnp.broadcast_to(seg == iseg_ref[i], (seg.shape[0], 2 * r)) for i in range(items)], axis=1
    )


def middle_body(
    iseg_ref, o_ref, x_ref, wo_ref, g_ref, s_ref, wq_ref, m_ref, tseg_ref, wr_ref, perm_ref,
    y1_ref, qc_ref, y2_ref, h3_ref, om_ref, ot_ref, h2m_ref, h2t_ref, ocm_ref, oct_ref, h3m_ref, h3t_ref,
    oc_scr,
):
    items = iseg_ref.shape[0]
    t, d = x_ref.shape
    r = t // items
    perm = perm_ref[...]

    def permuted(v, mine, theirs):
        vp = dot(v, perm).astype(BF)
        mine[...] = vp[:, : d // 2]
        theirs[...] = vp[:, d // 2 :]

    o = jnp.concatenate([o_ref[j] for j in range(o_ref.shape[0])], axis=1)
    permuted(o, om_ref, ot_ref)
    y1 = x_ref[...].astype(F32) + dot(o, wo_ref[...])
    y1_ref[...] = y1
    xhat, _ = normalise(y1)
    h2 = (xhat * g_ref[1:2] + s_ref[1:2]).astype(BF)
    permuted(h2, h2m_ref, h2t_ref)
    qc_ref[...] = dot(h2, wq_ref[...]).astype(BF)
    allowed = allowed_mask(tseg_ref, iseg_ref, items, r)
    for p in range(d // 128):
        at = slice(p * 128, (p + 1) * 128)
        q4 = stack_heads(qc_ref[:, at].astype(F32) * SCALE, items)
        a = cross_probs_t(m_ref[:, at], q4, allowed).astype(BF)
        o4 = dot(a, m_ref[:, d + p * 128 : d + (p + 1) * 128], 0, 0)
        oc_scr[:, at] = unstack_heads(o4, items).astype(BF)
    oc = oc_scr[...]
    permuted(oc, ocm_ref, oct_ref)
    y2 = y1 + dot(oc, wr_ref[...])
    y2_ref[...] = y2
    xhat, _ = normalise(y2)
    h3 = (xhat * g_ref[2:3] + s_ref[2:3]).astype(BF)
    h3_ref[...] = h3
    permuted(h3, h3m_ref, h3t_ref)


def middle(iseg, o, x, wo, gain, shift, wq, m, tseg, wr, perm):
    t, d = x.shape
    args = (iseg, o, x, wo, gain, shift, wq, m, tseg, wr, perm)
    half = jax.ShapeDtypeStruct((t, d // 2), BF)
    full = jax.ShapeDtypeStruct((t, d), BF)
    wide = jax.ShapeDtypeStruct((t, d), F32)
    outs = [wide, full, wide, full] + [half] * 8
    return pl.pallas_call(
        middle_body,
        in_specs=[SMEM] + [pl.BlockSpec(memory_space=pltpu.VMEM)] * 10,
        out_specs=[pl.BlockSpec(memory_space=pltpu.VMEM)] * len(outs),
        out_shape=outs,
        scratch_shapes=[pltpu.VMEM((t, d), BF)],
        compiler_params=params(40),
        cost_estimate=cost(2 * t * d * d * 7, 14 * MIB, 16 * 128 * t),
        name="middle",
    )(*args)


def mlp_body(
    c_ref, h3_ref, up_ref, ib_ref, down_ref, ob_ref, r_ref, y2_ref, g_ref,
    gm_ref, gt_ref, du_ref, inner_ref, out_ref, dy2_ref, dgain_ref, dshift_ref, outer_ref,
    y_scr, dh_scr,
):
    step = pl.program_id(0)

    @pl.when(step == 0)
    def _():
        y_scr[...] = jnp.zeros_like(y_scr)
        dh_scr[...] = jnp.zeros_like(dh_scr)

    up = up_ref[...]
    down = down_ref[...]
    cotangent = r_ref[...]
    u = dot(h3_ref[...], up) + ib_ref[...]
    dg = dot(cotangent, down, 1, 1).astype(BF).astype(F32)
    c0 = 0.7978845608028654
    c1 = 0.044715
    uu = u * u
    t = jnp.tanh(c0 * (u + c1 * (uu * u)))
    half = 0.5 * (1.0 + t)
    g = (u * half).astype(BF)
    slope = half + (0.5 * u) * (1.0 - t * t) * (c0 * (1.0 + (3.0 * c1) * uu))
    du = (slope * dg).astype(BF)
    du_ref[...] = du
    inner_ref[...] = jnp.sum(du.astype(F32), axis=0, keepdims=True)
    w = gm_ref.shape[1]
    first = c_ref[0] == 0

    @pl.when(first)
    def _():
        gm_ref[...] = g[:, :w]
        gt_ref[...] = g[:, w:]

    @pl.when(jnp.logical_not(first))
    def _():
        gm_ref[...] = g[:, w:]
        gt_ref[...] = g[:, :w]

    y_scr[...] += dot(g, down)
    dh_scr[...] += dot(du, up, 1, 1)

    @pl.when(step == pl.num_programs(0) - 1)
    def _():
        y2 = y2_ref[...]
        out_ref[...] = (y2 + y_scr[...] + ob_ref[...]).astype(BF)
        xhat, rstd = normalise(y2)
        back, dgain, dshift = norm_back(dh_scr[...], xhat, rstd, g_ref[2:3])
        cot = cotangent.astype(F32)
        dy2_ref[...] = cot + back
        dgain_ref[...] = dgain
        dshift_ref[...] = dshift
        outer_ref[...] = jnp.sum(cot, axis=0, keepdims=True)


def mlp(c, h3, up, ib, down, ob, cot, y2, gain):
    t, d = h3.shape
    ff = up.shape[1]
    tile = 512
    n = ff // tile
    row = jax.ShapeDtypeStruct((1, d), F32)
    return pl.pallas_call(
        mlp_body,
        grid=(n,),
        in_specs=[
            SMEM,
            whole((t, d)),
            pl.BlockSpec((d, tile), lambda i: (0, i)),
            pl.BlockSpec((1, tile), lambda i: (0, i)),
            pl.BlockSpec((tile, d), lambda i: (i, 0)),
            whole((1, d)),
            whole((t, d)),
            whole((t, d)),
            whole((3, d)),
        ],
        out_specs=[
            pl.BlockSpec((t, tile // 2), lambda i: (0, i)),
            pl.BlockSpec((t, tile // 2), lambda i: (0, i)),
            pl.BlockSpec((t, tile), lambda i: (0, i)),
            pl.BlockSpec((1, tile), lambda i: (0, i)),
            whole((t, d)),
            whole((t, d)),
            whole((1, d)),
            whole((1, d)),
            whole((1, d)),
        ],
        out_shape=[
            jax.ShapeDtypeStruct((t, ff // 2), BF),
            jax.ShapeDtypeStruct((t, ff // 2), BF),
            jax.ShapeDtypeStruct((t, ff), BF),
            jax.ShapeDtypeStruct((1, ff), F32),
            jax.ShapeDtypeStruct((t, d), BF),
            jax.ShapeDtypeStruct((t, d), F32),
            row,
            row,
            row,
        ],
        scratch_shapes=[pltpu.VMEM((t, d), F32), pltpu.VMEM((t, d), F32)],
        compiler_params=params(40),
        cost_estimate=cost(2 * t * d * ff * 4, 24 * MIB, t * ff),
        name="mlp",
    )(c, h3, up, ib, down, ob, cot, y2, gain)


def middle_back_body(
    iseg_ref, dy2_ref, wr_ref, qc_ref, m_ref, tseg_ref, wq_ref, y1_ref, g_ref, wo_ref,
    b2_ref, dqc_ref, b1_ref, dy1_ref, do_ref, dm_ref, dgain_ref, dshift_ref,
    doc_scr,
):
    items = iseg_ref.shape[0]
    t, d = dy2_ref.shape
    r = t // items
    dy2 = dy2_ref[...]
    b2 = dy2.astype(BF)
    b2_ref[...] = b2
    doc_scr[...] = dot(b2, wr_ref[...], 1, 1).astype(BF)
    allowed = allowed_mask(tseg_ref, iseg_ref, items, r)
    for p in range(d // 128):
        at = slice(p * 128, (p + 1) * 128)
        av = slice(d + p * 128, d + (p + 1) * 128)
        mk = m_ref[:, at]
        q4 = stack_heads(qc_ref[:, at].astype(F32) * SCALE, items)
        do4 = stack_heads(doc_scr[:, at].astype(F32), items)
        a = cross_probs_t(mk, q4, allowed)
        da = dot(m_ref[:, av], do4, 1, 1)
        dots = jnp.sum(a * da, axis=0, keepdims=True)
        ds = (a * (da - dots)).astype(BF)
        dm_ref[:, at] = dot(ds, q4)
        dm_ref[:, av] = dot(a.astype(BF), do4)
        dqc_ref[:, at] = (unstack_heads(dot(ds, mk, 0, 0), items) * SCALE).astype(BF)
    xhat, rstd = normalise(y1_ref[...])
    dh2 = dot(dqc_ref[...], wq_ref[...], 1, 1)
    back, dgain, dshift = norm_back(dh2, xhat, rstd, g_ref[1:2])
    dgain_ref[...] = dgain
    dshift_ref[...] = dshift
    dy1 = dy2 + back
    dy1_ref[...] = dy1
    b1 = dy1.astype(BF)
    b1_ref[...] = b1
    do = dot(b1, wo_ref[...], 1, 1).astype(BF)
    for j in range(do_ref.shape[0]):
        do_ref[j] = do[:, j * 128 : (j + 1) * 128]


def middle_back(iseg, dy2, wr, qc, m, tseg, wq, y1, gain, wo):
    t, d = dy2.shape
    args = (iseg, dy2, wr, qc, m, tseg, wq, y1, gain, wo)
    full = jax.ShapeDtypeStruct((t, d), BF)
    row = jax.ShapeDtypeStruct((1, d), F32)
    outs = [
        full, full, full, jax.ShapeDtypeStruct((t, d), F32), jax.ShapeDtypeStruct((d // 128, t, 128), BF),
        jax.ShapeDtypeStruct(m.shape, F32), row, row,
    ]
    return pl.pallas_call(
        middle_back_body,
        in_specs=[SMEM] + [pl.BlockSpec(memory_space=pltpu.VMEM)] * 9,
        out_specs=[pl.BlockSpec(memory_space=pltpu.VMEM)] * len(outs),
        out_shape=outs,
        scratch_shapes=[pltpu.VMEM((t, d), BF)],
        compiler_params=params(40),
        cost_estimate=cost(2 * t * d * d * 4, 14 * MIB, 16 * 128 * t),
        name="middle_back",
    )(*args)


def triple_back_body(dp_ref, wq_ref, wk_ref, wv_ref, x_ref, g_ref, dy1_ref, out_ref, dgain_ref, dshift_ref, flat_ref, acc):
    step = pl.program_id(0)
    n = pl.num_programs(0)

    @pl.when(step == 0)
    def _():
        acc[...] = jnp.zeros_like(acc)

    total = acc[...]
    for i, w in enumerate((wq_ref, wk_ref, wv_ref)):
        at = slice(i * 128, (i + 1) * 128)
        dp = jnp.concatenate([dp_ref[0, :, at], dp_ref[1, :, at]], axis=1)
        flat_ref[i] = dp
        total += dot(dp, w[...], 1, 1)
    acc[...] = total

    @pl.when(step == n - 1)
    def _():
        xhat, rstd = normalise(x_ref[...].astype(F32))
        back, dgain, dshift = norm_back(acc[...], xhat, rstd, g_ref[0:1])
        out_ref[...] = dy1_ref[...] + back
        dgain_ref[...] = dgain
        dshift_ref[...] = dshift


def triple_back(dp, w, x, gain, dy1):
    t, d = x.shape
    n = d // 256
    row = jax.ShapeDtypeStruct((1, d), F32)
    return pl.pallas_call(
        triple_back_body,
        grid=(n,),
        in_specs=[
            pl.BlockSpec((2, t, 384), lambda j: (j, 0, 0)),
            pl.BlockSpec((d, 256), lambda j: (0, j)),
            pl.BlockSpec((d, 256), lambda j: (0, n + j)),
            pl.BlockSpec((d, 256), lambda j: (0, 2 * n + j)),
            whole((t, d)),
            whole((3, d)),
            whole((t, d)),
        ],
        out_specs=[whole((t, d)), whole((1, d)), whole((1, d)), pl.BlockSpec((3, t, 256), lambda j: (0, 0, j))],
        out_shape=[
            jax.ShapeDtypeStruct((t, d), F32),
            row,
            row,
            jax.ShapeDtypeStruct((3, t, d), BF),
        ],
        scratch_shapes=[pltpu.VMEM((t, d), F32)],
        compiler_params=params(32),
        cost_estimate=cost(2 * t * d * 3 * d, 12 * MIB),
        name="triple_back",
    )(dp, w, w, w, x, gain, dy1)


def rows_grad_body(lm_ref, lp_ref, rm_ref, rp_ref, out_ref, lt_scr):
    t = lm_ref.shape[0]

    @pl.when(pl.program_id(0) == 0)
    def _():
        lt_scr[:, :t] = lm_ref[...].T
        lt_scr[:, t:] = lp_ref[...].T

    right = jnp.concatenate([rm_ref[...], rp_ref[...]], axis=0)
    out_ref[...] = dot(lt_scr[...], right).astype(BF)


def rows_grad(lm, lp, rm, rp, name):
    t, rows = lm.shape
    n = rm.shape[1]
    tile = 512
    return pl.pallas_call(
        rows_grad_body,
        grid=(n // tile,),
        in_specs=[
            whole((t, rows)),
            whole((t, rows)),
            pl.BlockSpec((t, tile), lambda j: (0, j)),
            pl.BlockSpec((t, tile), lambda j: (0, j)),
        ],
        out_specs=pl.BlockSpec((rows, tile), lambda j: (0, j)),
        out_shape=jax.ShapeDtypeStruct((rows, n), BF),
        scratch_shapes=[pltpu.VMEM((rows, 2 * t), BF)],
        compiler_params=params(32),
        cost_estimate=cost(2 * 2 * t * rows * n, 2 * (rows * n + 2 * t * n)),
        name=name,
    )(lm, lp, rm, rp)


def triple_grad_local(lm, lp, rm, rp):
    t, rows = lm.shape
    d = rm.shape[2]
    tile = 512
    per = d // tile
    return pl.pallas_call(
        rows_grad_body,
        grid=(3 * per,),
        in_specs=[
            whole((t, rows)),
            whole((t, rows)),
            pl.BlockSpec((None, t, tile), lambda j: (j // per, 0, j % per)),
            pl.BlockSpec((None, t, tile), lambda j: (j // per, 0, j % per)),
        ],
        out_specs=pl.BlockSpec((rows, tile), lambda j: (0, j)),
        out_shape=jax.ShapeDtypeStruct((rows, 3 * d), BF),
        scratch_shapes=[pltpu.VMEM((rows, 2 * t), BF)],
        compiler_params=params(32),
        cost_estimate=cost(2 * 2 * t * rows * 3 * d, 2 * (rows * 3 * d + 2 * t * 3 * d)),
        name="triple_grad_local",
    )(lm, lp, rm, rp)


def down_grad_body(gm_ref, gp_ref, rm_ref, rp_ref, out_ref):
    left = jnp.concatenate([gm_ref[...].T, gp_ref[...].T], axis=1)
    right = jnp.concatenate([rm_ref[...], rp_ref[...]], axis=0)
    out_ref[...] = dot(left, right).astype(BF).reshape(out_ref.shape)


def down_grad_local(gm, gp, rm, rp):
    t, d = rm.shape
    return pl.pallas_call(
        down_grad_body,
        grid=(4, 2),
        in_specs=[
            pl.BlockSpec((t, 256), lambda z, y: (0, 2 * z + y)),
            pl.BlockSpec((t, 256), lambda z, y: (0, 2 * z + y)),
            whole((t, d)),
            whole((t, d)),
        ],
        out_specs=pl.BlockSpec((1, 4, 2, 1, 32, d), lambda z, y: (z, 0, 0, y, 0, 0)),
        out_shape=jax.ShapeDtypeStruct((4, 4, 2, 2, 32, d), BF),
        compiler_params=params(32),
        cost_estimate=cost(2 * 2 * t * 2048 * d, 10 * MIB),
        name="down_grad_local",
    )(gm, gp, rm, rp)


RINGS = {"z": "z", "x": "x", "y": ("yl", "yh")}


def ring_place(axis):
    if axis == "y":
        return lax.axis_index("yh") * 2 + lax.axis_index("yl")
    return lax.axis_index(axis)


def ring_pairs(axis, step):
    if axis == "y":
        place = (0, 2, 1, 3)
        return [(place[i], place[(i + step) % 4]) for i in range(4)]
    return [(i, (i + step) % 4) for i in range(4)]


def ring_scatter(buf, axis, dim):
    me = ring_place(axis)

    def piece(k):
        return lax.dynamic_index_in_dim(buf, (me + k) % 4, dim, keepdims=False)

    got = [lax.ppermute(piece(k), RINGS[axis], ring_pairs(axis, k)) for k in (1, 3, 2)]
    total = piece(0).astype(F32)
    for g in got:
        total = total + g.astype(F32)
    return total


def scatter_all(buf, order):
    dims = ["z", "x", "y"]
    for i, axis in enumerate(order):
        total = ring_scatter(buf, axis, dims.index(axis))
        dims.remove(axis)
        buf = total.astype(BF) if i < 2 else total
    return buf


def to_partner(v):
    return lax.ppermute(v, "c", [(0, 1), (1, 0)])


def by_owner(v, rest):
    v = v.reshape(4, 2, 2, 4, 2, rest)
    return v.transpose(2, 0, 3, 4, 1, 5).reshape(2, 4, 4, 4, rest)


def local(
    image_rows, text_states, text_segment, item_segment, norm_gain, norm_shift, triple_weight, output_weight,
    query_weight, memory_weight, return_weight, up_weight, inner_bias, down_weight, outer_bias, cotangent,
):
    items, r, d = image_rows.shape
    t = items * r
    x = image_rows.reshape(t, d)
    cot = cotangent.reshape(t, d)
    core = lax.axis_index("c")
    c = core.reshape(1).astype(jnp.int32)
    tseg = text_segment.reshape(-1, 1)

    n = lax.iota(jnp.int32, d)
    low = n % 8
    yl, yh, px, pz, cs = (n // 8) % 2, (n // 16) % 2, (n // 32) % 4, (n // 128) % 4, n // 512
    source = ((((pz * 2 + yl) * 2 + (cs ^ core)) * 4 + px) * 2 + yh) * 8 + low
    perm = (lax.broadcasted_iota(jnp.int32, (d, d), 0) == source[None, :]).astype(BF)

    p, h1m, h1t = triple_forward(x, norm_gain[0:1], norm_shift[0:1], perm, triple_weight)
    p = lax.all_to_all(p, BLK, 0, 0).reshape(8, items, r, 384)
    o = attend(p)
    o = lax.all_to_all(o.reshape(8, t, 128), BLK, 0, 0)
    memory = jnp.dot(text_states, memory_weight, preferred_element_type=F32).astype(BF)
    y1, qc, y2, h3, om, ot, h2m, h2t, ocm, oct_, h3m, h3t = middle(
        item_segment, o, x, output_weight, norm_gain, norm_shift, query_weight, memory, tseg, return_weight, perm
    )
    gm, gt, du, inner, out, dy2, dgain2, dshift2, outer = mlp(
        c, h3, up_weight, inner_bias.reshape(1, -1), down_weight, outer_bias.reshape(1, -1), cot, y2, norm_gain
    )
    cot_p = to_partner(cot)
    down_part = down_grad_local(gm, to_partner(gt), cot, cot_p)
    up_part = rows_grad(h3m, to_partner(h3t), du, to_partner(du), "up_grad_local")
    down_sum = scatter_all(down_part.reshape(4, 4, 4, 32, d), "xzy")
    up_sum = scatter_all(up_part.reshape(4, 4, 4, 8, -1), "zxy")

    b2, dqc, b1, dy1, do, dm, dgain1, dshift1 = middle_back(
        item_segment, dy2, return_weight, qc, memory, tseg, query_weight, y1, norm_gain, output_weight
    )
    do = lax.all_to_all(do, BLK, 0, 0).reshape(8, items, r, 128)
    return_part = rows_grad(ocm, to_partner(oct_), b2, to_partner(b2), "return_grad_local")
    query_part = rows_grad(h2m, to_partner(h2t), dqc, to_partner(dqc), "query_grad_local")
    output_part = rows_grad(om, to_partner(ot), b1, to_partner(b1), "output_grad_local")

    dp = attend_back(p, do)
    dp = lax.all_to_all(dp.reshape(8, t, 384), BLK, 0, 0)
    input_grad, dgain0, dshift0, dp_flat = triple_back(dp, triple_weight, x, norm_gain, dy1)
    triple_part = triple_grad_local(h1m, to_partner(h1t), dp_flat, to_partner(dp_flat))
    triple_sum = scatter_all(triple_part.reshape(4, 4, 4, 8, 3 * d), "zxy")

    dm_rows = by_owner(dm.astype(BF), 2 * d).reshape(2, 4, 4, 4, 8, 2 * d // 8)
    rows = [dgain0, dgain1, dgain2, dshift0, dshift1, dshift2, outer, inner]
    thin = jnp.concatenate([by_owner(v.astype(BF), v.shape[1] // 128) for v in rows], axis=-1)
    used = thin.shape[-1]
    thin = jnp.pad(thin, ((0, 0),) * 4 + ((0, 1024 - used),)).reshape(2, 4, 4, 4, 8, 128)
    extra = jnp.concatenate([dm_rows, thin], axis=-1)
    theirs = lax.dynamic_index_in_dim(extra, 1 - core, 0, keepdims=False)
    extra = lax.dynamic_index_in_dim(extra, core, 0, keepdims=False).astype(F32) + to_partner(theirs).astype(F32)
    small = jnp.concatenate(
        [v.reshape(4, 4, 4, 8, d) for v in (return_part, query_part, output_part)] + [extra.astype(BF)], axis=-1
    )
    small_sum = scatter_all(small, "yzx")
    return_grad, query_grad, output_grad = (small_sum[:, i * d : (i + 1) * d] for i in range(3))
    dm_mine = small_sum[:, 3 * d : 3 * d + 2 * d // 8]
    thin_mine = small_sum[:, 3 * d + 2 * d // 8 :].reshape(-1)[:used]
    gains, shifts = thin_mine[:24].reshape(3, 8), thin_mine[24:48].reshape(3, 8)
    outer_mine, inner_mine = thin_mine[48:56], thin_mine[56:]
    dm_all = lax.all_to_all(jnp.broadcast_to(dm_mine.astype(BF), (128,) + dm_mine.shape), ALL, 0, 0)
    dm_all = dm_all.reshape(128, 2 * d)
    me = lax.axis_index(ALL)
    text_cols = lax.dynamic_slice_in_dim(text_states, me * 8, 8, 1)
    memory_rows = lax.dynamic_slice_in_dim(memory_weight, me * 8, 8, 0)
    memory_grad = dot(text_cols, dm_all, 0, 0)
    text_grad = dot(dm_all, memory_rows, 1, 1)
    return (
        out.reshape(items, r, d), input_grad.reshape(items, r, d), text_grad, gains, shifts, triple_sum, output_grad,
        query_grad, memory_grad, return_grad, up_sum, inner_mine, down_sum, outer_mine,
    )


def solution(mesh):
    fine = Mesh(mesh.devices.reshape(4, 2, 2, 4, 2), ALL)
    dp = ("z", "yl", "c")
    rows = P(dp, BLK, None)
    placed = (rows, P(), P(), P(dp)) + (P(),) * 11 + (rows,)
    outs = (
        rows, rows, P(None, ALL), P(None, ALL), P(None, ALL), P(ALL, None), P(ALL, None), P(ALL, None), P(ALL, None),
        P(ALL, None), P(ALL, None), P(ALL), P(ALL, None), P(ALL),
    )
    return jax.shard_map(local, mesh=fine, in_specs=placed, out_specs=outs, check_vma=False)
```

```python
import functools

import jax
import jax.numpy as jnp
from jax import lax
from jax.experimental import pallas as pl
from jax.experimental.pallas import tpu as pltpu
from jax.sharding import Mesh, PartitionSpec as P

DH = 64
EPS = 1e-05
SCALE = 0.125
MASKED = -1e30
BF = jnp.bfloat16
F32 = jnp.float32
MIB = 1 << 20

BLK = ("x", "yh")
ALL = ("z", "yl", "c", "x", "yh")


def dot(a, b, ca=1, cb=0):
    return lax.dot_general(a, b, (((ca,), (cb,)), ((), ())), preferred_element_type=F32)


def cost(us):
    return pl.CostEstimate(flops=1, bytes_accessed=int(us * 0.9e6), transcendentals=0)


def params(mib):
    return pltpu.CompilerParams(vmem_limit_bytes=mib * MIB)


SMEM = pl.BlockSpec(memory_space=pltpu.SMEM)
VMEM = pl.BlockSpec(memory_space=pltpu.VMEM)
ANY = pl.BlockSpec(memory_space=pl.ANY)


def whole(shape):
    return pl.BlockSpec(shape, lambda *_: (0,) * len(shape))


def fetch(source, target, sems, k):
    rows = source.shape[0] // 4
    copies = [
        pltpu.make_async_copy(source.at[pl.ds(i * rows, rows)], target.at[pl.ds(i * rows, rows)], sems.at[k, i])
        for i in range(4)
    ]
    for copy in copies:
        copy.start()

    def wait():
        for copy in copies:
            copy.wait()

    return wait


def normalise(v):
    mean = jnp.mean(v, axis=-1, keepdims=True)
    centred = v - mean
    var = jnp.mean(centred * centred, axis=-1, keepdims=True)
    rstd = lax.rsqrt(var + EPS)
    return centred * rstd, rstd


def norm_back(dy, xhat, rstd, gain):
    dx = dy * gain
    m1 = jnp.mean(dx, axis=-1, keepdims=True)
    m2 = jnp.mean(dx * xhat, axis=-1, keepdims=True)
    back = rstd * (dx - m1 - xhat * m2)
    dgain = jnp.sum(dy * xhat, axis=0, keepdims=True)
    dshift = jnp.sum(dy, axis=0, keepdims=True)
    return back, dgain, dshift


def triple_body(x_ref, g_ref, s_ref, wq_ref, wk_ref, wv_ref, p_ref, h_ref):
    @pl.when(pl.program_id(0) == 0)
    def _():
        xhat, _ = normalise(x_ref[...].astype(F32))
        h_ref[...] = (xhat * g_ref[0:1] + s_ref[0:1]).astype(BF)

    h = h_ref[...]
    for i, w in enumerate((wq_ref, wk_ref, wv_ref)):
        r = dot(h, w[...]).astype(BF)
        for k in range(p_ref.shape[0]):
            p_ref[k, :, i * 128 : (i + 1) * 128] = r[:, k * 128 : (k + 1) * 128]


def triple_forward(x, gain, shift, w):
    t, d = x.shape
    tile = 512
    n = d // tile
    return pl.pallas_call(
        triple_body,
        grid=(n,),
        in_specs=[
            whole((t, d)),
            whole((3, d)),
            whole((3, d)),
            pl.BlockSpec((d, tile), lambda j: (0, j)),
            pl.BlockSpec((d, tile), lambda j: (0, n + j)),
            pl.BlockSpec((d, tile), lambda j: (0, 2 * n + j)),
        ],
        out_specs=[pl.BlockSpec((tile // 128, t, 384), lambda j: (j, 0, 0)), whole((t, d))],
        out_shape=[jax.ShapeDtypeStruct((d // 128, t, 384), BF), jax.ShapeDtypeStruct((t, d), BF)],
        compiler_params=params(60),
        cost_estimate=cost(6),
        name="triple_forward",
    )(x, gain, shift, w, w, w)


def head_lanes(shape, h):
    return (lax.broadcasted_iota(jnp.int32, shape, 1) // DH) == h


def masked_head(v, h):
    return jnp.where(head_lanes(v.shape, h), v, 0.0).astype(BF)


def probs_t(k, qh, qb):
    kv = 256 * (qb + 1)
    st = dot(k[:kv], qh, 1, 1)
    kpos = lax.broadcasted_iota(jnp.int32, (256, 256), 0)
    qpos = lax.broadcasted_iota(jnp.int32, (256, 256), 1)
    last = jnp.where(kpos <= qpos, st[kv - 256 :], MASKED)
    st = jnp.concatenate([st[: kv - 256], last], axis=0) if qb else last
    top = jnp.max(st, axis=0, keepdims=True)
    e = jnp.exp(st - top)
    return e * (1.0 / jnp.sum(e, axis=0, keepdims=True))


def attend_body(p_ref, _, o_ref):
    rows = p_ref.shape[0] * p_ref.shape[2]
    k = p_ref[:, 0, :, 128:256].reshape(rows, 128)
    v = p_ref[:, 0, :, 256:384].reshape(rows, 128)
    vt = v.T
    for qb in range(rows // 256):
        q = p_ref[2 * qb : 2 * qb + 2, 0, :, 0:128].reshape(256, 128).astype(F32) * SCALE
        kv = 256 * (qb + 1)
        parts = []
        for h in range(2):
            a = probs_t(k, masked_head(q, h), qb).astype(BF)
            parts.append(dot(vt[h * DH : (h + 1) * DH, :kv], a))
        o = jnp.concatenate(parts, axis=0).T.astype(BF)
        o_ref[2 * qb : 2 * qb + 2, 0] = o.reshape(2, 128, 128)


def attend(p, token):
    b, items, r, _ = p.shape
    return pl.pallas_call(
        attend_body,
        grid=(items,),
        in_specs=[
            pl.BlockSpec((b, 1, r, 384), lambda i: (0, i, 0, 0)),
            ANY,
        ],
        out_specs=pl.BlockSpec((b, 1, r, 128), lambda i: (0, i, 0, 0)),
        out_shape=jax.ShapeDtypeStruct((b, items, r, 128), BF),
        compiler_params=params(60),
        cost_estimate=cost(10),
        name="attend",
    )(p, token)


def attend_back_body(p_ref, do_ref, _, dp_ref, dk_scr, dv_scr):
    rows = p_ref.shape[0] * p_ref.shape[2]
    blocks = p_ref.shape[0]
    k = p_ref[:, 0, :, 128:256].reshape(rows, 128)
    v = p_ref[:, 0, :, 256:384].reshape(rows, 128)
    kt = k.T
    dk_scr[...] = jnp.zeros_like(dk_scr)
    dv_scr[...] = jnp.zeros_like(dv_scr)
    for qb in range(rows // 256):
        q = p_ref[2 * qb : 2 * qb + 2, 0, :, 0:128].reshape(256, 128).astype(F32) * SCALE
        do = do_ref[2 * qb : 2 * qb + 2, 0].reshape(256, 128).astype(F32)
        kv = 256 * (qb + 1)
        parts = []
        for h in range(2):
            qh = masked_head(q, h)
            doh = masked_head(do, h)
            a = probs_t(k, qh, qb)
            da = dot(v[:kv], doh, 1, 1)
            dots = jnp.sum(a * da, axis=0, keepdims=True)
            ds = (a * (da - dots)).astype(BF)
            dv_scr[:kv] += dot(a.astype(BF), doh)
            dk_scr[:kv] += dot(ds, qh)
            parts.append(dot(kt[h * DH : (h + 1) * DH, :kv], ds))
        dq = (jnp.concatenate(parts, axis=0) * SCALE).T.astype(BF)
        dp_ref[2 * qb : 2 * qb + 2, 0, :, 0:128] = dq.reshape(2, 128, 128)
    dp_ref[:, 0, :, 128:256] = dk_scr[...].astype(BF).reshape(blocks, -1, 128)
    dp_ref[:, 0, :, 256:384] = dv_scr[...].astype(BF).reshape(blocks, -1, 128)


def attend_back(p, do, token):
    b, items, r, _ = p.shape
    return pl.pallas_call(
        attend_back_body,
        grid=(items,),
        in_specs=[
            pl.BlockSpec((b, 1, r, 384), lambda i: (0, i, 0, 0)),
            pl.BlockSpec((b, 1, r, 128), lambda i: (0, i, 0, 0)),
            ANY,
        ],
        out_specs=pl.BlockSpec((b, 1, r, 384), lambda i: (0, i, 0, 0)),
        out_shape=jax.ShapeDtypeStruct((b, items, r, 384), BF),
        scratch_shapes=[pltpu.VMEM((b * r, 128), F32), pltpu.VMEM((b * r, 128), F32)],
        compiler_params=params(60),
        cost_estimate=cost(0.02),
        name="attend_back",
    )(p, do, token)


def gate_body(*_):
    pass


def gate(values, *tokens):
    n = len(values)
    return pl.pallas_call(
        gate_body,
        in_specs=[ANY] * (n + len(tokens)),
        out_specs=[ANY] * n,
        out_shape=[jax.ShapeDtypeStruct(v.shape, v.dtype) for v in values],
        input_output_aliases={i: i for i in range(n)},
        cost_estimate=cost(0.5),
        name="gate",
    )(*values, *tokens)


def stack_heads(v, items):
    r = v.shape[0] // items
    parts = []
    for i in range(items):
        for h in range(2):
            parts.append(masked_head(v[i * r : (i + 1) * r], h))
    return jnp.concatenate(parts, axis=0)


def unstack_heads(v, items):
    r = v.shape[0] // (2 * items)
    parts = []
    for i in range(items):
        first = v[(2 * i) * r : (2 * i + 1) * r]
        second = v[(2 * i + 1) * r : (2 * i + 2) * r]
        parts.append(jnp.where(head_lanes(first.shape, 0), first, second))
    return jnp.concatenate(parts, axis=0)


def cross_probs_t(mk, q4, allowed):
    st = jnp.where(allowed, dot(mk, q4, 1, 1), MASKED)
    top = jnp.max(st, axis=0, keepdims=True)
    e = jnp.exp(st - top)
    return e * (1.0 / jnp.sum(e, axis=0, keepdims=True))


def allowed_mask(tseg_ref, iseg_ref, items, r):
    seg = tseg_ref[...]
    return jnp.concatenate(
        [jnp.broadcast_to(seg == iseg_ref[i], (seg.shape[0], 2 * r)) for i in range(items)], axis=1
    )


def middle_body(
    iseg_ref, o_ref, x_ref, g_ref, s_ref, m_ref, tseg_ref, h1_ref, hy_ref, wo_hbm, wq_hbm, wr_hbm,
    y1_ref, qc_ref, y2_ref, pack_ref, hs_ref, wo_ref, wq_ref, wr_ref, sems,
):
    wait_o, wait_q, wait_r = (
        fetch(a, b, sems, k) for k, (a, b) in enumerate(((wo_hbm, wo_ref), (wq_hbm, wq_ref), (wr_hbm, wr_ref)))
    )
    hs_ref[0] = h1_ref[...]
    hs_ref[1] = hy_ref[...]
    items = iseg_ref.shape[0]
    t, d = x_ref.shape
    r = t // items
    o = jnp.concatenate([o_ref[j] for j in range(o_ref.shape[0])], axis=1)
    pack_ref[:, 0:d] = o
    wait_o()
    y1 = x_ref[...].astype(F32) + dot(o, wo_ref[...])
    y1_ref[...] = y1
    xhat, _ = normalise(y1)
    h2 = (xhat * g_ref[1:2] + s_ref[1:2]).astype(BF)
    pack_ref[:, d : 2 * d] = h2
    wait_q()
    qc_ref[...] = dot(h2, wq_ref[...]).astype(BF)
    allowed = allowed_mask(tseg_ref, iseg_ref, items, r)
    for p in range(d // 128):
        at = slice(p * 128, (p + 1) * 128)
        q4 = stack_heads(qc_ref[:, at].astype(F32) * SCALE, items)
        a = cross_probs_t(m_ref[:, at], q4, allowed).astype(BF)
        o4 = dot(a, m_ref[:, d + p * 128 : d + (p + 1) * 128], 0, 0)
        pack_ref[:, 2 * d + p * 128 : 2 * d + (p + 1) * 128] = unstack_heads(o4, items).astype(BF)
    wait_r()
    y2 = y1 + dot(pack_ref[:, 2 * d : 3 * d], wr_ref[...])
    y2_ref[...] = y2
    xhat, _ = normalise(y2)
    pack_ref[:, 3 * d : 4 * d] = (xhat * g_ref[2:3] + s_ref[2:3]).astype(BF)


def middle(iseg, o, x, wo, gain, shift, wq, m, tseg, wr, h1, hy):
    t, d = x.shape
    args = (iseg, o, x, gain, shift, m, tseg, h1, hy, wo, wq, wr)
    full = jax.ShapeDtypeStruct((t, d), BF)
    wide = jax.ShapeDtypeStruct((t, d), F32)
    outs = [wide, full, wide, jax.ShapeDtypeStruct((t, 4 * d), BF), jax.ShapeDtypeStruct((2, t, d), BF)]
    return pl.pallas_call(
        middle_body,
        in_specs=[SMEM] + [VMEM] * 8 + [ANY] * 3,
        out_specs=[VMEM] * 5,
        out_shape=outs,
        scratch_shapes=[pltpu.VMEM((d, d), BF)] * 3 + [pltpu.SemaphoreType.DMA((3, 4))],
        compiler_params=params(60),
        cost_estimate=cost(4.5),
        name="middle",
    )(*args)


def act_grad_body(r_ref, down_ref, _, dg_ref, outer_ref):
    cot = r_ref[...]
    dg_ref[...] = dot(cot, down_ref[...], 1, 1).astype(BF)

    @pl.when(pl.program_id(0) == 0)
    def _():
        outer_ref[...] = jnp.sum(cot.astype(F32), axis=0, keepdims=True)


def act_grad(cot, down, token):
    t, d = cot.shape
    ff = down.shape[0]
    tile = 2048
    return pl.pallas_call(
        act_grad_body,
        grid=(ff // tile,),
        in_specs=[whole((t, d)), pl.BlockSpec((tile, d), lambda i: (i, 0)), ANY],
        out_specs=[pl.BlockSpec((t, tile), lambda i: (0, i)), whole((1, d))],
        out_shape=[jax.ShapeDtypeStruct((t, ff), BF), jax.ShapeDtypeStruct((1, d), F32)],
        compiler_params=params(60),
        cost_estimate=cost(400),
        name="act_grad",
    )(cot, down, token)


def mlp_body(c_ref, h3_ref, up_ref, ib_ref, down_ref, ob_ref, y2_ref, gm_ref, gt_ref, slope_ref, out_ref, y_scr):
    step = pl.program_id(0)

    @pl.when(step == 0)
    def _():
        y_scr[...] = y2_ref[...] + ob_ref[...]

    u = dot(h3_ref[...], up_ref[...]) + ib_ref[...]
    c0 = 0.7978845608028654
    c1 = 0.044715
    uu = u * u
    t = jnp.tanh(u * (c0 + (c0 * c1) * uu))
    half = 0.5 + 0.5 * t
    g = (u * half).astype(BF)
    slope_ref[...] = (half + (0.5 * u) * (1.0 - t * t) * (c0 + (3.0 * c0 * c1) * uu)).astype(BF)
    first = c_ref[0] == 0
    for k in range(gm_ref.shape[1] // 256):
        even, odd = g[:, 512 * k : 512 * k + 256], g[:, 512 * k + 256 : 512 * k + 512]
        at = slice(256 * k, 256 * k + 256)

        @pl.when(first)
        def _():
            gm_ref[:, at] = even
            gt_ref[:, at] = odd

        @pl.when(jnp.logical_not(first))
        def _():
            gm_ref[:, at] = odd
            gt_ref[:, at] = even

    y_scr[...] += dot(g, down_ref[...])

    @pl.when(step == pl.num_programs(0) - 1)
    def _():
        out_ref[...] = y_scr[...].astype(BF)


def mlp(c, pack, up, ib, down, ob, y2):
    t, d = y2.shape
    ff = up.shape[1]
    tile = 1024
    return pl.pallas_call(
        mlp_body,
        grid=(ff // tile,),
        in_specs=[
            SMEM,
            pl.BlockSpec((t, d), lambda i: (0, 3)),
            pl.BlockSpec((d, tile), lambda i: (0, i)),
            pl.BlockSpec((1, tile), lambda i: (0, i)),
            pl.BlockSpec((tile, d), lambda i: (i, 0)),
            whole((1, d)),
            whole((t, d)),
        ],
        out_specs=[
            pl.BlockSpec((t, tile // 2), lambda i: (0, i)),
            pl.BlockSpec((t, tile // 2), lambda i: (0, i)),
            pl.BlockSpec((t, tile), lambda i: (0, i)),
            whole((t, d)),
        ],
        out_shape=[
            jax.ShapeDtypeStruct((t, ff // 2), BF),
            jax.ShapeDtypeStruct((t, ff // 2), BF),
            jax.ShapeDtypeStruct((t, ff), BF),
            jax.ShapeDtypeStruct((t, d), BF),
        ],
        scratch_shapes=[pltpu.VMEM((t, d), F32)],
        compiler_params=params(60),
        cost_estimate=cost(0.02),
        name="mlp",
    )(c, pack, up, ib, down, ob, y2)


def mlp_back_body(
    dg_ref, slope_ref, up_ref, r_ref, y2_ref, g_ref, _, du_ref, inner_ref, dy2_ref, dgain_ref, dshift_ref, dh_scr
):
    step = pl.program_id(0)

    @pl.when(step == 0)
    def _():
        dh_scr[...] = jnp.zeros_like(dh_scr)

    du = (slope_ref[...].astype(F32) * dg_ref[...].astype(F32)).astype(BF)
    du_ref[...] = du
    inner = jnp.sum(du.astype(F32), axis=0, keepdims=True)
    for k in range(inner_ref.shape[0]):
        inner_ref[k : k + 1] = inner[:, 128 * k : 128 * k + 128]
    dh_scr[...] += dot(du, up_ref[...], 1, 1)

    @pl.when(step == pl.num_programs(0) - 1)
    def _():
        xhat, rstd = normalise(y2_ref[...])
        back, dgain, dshift = norm_back(dh_scr[...], xhat, rstd, g_ref[2:3])
        dy2_ref[...] = r_ref[...].astype(F32) + back
        dgain_ref[...] = dgain
        dshift_ref[...] = dshift


def mlp_back(dg, slope, up, cot, y2, gain, token):
    t, d = y2.shape
    ff = up.shape[1]
    tile = 1024
    row = jax.ShapeDtypeStruct((1, d), F32)
    return pl.pallas_call(
        mlp_back_body,
        grid=(ff // tile,),
        in_specs=[
            pl.BlockSpec((t, tile), lambda i: (0, i)),
            pl.BlockSpec((t, tile), lambda i: (0, i)),
            pl.BlockSpec((d, tile), lambda i: (0, i)),
            whole((t, d)),
            whole((t, d)),
            whole((3, d)),
            ANY,
        ],
        out_specs=[
            pl.BlockSpec((t, tile), lambda i: (0, i)),
            pl.BlockSpec((tile // 128, 128), lambda i: (i, 0)),
            whole((t, d)),
            whole((1, d)),
            whole((1, d)),
        ],
        out_shape=[
            jax.ShapeDtypeStruct((t, ff), BF),
            jax.ShapeDtypeStruct((ff // 128, 128), F32),
            jax.ShapeDtypeStruct((t, d), F32),
            row,
            row,
        ],
        scratch_shapes=[pltpu.VMEM((t, d), F32)],
        compiler_params=params(60),
        cost_estimate=cost(0.02),
        name="mlp_back",
    )(dg, slope, up, cot, y2, gain, token)


def middle_back_body(
    iseg_ref, dy2_ref, qc_ref, m_ref, tseg_ref, y1_ref, g_ref, dgain_ref, dshift_ref, outer_ref, inner_ref,
    wr_hbm, wq_hbm, wo_hbm, _t0, _t1,
    pack_ref, dy1_ref, do_ref, dm_ref, thin_ref,
    doc_scr, wr_ref, wq_ref, wo_ref, sems,
):
    wait_r, wait_q, wait_o = (
        fetch(a, b, sems, k) for k, (a, b) in enumerate(((wr_hbm, wr_ref), (wq_hbm, wq_ref), (wo_hbm, wo_ref)))
    )
    items = iseg_ref.shape[0]
    t, d = dy2_ref.shape
    r = t // items
    texts = m_ref.shape[0]
    dy2 = dy2_ref[...]
    b2 = dy2.astype(BF)
    pack_ref[:t, 0:d] = b2
    wait_r()
    doc_scr[...] = dot(b2, wr_ref[...], 1, 1).astype(BF)
    allowed = allowed_mask(tseg_ref, iseg_ref, items, r)
    for p in range(d // 128):
        at = slice(p * 128, (p + 1) * 128)
        av = slice(d + p * 128, d + (p + 1) * 128)
        mk = m_ref[:, at]
        q4 = stack_heads(qc_ref[:, at].astype(F32) * SCALE, items)
        do4 = stack_heads(doc_scr[:, at].astype(F32), items)
        a = cross_probs_t(mk, q4, allowed)
        da = dot(m_ref[:, av], do4, 1, 1)
        dots = jnp.sum(a * da, axis=0, keepdims=True)
        ds = (a * (da - dots)).astype(BF)
        dmk, dmv = dot(ds, q4), dot(a.astype(BF), do4)
        dm_ref[:, at] = dmk
        dm_ref[:, av] = dmv
        pack_ref[t:, at] = dmk.astype(BF)
        pack_ref[t:, av] = dmv.astype(BF)
        pack_ref[:t, d + p * 128 : d + (p + 1) * 128] = (unstack_heads(dot(ds, mk, 0, 0), items) * SCALE).astype(BF)
    xhat, rstd = normalise(y1_ref[...])
    wait_q()
    dh2 = dot(pack_ref[:t, d : 2 * d], wq_ref[...], 1, 1)
    back, dgain, dshift = norm_back(dh2, xhat, rstd, g_ref[1:2])
    dy1 = dy2 + back
    dy1_ref[...] = dy1
    b1 = dy1.astype(BF)
    pack_ref[:t, 2 * d : 3 * d] = b1
    wait_o()
    do = dot(b1, wo_ref[...], 1, 1).astype(BF)
    for j in range(do_ref.shape[0]):
        do_ref[j] = do[:, j * 128 : (j + 1) * 128]
    thin_ref[...] = jnp.zeros_like(thin_ref)
    for k, v in enumerate((dgain, dshift, dgain_ref[...], dshift_ref[...], outer_ref[...])):
        thin_ref[k : k + 1] = v
    n = inner_ref.shape[0]
    thin_ref[16 : 16 + n, 0:128] = inner_ref[...]
    pack_ref[t:, 2 * d : 3 * d] = jnp.zeros((texts, d), BF)
    pack_ref[t : t + 16 + n, 2 * d : 3 * d] = thin_ref[...].astype(BF)


def middle_back(iseg, dy2, wr, qc, m, tseg, wq, y1, gain, wo, dgain, dshift, outer, inner, tokens):
    t, d = dy2.shape
    texts = m.shape[0]
    args = (iseg, dy2, qc, m, tseg, y1, gain, dgain, dshift, outer, inner, wr, wq, wo, *tokens)
    outs = [
        jax.ShapeDtypeStruct((t + texts, 3 * d), BF),
        jax.ShapeDtypeStruct((t, d), F32),
        jax.ShapeDtypeStruct((d // 128, t, 128), BF),
        jax.ShapeDtypeStruct((texts, 2 * d), F32),
        jax.ShapeDtypeStruct((16 + inner.shape[0], d), F32),
    ]
    return pl.pallas_call(
        middle_back_body,
        in_specs=[SMEM] + [VMEM] * 10 + [ANY] * 5,
        out_specs=[VMEM] * len(outs),
        out_shape=outs,
        scratch_shapes=[pltpu.VMEM((t, d), BF)] + [pltpu.VMEM((d, d), BF)] * 3 + [pltpu.SemaphoreType.DMA((3, 4))],
        compiler_params=params(60),
        cost_estimate=cost(400),
        name="middle_back",
    )(*args)


def triple_back_body(dp_ref, wq_ref, wk_ref, wv_ref, x_ref, g_ref, dy1_ref, _, out_ref, acc):
    step = pl.program_id(0)
    n = pl.num_programs(0)

    @pl.when(step == 0)
    def _():
        acc[...] = jnp.zeros_like(acc)

    total = acc[...]
    for i, w in enumerate((wq_ref, wk_ref, wv_ref)):
        at = slice(i * 128, (i + 1) * 128)
        total += dot(jnp.concatenate([dp_ref[k, :, at] for k in range(dp_ref.shape[0])], axis=1), w[...], 1, 1)
    acc[...] = total

    @pl.when(step == n - 1)
    def _():
        xhat, rstd = normalise(x_ref[...].astype(F32))
        back, _, _ = norm_back(acc[...], xhat, rstd, g_ref[0:1])
        out_ref[...] = dy1_ref[...] + back


def triple_back(dp, w, x, gain, dy1, token):
    t, d = x.shape
    tile = 512
    n = d // tile
    return pl.pallas_call(
        triple_back_body,
        grid=(n,),
        in_specs=[
            pl.BlockSpec((tile // 128, t, 384), lambda j: (j, 0, 0)),
            pl.BlockSpec((d, tile), lambda j: (0, j)),
            pl.BlockSpec((d, tile), lambda j: (0, n + j)),
            pl.BlockSpec((d, tile), lambda j: (0, 2 * n + j)),
            whole((t, d)),
            whole((3, d)),
            whole((t, d)),
            ANY,
        ],
        out_specs=whole((t, d)),
        out_shape=jax.ShapeDtypeStruct((t, d), F32),
        scratch_shapes=[pltpu.VMEM((t, d), F32)],
        compiler_params=params(60),
        cost_estimate=cost(4.5),
        name="triple_back",
    )(dp, w, w, w, x, gain, dy1, token)


def selector(place_ref, first, rows=512, d=1024):
    n = lax.broadcasted_iota(jnp.int32, (rows, d), 0)
    at = lax.broadcasted_iota(jnp.int32, (rows, d), 1)
    third, second, ahead = (n // 8) % 4, (n // 32) % 4, n // 128
    if first == "y":
        py, pz, px = (place_ref[3] + ahead) % 4, second, third
        yl, yh = py % 2, py // 2
    else:
        pz, yl, px, yh = (place_ref[1] + ahead) % 4, (n // 64) % 2, (n // 16) % 4, (n // 8) % 2
    source = ((((pz * 2 + yl) * 2 + place_ref[0]) * 4 + px) * 2 + yh) * 8 + n % 8
    return (at == source).astype(F32).astype(BF)


def split_rows(value, c0_ref, s1_ref, s3_ref, k1_ref, k3_ref):
    n = value.shape[0] // 8
    c0_ref[...] = value[: 2 * n]
    k1_ref[...] = value[2 * n : 3 * n]
    s1_ref[:n] = value[3 * n : 4 * n]
    s1_ref[n:] = value[4 * n : 5 * n]
    s3_ref[n:] = value[5 * n : 6 * n]
    s3_ref[:n] = value[6 * n : 7 * n]
    k3_ref[...] = value[7 * n :]


def pieces(rows, cols):
    n = rows // 8
    return [jax.ShapeDtypeStruct((k, cols), BF) for k in (2 * n, 2 * n, 2 * n, n, n)]


def mlp_grad_body(
    place_ref, pack_hbm, pack_p_hbm, du_hbm, du_p_hbm, g_hbm, g_p_hbm, r_hbm, r_p_hbm, _,
    c0_hbm, s1_hbm, s3_hbm, k1_hbm, k3_hbm, c0, s1, s3, k1, k3, tokens, u_ref, g_ref, r_ref, sems, in_sems,
):
    t, d = r_hbm.shape
    last = pl.ds(3 * d, d)
    wait_h, wait_h_p, wait_u, wait_u_p, wait_g, wait_g_p, wait_r, wait_r_p = (
        fetch(a, b, in_sems, k)
        for k, (a, b) in enumerate((
            (pack_hbm.at[:, last], tokens.at[:t]), (pack_p_hbm.at[:, last], tokens.at[t:]),
            (du_hbm, u_ref.at[:t]), (du_p_hbm, u_ref.at[t:]), (g_hbm, g_ref.at[:t]), (g_p_hbm, g_ref.at[t:]),
            (r_hbm, r_ref.at[:t]), (r_p_hbm, r_ref.at[t:]),
        ))
    )
    half = {(0, 0): (c0, 0), (0, 1): (c0, 8), (1, 0): (k1, 0), (1, 1): (s1, 0), (2, 0): (s1, 8), (2, 1): (s3, 8),
            (3, 0): (s3, 0), (3, 1): (k3, 0)}
    sel = selector(place_ref, "z")
    wait_h()
    wait_h_p()
    left = dot(sel, tokens[...], 1, 1).astype(BF)
    wait_u()
    wait_u_p()
    for pair in range(2):
        value = []
        for block in (2 * pair, 2 * pair + 1):
            value.append(dot(left, u_ref[:, block * d : (block + 1) * d]).reshape(64, 8, d))
        value = jnp.concatenate(value, axis=1).astype(BF)
        for (k, yl), (ref, first) in half.items():
            ref[first : first + 8, 16 * pair : 16 * pair + 16] = value[16 * k + 8 * yl : 16 * k + 8 * yl + 8]
    for wait in (wait_g, wait_g_p, wait_r, wait_r_p):
        wait()
    right = r_ref[...]
    copies = []
    for k, yl in ((1, 1), (2, 0), (3, 0), (2, 1), (1, 0), (3, 1), (0, 0), (0, 1)):
        column = pl.multiple_of((lax.rem(place_ref[1] + k, 4) * 2 + yl) * 256, 256)
        both = g_ref[:, pl.ds(column, 256)].T
        ref, first = half[k, yl]
        ref[first : first + 8, 32:64] = dot(both, right).astype(BF).reshape(8, 32, d)
        done = {(2, 0): (s1, s1_hbm), (2, 1): (s3, s3_hbm), (1, 0): (k1, k1_hbm), (3, 1): (k3, k3_hbm),
                (0, 1): (c0, c0_hbm)}
        if (k, yl) in done:
            source, target = done[k, yl]
            copies.append(pltpu.make_async_copy(source, target, sems.at[len(copies)]))
            copies[-1].start()
    for copy in copies:
        copy.wait()


def mlp_grad(place, pack, pack_p, du, du_p, gm, gp, rm, rp, token):
    t, ff = du.shape
    d = pack.shape[1] // 4
    shapes = [(n, 64, d) for n in (16, 16, 16, 8, 8)]
    args = (pack, pack_p, du, du_p, gm, gp, rm, rp)
    return pl.pallas_call(
        mlp_grad_body,
        in_specs=[SMEM] + [ANY] * 9,
        out_specs=[ANY] * 5,
        out_shape=[jax.ShapeDtypeStruct(v, BF) for v in shapes],
        scratch_shapes=[pltpu.VMEM(v, BF) for v in shapes]
        + [pltpu.VMEM((2 * t, n), BF) for n in (d, ff, ff // 2, d)]
        + [pltpu.SemaphoreType.DMA((5,)), pltpu.SemaphoreType.DMA((8, 4))],
        compiler_params=params(60),
        cost_estimate=cost(400),
        name="mlp_grad",
    )(place, *args, token)


def small_grad_body(
    place_ref, pack_hbm, pack_p_hbm, b_hbm, b_p_hbm, dm_ref, thin_ref, text_ref, wm_hbm, _t0, _t1,
    c0_hbm, s1_hbm, s3_hbm, k1_hbm, k3_hbm, c0, s1, s3, k1, k3, left_scr, right_scr, extra, wm_ref, in_sems, sems,
):
    t, d = left_scr.shape[1] // 2, left_scr.shape[2]
    rows = d // 2
    outs = ((c0, c0_hbm), (s1, s1_hbm), (s3, s3_hbm), (k1, k1_hbm), (k3, k3_hbm))
    waits = []
    for i, column in enumerate((2, 1, 0)):
        at, of = pl.ds(column * d, d), pl.ds(i * d, d)
        waits.append([
            fetch(source, target, in_sems, 4 * i + k)
            for k, (source, target) in enumerate((
                (pack_hbm.at[:, at], left_scr.at[i, :t]), (pack_p_hbm.at[:, at], left_scr.at[i, t:]),
                (b_hbm.at[:t, of], right_scr.at[i, :t]), (b_p_hbm.at[:t, of], right_scr.at[i, t:]),
            ))
        ])
    wait_extra = fetch(b_p_hbm.at[t:], extra, in_sems, 12)
    wait_wm = fetch(wm_hbm, wm_ref, in_sems, 13)
    copies = []

    def put(value, first):
        columns = pl.ds(first, value.shape[1])
        split_rows(value, *(o.at[:, columns] for o, _ in outs))

    def send(k, first, columns):
        at = pl.ds(first, columns)
        for j, (o, hbm) in enumerate(outs):
            copies.append(pltpu.make_async_copy(o.at[:, at], hbm.at[:, at], sems.at[k, j]))
            copies[-1].start()

    sel = selector(place_ref, "y")
    for i in range(3):
        for wait in waits[i]:
            wait()
        left = dot(sel, left_scr[i], 1, 1).astype(BF)
        put(dot(left, right_scr[i]).astype(BF), i * d)
        send(i, i * d, d)
    wait_extra()
    dm = (dm_ref[...] + extra[:, 0 : 2 * d].astype(F32)).astype(BF)
    left = dot(sel, text_ref[...], 1, 1).astype(BF)
    put(dot(left, dm).astype(BF), 3 * d)
    send(3, 3 * d, 2 * d)
    thin = (thin_ref[...] + extra[0:48, 2 * d : 3 * d].astype(F32)).astype(BF)
    values = dot(sel, thin[:16], 1, 1)
    lane = lax.broadcasted_iota(jnp.int32, (rows, 128), 1)
    feature = lax.broadcasted_iota(jnp.int32, (rows, d), 1).astype(F32) * sel.astype(F32)
    source = jnp.sum(feature, axis=1, keepdims=True).astype(jnp.int32)
    line = (lax.broadcasted_iota(jnp.int32, (rows, 32), 1) == source // 32).astype(F32).astype(BF)
    inner = dot(line, thin[16:48, 0:128])
    inner = jnp.where(lane // 4 == source % 32, inner, 0.0).astype(BF)
    fold_from = lax.broadcasted_iota(jnp.int32, (128, 128), 0)
    fold_to = lax.broadcasted_iota(jnp.int32, (128, 128), 1)
    fold = (fold_to == 16 + fold_from % 4).astype(F32).astype(BF)
    values = jnp.concatenate([values, jnp.zeros((rows, 112), F32)], axis=1) + dot(inner, fold)
    put(values.astype(BF), 5 * d)
    wait_wm()
    texts = dot(wm_ref[...], dm, 1, 1).astype(BF)
    put(dot(sel, texts).astype(BF), 5 * d + 128)
    send(4, 5 * d, 256)
    for copy in copies:
        copy.wait()


def small_grad(place, pack, pack_p, b, b_p, dm, thin, text, wm, tokens):
    t = pack.shape[0]
    d = pack.shape[1] // 4
    outs = pieces(d // 2, 5 * d + 256)
    args = (place, pack, pack_p, b, b_p, dm, thin, text, wm, *tokens)
    return pl.pallas_call(
        small_grad_body,
        in_specs=[SMEM] + [ANY] * 4 + [VMEM] * 3 + [ANY] * 3,
        out_specs=[ANY] * 5,
        out_shape=outs,
        scratch_shapes=[pltpu.VMEM(o.shape, BF) for o in outs]
        + [pltpu.VMEM((3, 2 * t, d), BF), pltpu.VMEM((3, 2 * t, d), BF)]
        + [pltpu.VMEM((b.shape[0] - t, 3 * d), BF), pltpu.VMEM(wm.shape, BF)]
        + [pltpu.SemaphoreType.DMA((14, 4)), pltpu.SemaphoreType.DMA((5, 5))],
        compiler_params=params(60),
        cost_estimate=cost(400),
        name="small_grad",
    )(*args)


def triple_grad_body(
    src_ref, hs_ref, hx1_ref, hx2_ref, hx3_ref, dp_ref, wq_ref, wk_ref, wv_ref, g_ref, s_ref, _, mine_ref, theirs_ref
):
    d = hs_ref.shape[2]
    cols = dp_ref.shape[2]
    total = jnp.zeros((cols, d), F32)
    sums = jnp.zeros((1, cols), F32)
    for k, ref in enumerate((hs_ref, hx1_ref, hx2_ref, hx3_ref)):
        for other in range(2):
            dp = dp_ref[src_ref[2 + 2 * k + other]]
            total += dot(dp.T, ref[other])
            sums += jnp.sum(dp.astype(F32), axis=0, keepdims=True)
    total = total.T
    w = jnp.concatenate([wq_ref[...], wk_ref[...], wv_ref[...]], axis=1).astype(F32)
    norm = jnp.concatenate([g_ref[0:1], s_ref[0:1], jnp.zeros((6, d), F32)], axis=0).T
    dshift = jnp.sum(w * sums, axis=1, keepdims=True)
    dgain = (jnp.sum(w * total, axis=1, keepdims=True) - norm[:, 1:2] * dshift) / norm[:, 0:1]
    lane = lax.broadcasted_iota(jnp.int32, (d, 128), 1)
    extra = jnp.where(lane == 0, dgain, 0.0) + jnp.where(lane == 1, dshift, 0.0)
    value = jnp.concatenate([total, extra], axis=1).astype(BF).reshape(8, 2, 64, 512)
    core = src_ref[0]

    @pl.when(core == 0)
    def _():
        mine_ref[...] = value[:, 0]
        theirs_ref[...] = value[:, 1]

    @pl.when(core == 1)
    def _():
        mine_ref[...] = value[:, 1]
        theirs_ref[...] = value[:, 0]


def triple_grad(src, hs, hx, dp, w, gain, shift, token):
    _, t, d = hs.shape
    cols = dp.shape[2]
    part = jax.ShapeDtypeStruct((8, 64, 512), BF)

    def columns(k):
        return pl.BlockSpec((d, 128), lambda i, src_ref: (0, k * (d // 128) + src_ref[1]))

    return pl.pallas_call(
        triple_grad_body,
        grid_spec=pltpu.PrefetchScalarGridSpec(
            num_scalar_prefetch=1,
            grid=(1,),
            in_specs=[whole(hs.shape)] * 4
            + [whole(dp.shape), columns(0), columns(1), columns(2), whole((3, d)), whole((3, d)), ANY],
            out_specs=[whole(part.shape)] * 2,
        ),
        out_shape=[part, part],
        compiler_params=params(60),
        cost_estimate=cost(400),
        name="triple_grad",
    )(src, hs, *hx, dp, w, w, w, gain, shift, token)


def encoder_body(t_ref, w_ref, _, m_ref):
    m_ref[...] = dot(t_ref[...], w_ref[...]).astype(BF)


def encoder_memory(text, w, token):
    n, d = text.shape
    cols = w.shape[1]
    tile = 1024
    return pl.pallas_call(
        encoder_body,
        grid=(cols // tile,),
        in_specs=[whole((n, d)), pl.BlockSpec((d, tile), lambda j: (0, j)), ANY],
        out_specs=pl.BlockSpec((n, tile), lambda j: (0, j)),
        out_shape=jax.ShapeDtypeStruct((n, cols), BF),
        compiler_params=params(32),
        cost_estimate=cost(1.5),
        name="encoder_memory",
    )(text, w, token)


def add_two_body(a_ref, b_ref, _, out_ref):
    out_ref[...] = (a_ref[...].astype(F32) + b_ref[...].astype(F32)).astype(out_ref.dtype)


def add_two(a, b, token):
    return pl.pallas_call(
        add_two_body,
        grid=(1,),
        in_specs=[whole(a.shape), whole(a.shape), ANY],
        out_specs=whole(a.shape),
        out_shape=jax.ShapeDtypeStruct(a.shape, BF),
        compiler_params=params(32),
        cost_estimate=cost(1),
        name="add_two",
    )(a, b, token)


def add_waiting_body(k1_ref, r1_ref, k3_ref, r3_ref, *refs):
    q1_ref, q3_ref = refs[-2:]
    q1_ref[...] = (k1_ref[...].astype(F32) + r1_ref[...].astype(F32)).astype(BF)
    q3_ref[...] = (k3_ref[...].astype(F32) + r3_ref[...].astype(F32)).astype(BF)


def add_waiting(k1, r1, k3, r3, token, name):
    half = whole(k1.shape)
    second = pl.BlockSpec(k1.shape, lambda i: (1,) + (0,) * (len(k1.shape) - 1))
    out = jax.ShapeDtypeStruct(k1.shape, BF)
    return pl.pallas_call(
        add_waiting_body,
        grid=(1,),
        in_specs=[half, second, half, second, ANY],
        out_specs=[half, half],
        out_shape=[out, out],
        compiler_params=params(32),
        cost_estimate=cost(2),
        name=name,
    )(k1, r1, k3, r3, token)


def add_ring_body(at_ref, c0_ref, r1_ref, r3_ref, q1_ref, q3_ref, _, *refs):
    n = q1_ref.shape[0]
    first = c0_ref[:n].astype(F32) + q1_ref[...].astype(F32) + r3_ref[...].astype(F32)
    second = c0_ref[n:].astype(F32) + r1_ref[...].astype(F32) + q3_ref[...].astype(F32)
    if len(refs) == 1:
        refs[0][:n] = first.astype(BF)
        refs[0][n:] = second.astype(BF)
        return
    outs, scr = refs[:4], refs[4]
    scr[0] = first
    scr[1] = second
    for k, out in enumerate(outs):
        place = lax.rem(at_ref[0] + k, 4)
        rows = out.shape[0]
        out[...] = scr[place // 2, pl.ds(pl.multiple_of(lax.rem(place, 2) * rows, rows), rows)].astype(BF)


def add_ring(at, c0, r1, r3, q1, q3, token, cut, name):
    n = q1.shape[0]
    first = pl.BlockSpec(q1.shape, lambda i: (0,) * len(q1.shape))
    shape = (n // 2, q1.shape[1]) if cut else c0.shape
    out = jax.ShapeDtypeStruct(shape, BF)
    return pl.pallas_call(
        add_ring_body,
        grid=(1,),
        in_specs=[SMEM, whole(c0.shape), first, first, first, first, ANY],
        out_specs=[whole(shape)] * (4 if cut else 1),
        out_shape=[out] * (4 if cut else 1),
        scratch_shapes=[pltpu.VMEM((2,) + q1.shape, F32)] if cut else [],
        compiler_params=params(48),
        cost_estimate=cost(2.5),
        name=name,
    )(at, c0, r1, r3, q1, q3, token)


def add_parts_body(at_ref, a_ref, b_ref, c_ref, d_ref, _, *refs):
    outs, scr = refs[:4], refs[4]
    scr[...] = (
        (a_ref[...].astype(F32) + b_ref[...].astype(F32)) + (c_ref[...].astype(F32) + d_ref[...].astype(F32))
    ).reshape(scr.shape)
    for k, out in enumerate(outs):
        place = lax.rem(at_ref[0] + k, 4)
        rows = out.shape[0]
        out[...] = scr[pl.ds(pl.multiple_of(place * rows, rows), rows)].astype(BF)


def add_parts(at, parts, token, name):
    shape = parts[0].shape
    cols = shape[-1]
    rows = parts[0].size // cols
    out = jax.ShapeDtypeStruct((rows // 4, cols), BF)
    return pl.pallas_call(
        add_parts_body,
        grid=(1,),
        in_specs=[SMEM] + [whole(shape)] * 4 + [ANY],
        out_specs=[whole(out.shape)] * 4,
        out_shape=[out] * 4,
        scratch_shapes=[pltpu.VMEM((rows, cols), F32)],
        compiler_params=params(32),
        cost_estimate=cost(2),
        name=name,
    )(at, *parts, token)


def encoder_body(t_ref, w_ref, _, m_ref):
    m_ref[...] = dot(t_ref[...], w_ref[...]).astype(BF)


def encoder_memory(text, w, token):
    n, d = text.shape
    cols = w.shape[1]
    tile = 1024
    return pl.pallas_call(
        encoder_body,
        grid=(cols // tile,),
        in_specs=[whole((n, d)), pl.BlockSpec((d, tile), lambda j: (0, j)), ANY],
        out_specs=pl.BlockSpec((n, tile), lambda j: (0, j)),
        out_shape=jax.ShapeDtypeStruct((n, cols), BF),
        compiler_params=params(32),
        cost_estimate=cost(1.5),
        name="encoder_memory",
    )(text, w, token)


def last_triple_body(v_ref, _, out_ref, thin_ref):
    groups = 8
    d = out_ref.shape[1] // 3
    thin = jnp.zeros(thin_ref.shape, F32)
    for g in range(groups):
        total = v_ref[g].astype(F32)
        for k in range(1, v_ref.shape[0] // groups):
            total += v_ref[k * groups + g].astype(F32)
        for j in range(3):
            out_ref[:, j * d + g * 128 : j * d + g * 128 + 128] = total[:, 128 * j : 128 * j + 128]
        thin += total[:, 384:]
    thin_ref[...] = thin


def last_triple(v, token):
    _, rows, cols = v.shape
    shapes = [(rows, 8 * 384), (rows, 128)]
    return pl.pallas_call(
        last_triple_body,
        grid=(1,),
        in_specs=[whole(v.shape), ANY],
        out_specs=[whole(n) for n in shapes],
        out_shape=[jax.ShapeDtypeStruct(n, F32) for n in shapes],
        compiler_params=params(32),
        cost_estimate=cost(1),
        name="last_triple",
    )(v, token)


def last_mlp_body(v_ref, _, up_ref, down_ref):
    total = v_ref[0].astype(F32)
    for k in range(1, v_ref.shape[0]):
        total += v_ref[k].astype(F32)
    d = down_ref.shape[1]
    for block in range(4):
        up_ref[:, block * d : (block + 1) * d] = total[8 * block : 8 * block + 8]
    down_ref[...] = total[32:]


def last_mlp(v, token):
    d = v.shape[2]
    shapes = [(8, 4 * d), (32, d)]
    return pl.pallas_call(
        last_mlp_body,
        grid=(1,),
        in_specs=[whole(v.shape), ANY],
        out_specs=[whole(n) for n in shapes],
        out_shape=[jax.ShapeDtypeStruct(n, F32) for n in shapes],
        compiler_params=params(32),
        cost_estimate=cost(1.5),
        name="last_mlp",
    )(v, token)


RINGS = {"z": "z", "x": "x", "y": ("yl", "yh")}


def ring_place(axis):
    if axis == "y":
        return lax.axis_index("yh") * 2 + lax.axis_index("yl")
    return lax.axis_index(axis)


def ring_pairs(axis, step):
    if axis == "y":
        place = (0, 2, 1, 3)
        return [(place[i], place[(i + step) % 4]) for i in range(4)]
    return [(i, (i + step) % 4) for i in range(4)]


def shift_ring(v, axis, step):
    return lax.ppermute(v, RINGS[axis], ring_pairs(axis, step))


def first_step(parts, axis):
    return shift_ring(parts[1], axis, 1), shift_ring(parts[2], axis, 3)


def second_step(parts, got, axis, token, name):
    q1, q3 = add_waiting(parts[3], got[0], parts[4], got[1], token, name)
    return shift_ring(q1, axis, 1), shift_ring(q3, axis, 3), q1


def straight(parts, axis):
    return [parts[0]] + [shift_ring(parts[k], axis, k) for k in (1, 3, 2)]


def last_sum(parts):
    total = parts[0].astype(F32)
    for p in parts[1:]:
        total = total + p.astype(F32)
    return total


def swap_yh(v):
    return lax.ppermute(v, "yh", [(0, 1), (1, 0)])


def to_partner(v):
    return lax.ppermute(v, "c", [(0, 1), (1, 0)])


def local(
    image_rows, text_states, text_segment, item_segment, norm_gain, norm_shift, triple_weight, output_weight,
    query_weight, memory_weight, return_weight, up_weight, inner_bias, down_weight, outer_bias, cotangent,
):
    items, r, d = image_rows.shape
    t = items * r
    ff = up_weight.shape[1]
    x = image_rows.reshape(t, d)
    cot = cotangent.reshape(t, d)
    core, pz, px, py = lax.axis_index("c"), lax.axis_index("z"), lax.axis_index("x"), ring_place("y")
    place = jnp.stack([core, pz, px, py]).astype(jnp.int32)
    at_z, at_x = place[1:2], place[2:3]
    yh = lax.axis_index("yh")
    tseg = text_segment.reshape(-1, 1)

    p, h1 = triple_forward(x, norm_gain, norm_shift, triple_weight)
    cot_p = to_partner(cot)
    dg, outer = act_grad(cot, down_weight, p)
    p = lax.all_to_all(p, BLK, 0, 0).reshape(8, items, r, 384)
    memory = encoder_memory(text_states, memory_weight, dg)
    (h1,) = gate((h1,), p, memory, cot_p)
    hy = swap_yh(h1)
    o = attend(p, h1)
    o = lax.all_to_all(o.reshape(8, t, 128), BLK, 0, 0)
    y1, qc, y2, pack, hs = middle(
        item_segment, o, x, output_weight, norm_gain, norm_shift, query_weight, memory, tseg, return_weight, h1, hy
    )
    hx1, hx3 = shift_ring(hs, "x", 1), shift_ring(hs, "x", 3)
    pack_p = to_partner(pack)
    gm, gt, slope, out = mlp(
        place, pack, up_weight, inner_bias.reshape(1, -1), down_weight, outer_bias.reshape(1, -1), y2
    )
    du, inner, dy2, dgain2, dshift2 = mlp_back(dg, slope, up_weight, cot, y2, norm_gain, pack_p)
    du_p = to_partner(du)
    (gt,) = gate((gt,), du)
    gp = to_partner(gt)
    b, dy1, do, dm, thin = middle_back(
        item_segment, dy2, return_weight, qc, memory, tseg, query_weight, y1, norm_gain, output_weight,
        dgain2, dshift2, outer, inner, (hx1, hx3),
    )
    b_p = to_partner(b)
    do = lax.all_to_all(do, BLK, 0, 0).reshape(8, items, r, 128)
    deep = list(mlp_grad(place, pack, pack_p, du, du_p, gm, gp, cot, cot_p, b))
    deep[1], deep[2], hs = gate((deep[1], deep[2], hs), do, hx1, hx3)
    deep_r = first_step(deep, "z")
    hx2 = shift_ring(hs, "x", 2)
    small = small_grad(place, pack, pack_p, b, b_p, dm, thin, text_states, memory_weight, (hs, deep[1]))
    small_r = first_step(small, "y")
    dp = attend_back(p, do, small[3])
    source = [core, px * 2 + yh]
    for k in range(4):
        sx = (px - k) % 4
        source += [sx * 2 + yh, sx * 2 + (1 - yh)]
    dp_flat = dp.reshape(8, t, 384)
    dp_home = lax.all_to_all(dp_flat, BLK, 0, 0)
    deep_q = second_step(deep, deep_r, "z", dp, "add_deep")
    small_q = second_step(small, small_r, "y", deep_q[2], "add_small")
    mine, theirs = triple_grad(
        jnp.stack(source).astype(jnp.int32), hs, (hx1, hx2, hx3), dp_flat, triple_weight, norm_gain, norm_shift,
        small_q[2],
    )
    theirs = to_partner(theirs)
    input_grad = triple_back(dp_home, triple_weight, x, norm_gain, dy1, mine)
    part = add_two(mine, theirs, input_grad)
    part = lax.all_to_all(part.reshape(64, 8, 512), ("z", "yl", "x", "yh"), 0, 0)
    small_sum = straight(add_ring(at_z, small[0], *small_r, *small_q[:2], input_grad, True, "sum_small"), "z")
    (deep_sum,) = add_ring(at_z, deep[0], *deep_r, *deep_q[:2], small_sum[0], False, "sum_deep")
    small_sum = straight(add_parts(at_x, small_sum, deep_sum, "parts_small"), "x")
    triple_sum, norm_zero = last_triple(part, small_sum[0])
    deep_sum = lax.all_to_all(*gate((deep_sum,), norm_zero), ("yl", "x", "yh"), 0, 0)
    small_sum = last_sum(small_sum)
    up_sum, down_sum = last_mlp(deep_sum, norm_zero)

    return_grad, query_grad, output_grad = (small_sum[:, i * d : (i + 1) * d] for i in range(3))
    memory_grad = small_sum[:, 3 * d : 5 * d]
    thin_mine = small_sum[:, 5 * d : 5 * d + 128]
    text_grad = small_sum[:, 5 * d + 128 :].T
    gains = jnp.stack([norm_zero[:, 0], thin_mine[:, 0], thin_mine[:, 2]])
    shifts = jnp.stack([norm_zero[:, 1], thin_mine[:, 1], thin_mine[:, 3]])
    outer_mine = thin_mine[:, 4]
    inner_mine = thin_mine[:, 16:20].reshape(-1)
    return (
        out.reshape(items, r, d), input_grad.reshape(items, r, d), text_grad, gains, shifts, triple_sum, output_grad,
        query_grad, memory_grad, return_grad, up_sum, inner_mine, down_sum, outer_mine,
    )


def solution(mesh):
    fine = Mesh(mesh.devices.reshape(4, 2, 2, 4, 2), ALL)
    dp = ("z", "yl", "c")
    rows = P(dp, BLK, None)
    placed = (rows, P(), P(), P(dp)) + (P(),) * 11 + (rows,)
    outs = (
        rows, rows, P(None, ALL), P(None, ALL), P(None, ALL), P(ALL, None), P(ALL, None), P(ALL, None), P(ALL, None),
        P(ALL, None), P(ALL, None), P(ALL), P(ALL, None), P(ALL),
    )
    return jax.shard_map(local, mesh=fine, in_specs=placed, out_specs=outs, check_vma=False)
```

```python
import functools

import jax
import jax.numpy as jnp
from jax import lax
from jax.experimental import pallas as pl
from jax.experimental.pallas import tpu as pltpu
from jax.sharding import Mesh, PartitionSpec as P

DH = 64
EPS = 1e-05
SCALE = 0.125
MASKED = -1e30
BF = jnp.bfloat16
F32 = jnp.float32
MIB = 1 << 20

BLK = ("x", "yh")
ALL = ("z", "yl", "c", "x", "yh")


def dot(a, b, ca=1, cb=0):
    return lax.dot_general(a, b, (((ca,), (cb,)), ((), ())), preferred_element_type=F32)


def cost(us):
    return pl.CostEstimate(flops=1, bytes_accessed=int(us * 0.9e6), transcendentals=0)


def params(mib):
    return pltpu.CompilerParams(vmem_limit_bytes=mib * MIB)


SMEM = pl.BlockSpec(memory_space=pltpu.SMEM)
VMEM = pl.BlockSpec(memory_space=pltpu.VMEM)
HBM = pl.BlockSpec(memory_space=pltpu.HBM)
ANY = pl.BlockSpec(memory_space=pl.ANY)


def whole(shape):
    return pl.BlockSpec(shape, lambda *_: (0,) * len(shape))


def fetch(source, target, sems, k):
    rows = source.shape[0] // 4
    copies = [
        pltpu.make_async_copy(source.at[pl.ds(i * rows, rows)], target.at[pl.ds(i * rows, rows)], sems.at[k, i])
        for i in range(4)
    ]
    for copy in copies:
        copy.start()

    def wait():
        for copy in copies:
            copy.wait()

    return wait


def normalise(v):
    mean = jnp.mean(v, axis=-1, keepdims=True)
    centred = v - mean
    var = jnp.mean(centred * centred, axis=-1, keepdims=True)
    rstd = lax.rsqrt(var + EPS)
    return centred * rstd, rstd


def norm_back(dy, xhat, rstd, gain):
    dx = dy * gain
    m1 = jnp.mean(dx, axis=-1, keepdims=True)
    m2 = jnp.mean(dx * xhat, axis=-1, keepdims=True)
    back = rstd * (dx - m1 - xhat * m2)
    dgain = jnp.sum(dy * xhat, axis=0, keepdims=True)
    dshift = jnp.sum(dy, axis=0, keepdims=True)
    return back, dgain, dshift


def triple_body(x_ref, g_ref, s_ref, wq_ref, wk_ref, wv_ref, p_ref, h_ref):
    @pl.when(pl.program_id(0) == 0)
    def _():
        xhat, _ = normalise(x_ref[...].astype(F32))
        h_ref[...] = (xhat * g_ref[0:1] + s_ref[0:1]).astype(BF)

    h = h_ref[...]
    for i, w in enumerate((wq_ref, wk_ref, wv_ref)):
        r = dot(h, w[...]).astype(BF)
        for k in range(p_ref.shape[0]):
            p_ref[k, :, i * 128 : (i + 1) * 128] = r[:, k * 128 : (k + 1) * 128]


def triple_forward(x, gain, shift, w):
    t, d = x.shape
    tile = 512
    n = d // tile
    return pl.pallas_call(
        triple_body,
        grid=(n,),
        in_specs=[
            whole((t, d)),
            whole((3, d)),
            whole((3, d)),
            pl.BlockSpec((d, tile), lambda j: (0, j)),
            pl.BlockSpec((d, tile), lambda j: (0, n + j)),
            pl.BlockSpec((d, tile), lambda j: (0, 2 * n + j)),
        ],
        out_specs=[pl.BlockSpec((tile // 128, t, 384), lambda j: (j, 0, 0)), whole((t, d))],
        out_shape=[jax.ShapeDtypeStruct((d // 128, t, 384), BF), jax.ShapeDtypeStruct((t, d), BF)],
        compiler_params=params(60),
        cost_estimate=cost(6),
        name="triple_forward",
    )(x, gain, shift, w, w, w)


def head_lanes(shape, h):
    return (lax.broadcasted_iota(jnp.int32, shape, 1) // DH) == h


def masked_head(v, h):
    return jnp.where(head_lanes(v.shape, h), v, 0.0).astype(BF)


def probs_t(k, qh, qb):
    kv = 256 * (qb + 1)
    st = dot(k[:kv], qh, 1, 1)
    kpos = lax.broadcasted_iota(jnp.int32, (256, 256), 0)
    qpos = lax.broadcasted_iota(jnp.int32, (256, 256), 1)
    last = jnp.where(kpos <= qpos, st[kv - 256 :], MASKED)
    st = jnp.concatenate([st[: kv - 256], last], axis=0) if qb else last
    top = jnp.max(st, axis=0, keepdims=True)
    e = jnp.exp(st - top)
    return e * (1.0 / jnp.sum(e, axis=0, keepdims=True))


def attend_body(p_ref, _t0, _t1, o_ref):
    rows = p_ref.shape[0] * p_ref.shape[2]
    k = p_ref[:, 0, :, 128:256].reshape(rows, 128)
    v = p_ref[:, 0, :, 256:384].reshape(rows, 128)
    vt = v.T
    for qb in range(rows // 256):
        q = p_ref[2 * qb : 2 * qb + 2, 0, :, 0:128].reshape(256, 128).astype(F32) * SCALE
        kv = 256 * (qb + 1)
        parts = []
        for h in range(2):
            a = probs_t(k, masked_head(q, h), qb).astype(BF)
            parts.append(dot(vt[h * DH : (h + 1) * DH, :kv], a))
        o = jnp.concatenate(parts, axis=0).T.astype(BF)
        o_ref[2 * qb : 2 * qb + 2, 0] = o.reshape(2, 128, 128)


def attend(p, *tokens):
    b, items, r, _ = p.shape
    return pl.pallas_call(
        attend_body,
        grid=(items,),
        in_specs=[
            pl.BlockSpec((b, 1, r, 384), lambda i: (0, i, 0, 0)),
            ANY,
            ANY,
        ],
        out_specs=pl.BlockSpec((b, 1, r, 128), lambda i: (0, i, 0, 0)),
        out_shape=jax.ShapeDtypeStruct((b, items, r, 128), BF),
        compiler_params=params(32),
        cost_estimate=cost(10),
        name="attend",
    )(p, *tokens)


def attend_back_body(p_ref, do_ref, _, dp_ref, dk_scr, dv_scr):
    rows = p_ref.shape[0] * p_ref.shape[2]
    blocks = p_ref.shape[0]
    k = p_ref[:, 0, :, 128:256].reshape(rows, 128)
    v = p_ref[:, 0, :, 256:384].reshape(rows, 128)
    kt = k.T
    dk_scr[...] = jnp.zeros_like(dk_scr)
    dv_scr[...] = jnp.zeros_like(dv_scr)
    for qb in range(rows // 256):
        q = p_ref[2 * qb : 2 * qb + 2, 0, :, 0:128].reshape(256, 128).astype(F32) * SCALE
        do = do_ref[2 * qb : 2 * qb + 2, 0].reshape(256, 128).astype(F32)
        kv = 256 * (qb + 1)
        parts = []
        for h in range(2):
            qh = masked_head(q, h)
            doh = masked_head(do, h)
            a = probs_t(k, qh, qb)
            da = dot(v[:kv], doh, 1, 1)
            dots = jnp.sum(a * da, axis=0, keepdims=True)
            ds = (a * (da - dots)).astype(BF)
            dv_scr[:kv] += dot(a.astype(BF), doh)
            dk_scr[:kv] += dot(ds, qh)
            parts.append(dot(kt[h * DH : (h + 1) * DH, :kv], ds))
        dq = (jnp.concatenate(parts, axis=0) * SCALE).T.astype(BF)
        dp_ref[2 * qb : 2 * qb + 2, 0, :, 0:128] = dq.reshape(2, 128, 128)
    dp_ref[:, 0, :, 128:256] = dk_scr[...].astype(BF).reshape(blocks, -1, 128)
    dp_ref[:, 0, :, 256:384] = dv_scr[...].astype(BF).reshape(blocks, -1, 128)


def attend_back(p, do, token):
    b, items, r, _ = p.shape
    return pl.pallas_call(
        attend_back_body,
        grid=(items,),
        in_specs=[
            pl.BlockSpec((b, 1, r, 384), lambda i: (0, i, 0, 0)),
            pl.BlockSpec((b, 1, r, 128), lambda i: (0, i, 0, 0)),
            ANY,
        ],
        out_specs=pl.BlockSpec((b, 1, r, 384), lambda i: (0, i, 0, 0)),
        out_shape=jax.ShapeDtypeStruct((b, items, r, 384), BF),
        scratch_shapes=[pltpu.VMEM((b * r, 128), F32), pltpu.VMEM((b * r, 128), F32)],
        compiler_params=params(40),
        cost_estimate=cost(0.02),
        name="attend_back",
    )(p, do, token)


def gate_body(*_):
    pass


def gate(values, *tokens):
    n = len(values)
    return pl.pallas_call(
        gate_body,
        in_specs=[ANY] * (n + len(tokens)),
        out_specs=[ANY] * n,
        out_shape=[jax.ShapeDtypeStruct(v.shape, v.dtype) for v in values],
        input_output_aliases={i: i for i in range(n)},
        cost_estimate=cost(0.5),
        name="gate",
    )(*values, *tokens)


def stack_heads(v, items):
    r = v.shape[0] // items
    parts = []
    for i in range(items):
        for h in range(2):
            parts.append(masked_head(v[i * r : (i + 1) * r], h))
    return jnp.concatenate(parts, axis=0)


def unstack_heads(v, items):
    r = v.shape[0] // (2 * items)
    parts = []
    for i in range(items):
        first = v[(2 * i) * r : (2 * i + 1) * r]
        second = v[(2 * i + 1) * r : (2 * i + 2) * r]
        parts.append(jnp.where(head_lanes(first.shape, 0), first, second))
    return jnp.concatenate(parts, axis=0)


def cross_probs_t(mk, q4, allowed):
    st = jnp.where(allowed, dot(mk, q4, 1, 1), MASKED)
    top = jnp.max(st, axis=0, keepdims=True)
    e = jnp.exp(st - top)
    return e * (1.0 / jnp.sum(e, axis=0, keepdims=True))


def allowed_mask(tseg_ref, iseg_ref, items, r):
    seg = tseg_ref[...]
    return jnp.concatenate(
        [jnp.broadcast_to(seg == iseg_ref[i], (seg.shape[0], 2 * r)) for i in range(items)], axis=1
    )


def act_grad_body(r_ref, down_ref, _, dg_ref, outer_ref):
    cot = r_ref[...]
    dg_ref[...] = dot(cot, down_ref[...], 1, 1).astype(BF)

    @pl.when(pl.program_id(0) == 0)
    def _():
        outer_ref[...] = jnp.sum(cot.astype(F32), axis=0, keepdims=True)


def act_grad(cot, down, token):
    t, d = cot.shape
    ff = down.shape[0]
    tile = 2048
    return pl.pallas_call(
        act_grad_body,
        grid=(ff // tile,),
        in_specs=[whole((t, d)), pl.BlockSpec((tile, d), lambda i: (i, 0)), ANY],
        out_specs=[pl.BlockSpec((t, tile), lambda i: (0, i)), whole((1, d))],
        out_shape=[jax.ShapeDtypeStruct((t, ff), BF), jax.ShapeDtypeStruct((1, d), F32)],
        compiler_params=params(60),
        cost_estimate=cost(400),
        name="act_grad",
    )(cot, down, token)


def trunk_body(
    iseg_ref, place_ref, x_ref, g_ref, s_ref, m_ref, tseg_ref, ib_ref, ob_ref,
    o_hbm, dg_hbm, r_hbm, wo_hbm, wq_hbm, wr_hbm, up_hbm, down_hbm, _,
    inner_ref, dgain_ref, dshift_ref, y1_hbm, qc_hbm, pack_hbm, gm_hbm, mail_hbm, out_hbm, dy2_hbm,
    o_ref, wo_ref, wq_ref, wr_ref, up_ref, down_ref, dg_ref, r_ref,
    y1_ref, qc_ref, pack_ref, gm_ref, mail_ref, out_ref, dy2_ref, y_scr, dh_scr, in_sems, out_sems,
):
    items = iseg_ref.shape[0]
    t, d = x_ref.shape
    r = t // items
    tile = 1024
    tiles = up_ref.shape[1] // tile
    loads = [(wo_hbm, wo_ref), (wq_hbm, wq_ref), (wr_hbm, wr_ref)]
    for j in range(tiles):
        at = pl.ds(j * tile, tile)
        loads += [(up_hbm.at[:, at], up_ref.at[:, at]), (dg_hbm.at[:, at], dg_ref.at[:, at])]
        loads += [(down_hbm.at[at], down_ref.at[at])]
    loads += [(r_hbm, r_ref)]
    wait_x = fetch(o_hbm, o_ref, in_sems, len(loads))
    waits = [fetch(source, target, in_sems, k) for k, (source, target) in enumerate(loads)]
    stores = []

    def store(source, target):
        stores.append(pltpu.make_async_copy(source, target, out_sems.at[len(stores)]))
        stores[-1].start()

    wait_x()
    o = jnp.concatenate([o_ref[j] for j in range(o_ref.shape[0])], axis=1)
    pack_ref[:, 0:d] = o
    waits[0]()
    y1 = x_ref[...].astype(F32) + dot(o, wo_ref[...])
    y1_ref[...] = y1
    store(y1_ref, y1_hbm)
    xhat, _ = normalise(y1)
    h2 = (xhat * g_ref[1:2] + s_ref[1:2]).astype(BF)
    pack_ref[:, d : 2 * d] = h2
    waits[1]()
    qc_ref[...] = dot(h2, wq_ref[...]).astype(BF)
    store(qc_ref, qc_hbm)
    allowed = allowed_mask(tseg_ref, iseg_ref, items, r)
    for p in range(d // 128):
        at = slice(p * 128, (p + 1) * 128)
        q4 = stack_heads(qc_ref[:, at].astype(F32) * SCALE, items)
        a = cross_probs_t(m_ref[:, at], q4, allowed).astype(BF)
        o4 = dot(a, m_ref[:, d + p * 128 : d + (p + 1) * 128], 0, 0)
        pack_ref[:, 2 * d + p * 128 : 2 * d + (p + 1) * 128] = unstack_heads(o4, items).astype(BF)
    waits[2]()
    y2 = y1 + dot(pack_ref[:, 2 * d : 3 * d], wr_ref[...])
    dy2_ref[...] = y2
    xhat, _ = normalise(y2)
    h3 = (xhat * g_ref[2:3] + s_ref[2:3]).astype(BF)
    store(pack_ref, pack_hbm)
    ff = up_ref.shape[1]
    mail_ref[:, ff + ff // 2 :] = h3
    store(mail_ref.at[:, pl.ds(ff + ff // 2, d)], mail_hbm.at[:, pl.ds(ff + ff // 2, d)])
    y_scr[...] = y2 + ob_ref[...]

    c0 = 0.7978845608028654
    c1 = 0.044715
    first = place_ref[0] == 0
    for j in range(tiles):
        at = slice(j * tile, (j + 1) * tile)
        waits[3 + 3 * j]()
        waits[4 + 3 * j]()
        u = dot(h3, up_ref[:, at]) + ib_ref[:, at]
        uu = u * u
        th = jnp.tanh(u * (c0 + (c0 * c1) * uu))
        half = 0.5 + 0.5 * th
        g = (u * half).astype(BF)
        slope = half + (0.5 * u) * (1.0 - th * th) * (c0 + (3.0 * c0 * c1) * uu)
        du = (slope * dg_ref[:, at].astype(F32)).astype(BF)
        mail_ref[:, at] = du
        store(mail_ref.at[:, pl.ds(j * tile, tile)], mail_hbm.at[:, pl.ds(j * tile, tile)])
        inner = jnp.sum(du.astype(F32), axis=0, keepdims=True)
        for k in range(tile // 128):
            inner_ref[8 * j + k : 8 * j + k + 1] = inner[:, 128 * k : 128 * k + 128]
        for k in range(tile // 512):
            even, odd = g[:, 512 * k : 512 * k + 256], g[:, 512 * k + 256 : 512 * k + 512]
            half_at = j * tile // 2 + 256 * k
            gm_ref[:, half_at : half_at + 256] = jnp.where(first, even, odd)
            mail_ref[:, ff + half_at : ff + half_at + 256] = jnp.where(first, odd, even)
        waits[5 + 3 * j]()
        y_scr[...] += dot(g, down_ref[at])
        back = dot(du, up_ref[:, at], 1, 1)
        dh_scr[...] = dh_scr[...] + back if j else back
    store(gm_ref, gm_hbm)
    store(mail_ref.at[:, pl.ds(ff, ff // 2)], mail_hbm.at[:, pl.ds(ff, ff // 2)])
    out_ref[...] = y_scr[...].astype(BF)
    store(out_ref, out_hbm)
    xhat, rstd = normalise(dy2_ref[...])
    back, dgain, dshift = norm_back(dh_scr[...], xhat, rstd, g_ref[2:3])
    waits[-1]()
    dy2_ref[...] = r_ref[...].astype(F32) + back
    store(dy2_ref, dy2_hbm)
    dgain_ref[...] = dgain
    dshift_ref[...] = dshift
    for copy in stores:
        copy.wait()


def trunk(iseg, place, o, x, gain, shift, m, tseg, ib, ob, dg, cot, wo, wq, wr, up, down, token):
    t, d = x.shape
    ff = up.shape[1]
    args = (iseg, place, x, gain, shift, m, tseg, ib, ob, o, dg, cot, wo, wq, wr, up, down, token)
    small = [((ff // 128, 128), F32), ((1, d), F32), ((1, d), F32)]
    large = [((t, d), F32), ((t, d), BF), ((t, 3 * d), BF), ((t, ff // 2), BF), ((t, ff + ff // 2 + d), BF),
             ((t, d), BF), ((t, d), F32)]
    weights = [(v.shape, BF) for v in (o, wo, wq, wr, up, down, dg, cot)]
    return pl.pallas_call(
        trunk_body,
        in_specs=[SMEM, SMEM] + [VMEM] * 7 + [HBM] * 8 + [ANY],
        out_specs=[VMEM] * 3 + [ANY] * 7,
        out_shape=[jax.ShapeDtypeStruct(*v) for v in small + large],
        scratch_shapes=[pltpu.VMEM(*v) for v in weights + large]
        + [pltpu.VMEM((t, d), F32)] * 2
        + [pltpu.SemaphoreType.DMA((17, 4)), pltpu.SemaphoreType.DMA((12,))],
        compiler_params=params(60),
        cost_estimate=cost(0.02),
        name="trunk",
    )(*args)


def middle_back_body(
    iseg_ref, dy2_ref, qc_ref, m_ref, tseg_ref, y1_ref, g_ref, dgain_ref, dshift_ref, outer_ref, inner_ref,
    h1_ref, hy_ref, wr_hbm, wq_hbm, wo_hbm, _,
    pack_ref, dy1_ref, do_ref, dm_ref, thin_ref, hs_ref,
    doc_scr, wr_ref, wq_ref, wo_ref, sems,
):
    wait_r, wait_q, wait_o = (
        fetch(a, b, sems, k) for k, (a, b) in enumerate(((wr_hbm, wr_ref), (wq_hbm, wq_ref), (wo_hbm, wo_ref)))
    )
    hs_ref[0] = h1_ref[...]
    hs_ref[1] = hy_ref[...]
    items = iseg_ref.shape[0]
    t, d = dy2_ref.shape
    r = t // items
    texts = m_ref.shape[0]
    dy2 = dy2_ref[...]
    b2 = dy2.astype(BF)
    pack_ref[:t, 0:d] = b2
    wait_r()
    doc_scr[...] = dot(b2, wr_ref[...], 1, 1).astype(BF)
    allowed = allowed_mask(tseg_ref, iseg_ref, items, r)
    for p in range(d // 128):
        at = slice(p * 128, (p + 1) * 128)
        av = slice(d + p * 128, d + (p + 1) * 128)
        mk = m_ref[:, at]
        q4 = stack_heads(qc_ref[:, at].astype(F32) * SCALE, items)
        do4 = stack_heads(doc_scr[:, at].astype(F32), items)
        a = cross_probs_t(mk, q4, allowed)
        da = dot(m_ref[:, av], do4, 1, 1)
        dots = jnp.sum(a * da, axis=0, keepdims=True)
        ds = (a * (da - dots)).astype(BF)
        dmk, dmv = dot(ds, q4), dot(a.astype(BF), do4)
        dm_ref[:, at] = dmk
        dm_ref[:, av] = dmv
        pack_ref[t:, at] = dmk.astype(BF)
        pack_ref[t:, av] = dmv.astype(BF)
        pack_ref[:t, d + p * 128 : d + (p + 1) * 128] = (unstack_heads(dot(ds, mk, 0, 0), items) * SCALE).astype(BF)
    xhat, rstd = normalise(y1_ref[...])
    wait_q()
    dh2 = dot(pack_ref[:t, d : 2 * d], wq_ref[...], 1, 1)
    back, dgain, dshift = norm_back(dh2, xhat, rstd, g_ref[1:2])
    dy1 = dy2 + back
    dy1_ref[...] = dy1
    b1 = dy1.astype(BF)
    pack_ref[:t, 2 * d : 3 * d] = b1
    wait_o()
    do = dot(b1, wo_ref[...], 1, 1).astype(BF)
    for j in range(do_ref.shape[0]):
        do_ref[j] = do[:, j * 128 : (j + 1) * 128]
    thin_ref[...] = jnp.zeros_like(thin_ref)
    for k, v in enumerate((dgain, dshift, dgain_ref[...], dshift_ref[...], outer_ref[...])):
        thin_ref[k : k + 1] = v
    n = inner_ref.shape[0]
    thin_ref[16 : 16 + n, 0:128] = inner_ref[...]
    pack_ref[t:, 2 * d : 3 * d] = jnp.zeros((texts, d), BF)
    pack_ref[t : t + 16 + n, 2 * d : 3 * d] = thin_ref[...].astype(BF)


def middle_back(iseg, dy2, wr, qc, m, tseg, wq, y1, gain, wo, dgain, dshift, outer, inner, h1, hy, token):
    t, d = dy2.shape
    texts = m.shape[0]
    args = (iseg, dy2, qc, m, tseg, y1, gain, dgain, dshift, outer, inner, h1, hy, wr, wq, wo, token)
    outs = [
        jax.ShapeDtypeStruct((t + texts, 3 * d), BF),
        jax.ShapeDtypeStruct((t, d), F32),
        jax.ShapeDtypeStruct((d // 128, t, 128), BF),
        jax.ShapeDtypeStruct((texts, 2 * d), F32),
        jax.ShapeDtypeStruct((16 + inner.shape[0], d), F32),
        jax.ShapeDtypeStruct((2, t, d), BF),
    ]
    return pl.pallas_call(
        middle_back_body,
        in_specs=[SMEM] + [VMEM] * 12 + [HBM] * 3 + [ANY],
        out_specs=[VMEM] * len(outs),
        out_shape=outs,
        scratch_shapes=[pltpu.VMEM((t, d), BF)] + [pltpu.VMEM((d, d), BF)] * 3 + [pltpu.SemaphoreType.DMA((3, 4))],
        compiler_params=params(60),
        cost_estimate=cost(400),
        name="middle_back",
    )(*args)


def triple_back_body(dp_ref, wq_ref, wk_ref, wv_ref, x_ref, g_ref, dy1_ref, _, out_ref, acc):
    step = pl.program_id(0)
    n = pl.num_programs(0)

    @pl.when(step == 0)
    def _():
        acc[...] = jnp.zeros_like(acc)

    total = acc[...]
    for i, w in enumerate((wq_ref, wk_ref, wv_ref)):
        at = slice(i * 128, (i + 1) * 128)
        total += dot(jnp.concatenate([dp_ref[k, :, at] for k in range(dp_ref.shape[0])], axis=1), w[...], 1, 1)
    acc[...] = total

    @pl.when(step == n - 1)
    def _():
        xhat, rstd = normalise(x_ref[...].astype(F32))
        back, _, _ = norm_back(acc[...], xhat, rstd, g_ref[0:1])
        out_ref[...] = dy1_ref[...] + back


def triple_back(dp, w, x, gain, dy1, token):
    t, d = x.shape
    tile = 512
    n = d // tile
    return pl.pallas_call(
        triple_back_body,
        grid=(n,),
        in_specs=[
            pl.BlockSpec((tile // 128, t, 384), lambda j: (j, 0, 0)),
            pl.BlockSpec((d, tile), lambda j: (0, j)),
            pl.BlockSpec((d, tile), lambda j: (0, n + j)),
            pl.BlockSpec((d, tile), lambda j: (0, 2 * n + j)),
            whole((t, d)),
            whole((3, d)),
            whole((t, d)),
            ANY,
        ],
        out_specs=whole((t, d)),
        out_shape=jax.ShapeDtypeStruct((t, d), F32),
        scratch_shapes=[pltpu.VMEM((t, d), F32)],
        compiler_params=params(60),
        cost_estimate=cost(4.5),
        name="triple_back",
    )(dp, w, w, w, x, gain, dy1, token)


def selector(place_ref, first, rows=512, d=1024):
    n = lax.broadcasted_iota(jnp.int32, (rows, d), 0)
    at = lax.broadcasted_iota(jnp.int32, (rows, d), 1)
    third, second, ahead = (n // 8) % 4, (n // 32) % 4, n // 128
    if first == "y":
        py, pz, px = (place_ref[3] + ahead) % 4, second, third
        yl, yh = py % 2, py // 2
    else:
        pz, yl, px, yh = (place_ref[1] + ahead) % 4, (n // 64) % 2, (n // 16) % 4, (n // 8) % 2
    source = ((((pz * 2 + yl) * 2 + place_ref[0]) * 4 + px) * 2 + yh) * 8 + n % 8
    return (at == source).astype(F32).astype(BF)


def split_rows(value, c0_ref, s1_ref, s3_ref, k1_ref, k3_ref):
    n = value.shape[0] // 8
    c0_ref[...] = value[: 2 * n]
    k1_ref[...] = value[2 * n : 3 * n]
    s1_ref[:n] = value[3 * n : 4 * n]
    s1_ref[n:] = value[4 * n : 5 * n]
    s3_ref[n:] = value[5 * n : 6 * n]
    s3_ref[:n] = value[6 * n : 7 * n]
    k3_ref[...] = value[7 * n :]


def pieces(rows, cols):
    n = rows // 8
    return [jax.ShapeDtypeStruct((k, cols), BF) for k in (2 * n, 2 * n, 2 * n, n, n)]


def mlp_grad_body(
    place_ref, mail_hbm, mail_p_hbm, g_hbm, r_hbm, r_p_hbm, _,
    c0_hbm, s1_hbm, s3_hbm, k1_hbm, k3_hbm, c0, s1, s3, k1, k3, tokens, u_ref, g_ref, r_ref, sems, in_sems,
):
    t, d = r_hbm.shape
    ff = u_ref.shape[1]
    of_u, of_g, of_h = pl.ds(0, ff), pl.ds(ff, ff // 2), pl.ds(ff + ff // 2, d)
    wait_h, wait_h_p, wait_u, wait_u_p, wait_g, wait_g_p, wait_r, wait_r_p = (
        fetch(a, b, in_sems, k)
        for k, (a, b) in enumerate((
            (mail_hbm.at[:, of_h], tokens.at[:t]), (mail_p_hbm.at[:, of_h], tokens.at[t:]),
            (mail_hbm.at[:, of_u], u_ref.at[:t]), (mail_p_hbm.at[:, of_u], u_ref.at[t:]),
            (g_hbm, g_ref.at[:t]), (mail_p_hbm.at[:, of_g], g_ref.at[t:]),
            (r_hbm, r_ref.at[:t]), (r_p_hbm, r_ref.at[t:]),
        ))
    )
    half = {(0, 0): (c0, 0), (0, 1): (c0, 8), (1, 0): (k1, 0), (1, 1): (s1, 0), (2, 0): (s1, 8), (2, 1): (s3, 8),
            (3, 0): (s3, 0), (3, 1): (k3, 0)}
    sel = selector(place_ref, "z")
    wait_h()
    wait_h_p()
    left = dot(sel, tokens[...], 1, 1).astype(BF)
    wait_u()
    wait_u_p()
    for pair in range(2):
        value = []
        for block in (2 * pair, 2 * pair + 1):
            value.append(dot(left, u_ref[:, block * d : (block + 1) * d]).reshape(64, 8, d))
        value = jnp.concatenate(value, axis=1).astype(BF)
        for (k, yl), (ref, first) in half.items():
            ref[first : first + 8, 16 * pair : 16 * pair + 16] = value[16 * k + 8 * yl : 16 * k + 8 * yl + 8]
    for wait in (wait_g, wait_g_p, wait_r, wait_r_p):
        wait()
    right = r_ref[...]
    copies = []
    for k, yl in ((1, 1), (2, 0), (3, 0), (2, 1), (1, 0), (3, 1), (0, 0), (0, 1)):
        column = pl.multiple_of((lax.rem(place_ref[1] + k, 4) * 2 + yl) * 256, 256)
        both = g_ref[:, pl.ds(column, 256)].T
        ref, first = half[k, yl]
        ref[first : first + 8, 32:64] = dot(both, right).astype(BF).reshape(8, 32, d)
        done = {(2, 0): (s1, s1_hbm), (2, 1): (s3, s3_hbm), (1, 0): (k1, k1_hbm), (3, 1): (k3, k3_hbm),
                (0, 1): (c0, c0_hbm)}
        if (k, yl) in done:
            source, target = done[k, yl]
            copies.append(pltpu.make_async_copy(source, target, sems.at[len(copies)]))
            copies[-1].start()
    for copy in copies:
        copy.wait()


def mlp_grad(place, mail, mail_p, gm, rm, rp, token):
    t, d = rm.shape
    ff = 2 * gm.shape[1]
    shapes = [(n, 64, d) for n in (16, 16, 16, 8, 8)]
    args = (mail, mail_p, gm, rm, rp)
    return pl.pallas_call(
        mlp_grad_body,
        in_specs=[SMEM] + [ANY] * 6,
        out_specs=[ANY] * 5,
        out_shape=[jax.ShapeDtypeStruct(v, BF) for v in shapes],
        scratch_shapes=[pltpu.VMEM(v, BF) for v in shapes]
        + [pltpu.VMEM((2 * t, n), BF) for n in (d, ff, ff // 2, d)]
        + [pltpu.SemaphoreType.DMA((5,)), pltpu.SemaphoreType.DMA((8, 4))],
        compiler_params=params(60),
        cost_estimate=cost(400),
        name="mlp_grad",
    )(place, *args, token)


def small_grad_body(
    place_ref, pack_hbm, pack_p_hbm, b_hbm, b_p_hbm, dm_ref, thin_ref, text_ref, wm_hbm, _,
    c0_hbm, s1_hbm, s3_hbm, k1_hbm, k3_hbm, c0, s1, s3, k1, k3, left_scr, right_scr, extra, wm_ref, in_sems, sems,
):
    t, d = left_scr.shape[1] // 2, left_scr.shape[2]
    rows = d // 2
    outs = ((c0, c0_hbm), (s1, s1_hbm), (s3, s3_hbm), (k1, k1_hbm), (k3, k3_hbm))
    waits = []
    for i, column in enumerate((2, 1, 0)):
        at, of = pl.ds(column * d, d), pl.ds(i * d, d)
        waits.append([
            fetch(source, target, in_sems, 4 * i + k)
            for k, (source, target) in enumerate((
                (pack_hbm.at[:, at], left_scr.at[i, :t]), (pack_p_hbm.at[:, at], left_scr.at[i, t:]),
                (b_hbm.at[:t, of], right_scr.at[i, :t]), (b_p_hbm.at[:t, of], right_scr.at[i, t:]),
            ))
        ])
    wait_extra = fetch(b_p_hbm.at[t:], extra, in_sems, 12)
    wait_wm = fetch(wm_hbm, wm_ref, in_sems, 13)
    copies = []

    def put(value, first):
        columns = pl.ds(first, value.shape[1])
        split_rows(value, *(o.at[:, columns] for o, _ in outs))

    def send(k, first, columns):
        at = pl.ds(first, columns)
        for j, (o, hbm) in enumerate(outs):
            copies.append(pltpu.make_async_copy(o.at[:, at], hbm.at[:, at], sems.at[k, j]))
            copies[-1].start()

    sel = selector(place_ref, "y")
    for i in range(3):
        for wait in waits[i]:
            wait()
        left = dot(sel, left_scr[i], 1, 1).astype(BF)
        put(dot(left, right_scr[i]).astype(BF), i * d)
        send(i, i * d, d)
    wait_extra()
    dm = (dm_ref[...] + extra[:, 0 : 2 * d].astype(F32)).astype(BF)
    left = dot(sel, text_ref[...], 1, 1).astype(BF)
    put(dot(left, dm).astype(BF), 3 * d)
    send(3, 3 * d, 2 * d)
    thin = (thin_ref[...] + extra[0:48, 2 * d : 3 * d].astype(F32)).astype(BF)
    values = dot(sel, thin[:16], 1, 1)
    lane = lax.broadcasted_iota(jnp.int32, (rows, 128), 1)
    feature = lax.broadcasted_iota(jnp.int32, (rows, d), 1).astype(F32) * sel.astype(F32)
    source = jnp.sum(feature, axis=1, keepdims=True).astype(jnp.int32)
    line = (lax.broadcasted_iota(jnp.int32, (rows, 32), 1) == source // 32).astype(F32).astype(BF)
    inner = dot(line, thin[16:48, 0:128])
    inner = jnp.where(lane // 4 == source % 32, inner, 0.0).astype(BF)
    fold_from = lax.broadcasted_iota(jnp.int32, (128, 128), 0)
    fold_to = lax.broadcasted_iota(jnp.int32, (128, 128), 1)
    fold = (fold_to == 16 + fold_from % 4).astype(F32).astype(BF)
    values = jnp.concatenate([values, jnp.zeros((rows, 112), F32)], axis=1) + dot(inner, fold)
    put(values.astype(BF), 5 * d)
    wait_wm()
    texts = dot(wm_ref[...], dm, 1, 1).astype(BF)
    put(dot(sel, texts).astype(BF), 5 * d + 128)
    send(4, 5 * d, 256)
    for copy in copies:
        copy.wait()


def small_grad(place, pack, pack_p, b, b_p, dm, thin, text, wm, token):
    t = pack.shape[0]
    d = pack.shape[1] // 3
    outs = pieces(d // 2, 5 * d + 256)
    args = (place, pack, pack_p, b, b_p, dm, thin, text, wm, token)
    return pl.pallas_call(
        small_grad_body,
        in_specs=[SMEM] + [ANY] * 4 + [VMEM] * 3 + [ANY] * 2,
        out_specs=[ANY] * 5,
        out_shape=outs,
        scratch_shapes=[pltpu.VMEM(o.shape, BF) for o in outs]
        + [pltpu.VMEM((3, 2 * t, d), BF), pltpu.VMEM((3, 2 * t, d), BF)]
        + [pltpu.VMEM((b.shape[0] - t, 3 * d), BF), pltpu.VMEM(wm.shape, BF)]
        + [pltpu.SemaphoreType.DMA((14, 4)), pltpu.SemaphoreType.DMA((5, 5))],
        compiler_params=params(60),
        cost_estimate=cost(400),
        name="small_grad",
    )(*args)


def triple_grad_body(
    src_ref, hs_ref, hx1_ref, hx2_ref, hx3_ref, dp_ref, wq_ref, wk_ref, wv_ref, g_ref, s_ref, _, mine_ref, theirs_ref
):
    d = hs_ref.shape[2]
    cols = dp_ref.shape[2]
    total = jnp.zeros((cols, d), F32)
    sums = jnp.zeros((1, cols), F32)
    for k, ref in enumerate((hs_ref, hx1_ref, hx2_ref, hx3_ref)):
        for other in range(2):
            dp = dp_ref[src_ref[2 + 2 * k + other]]
            total += dot(dp.T, ref[other])
            sums += jnp.sum(dp.astype(F32), axis=0, keepdims=True)
    total = total.T
    w = jnp.concatenate([wq_ref[...], wk_ref[...], wv_ref[...]], axis=1).astype(F32)
    norm = jnp.concatenate([g_ref[0:1], s_ref[0:1], jnp.zeros((6, d), F32)], axis=0).T
    dshift = jnp.sum(w * sums, axis=1, keepdims=True)
    dgain = (jnp.sum(w * total, axis=1, keepdims=True) - norm[:, 1:2] * dshift) / norm[:, 0:1]
    lane = lax.broadcasted_iota(jnp.int32, (d, 128), 1)
    extra = jnp.where(lane == 0, dgain, 0.0) + jnp.where(lane == 1, dshift, 0.0)
    value = jnp.concatenate([total, extra], axis=1).astype(BF).reshape(8, 2, 64, 512)
    core = src_ref[0]

    @pl.when(core == 0)
    def _():
        mine_ref[...] = value[:, 0]
        theirs_ref[...] = value[:, 1]

    @pl.when(core == 1)
    def _():
        mine_ref[...] = value[:, 1]
        theirs_ref[...] = value[:, 0]


def triple_grad(src, hs, hx, dp, w, gain, shift, token):
    _, t, d = hs.shape
    cols = dp.shape[2]
    part = jax.ShapeDtypeStruct((8, 64, 512), BF)

    def columns(k):
        return pl.BlockSpec((d, 128), lambda i, src_ref: (0, k * (d // 128) + src_ref[1]))

    return pl.pallas_call(
        triple_grad_body,
        grid_spec=pltpu.PrefetchScalarGridSpec(
            num_scalar_prefetch=1,
            grid=(1,),
            in_specs=[whole(hs.shape)] * 4
            + [whole(dp.shape), columns(0), columns(1), columns(2), whole((3, d)), whole((3, d)), ANY],
            out_specs=[whole(part.shape)] * 2,
        ),
        out_shape=[part, part],
        compiler_params=params(60),
        cost_estimate=cost(0.02),
        name="triple_grad",
    )(src, hs, *hx, dp, w, w, w, gain, shift, token)


def encoder_body(t_ref, w_ref, _, m_ref):
    m_ref[...] = dot(t_ref[...], w_ref[...]).astype(BF)


def encoder_memory(text, w, token):
    n, d = text.shape
    cols = w.shape[1]
    tile = 1024
    return pl.pallas_call(
        encoder_body,
        grid=(cols // tile,),
        in_specs=[whole((n, d)), pl.BlockSpec((d, tile), lambda j: (0, j)), ANY],
        out_specs=pl.BlockSpec((n, tile), lambda j: (0, j)),
        out_shape=jax.ShapeDtypeStruct((n, cols), BF),
        compiler_params=params(32),
        cost_estimate=cost(1.5),
        name="encoder_memory",
    )(text, w, token)


def add_two_body(a_ref, b_ref, _, out_ref):
    out_ref[...] = (a_ref[...].astype(F32) + b_ref[...].astype(F32)).astype(out_ref.dtype)


def add_two(a, b, token):
    return pl.pallas_call(
        add_two_body,
        grid=(1,),
        in_specs=[whole(a.shape), whole(a.shape), ANY],
        out_specs=whole(a.shape),
        out_shape=jax.ShapeDtypeStruct(a.shape, BF),
        compiler_params=params(60),
        cost_estimate=cost(1),
        name="add_two",
    )(a, b, token)


def add_waiting_body(k1_ref, r1_ref, k3_ref, r3_ref, *refs):
    q1_ref, q3_ref = refs[-2:]
    q1_ref[...] = (k1_ref[...].astype(F32) + r1_ref[...].astype(F32)).astype(BF)
    q3_ref[...] = (k3_ref[...].astype(F32) + r3_ref[...].astype(F32)).astype(BF)


def add_waiting(k1, r1, k3, r3, token, us, name):
    half = whole(k1.shape)
    second = pl.BlockSpec(k1.shape, lambda i: (1,) + (0,) * (len(k1.shape) - 1))
    out = jax.ShapeDtypeStruct(k1.shape, BF)
    return pl.pallas_call(
        add_waiting_body,
        grid=(1,),
        in_specs=[half, second, half, second, ANY],
        out_specs=[half, half],
        out_shape=[out, out],
        compiler_params=params(60),
        cost_estimate=cost(us),
        name=name,
    )(k1, r1, k3, r3, token)


def add_ring_body(at_ref, c0_ref, r1_ref, r3_ref, q1_ref, q3_ref, _, *refs):
    n = q1_ref.shape[0]
    first = c0_ref[:n].astype(F32) + q1_ref[...].astype(F32) + r3_ref[...].astype(F32)
    second = c0_ref[n:].astype(F32) + r1_ref[...].astype(F32) + q3_ref[...].astype(F32)
    if len(refs) == 1:
        refs[0][:n] = first.astype(BF)
        refs[0][n:] = second.astype(BF)
        return
    outs, scr = refs[:4], refs[4]
    scr[0] = first
    scr[1] = second
    for k, out in enumerate(outs):
        place = lax.rem(at_ref[0] + k, 4)
        rows = out.shape[0]
        out[...] = scr[place // 2, pl.ds(pl.multiple_of(lax.rem(place, 2) * rows, rows), rows)].astype(BF)


def add_ring(at, c0, r1, r3, q1, q3, token, cut, name):
    n = q1.shape[0]
    first = pl.BlockSpec(q1.shape, lambda i: (0,) * len(q1.shape))
    shape = (n // 2, q1.shape[1]) if cut else c0.shape
    out = jax.ShapeDtypeStruct(shape, BF)
    return pl.pallas_call(
        add_ring_body,
        grid=(1,),
        in_specs=[SMEM, whole(c0.shape), first, first, first, first, ANY],
        out_specs=[whole(shape)] * (4 if cut else 1),
        out_shape=[out] * (4 if cut else 1),
        scratch_shapes=[pltpu.VMEM((2,) + q1.shape, F32)] if cut else [],
        compiler_params=params(60),
        cost_estimate=cost(2.5),
        name=name,
    )(at, c0, r1, r3, q1, q3, token)


def add_parts_body(at_ref, a_ref, b_ref, c_ref, d_ref, _, *refs):
    outs, scr = refs[:4], refs[4]
    scr[...] = (
        (a_ref[...].astype(F32) + b_ref[...].astype(F32)) + (c_ref[...].astype(F32) + d_ref[...].astype(F32))
    ).reshape(scr.shape)
    for k, out in enumerate(outs):
        place = lax.rem(at_ref[0] + k, 4)
        rows = out.shape[0]
        out[...] = scr[pl.ds(pl.multiple_of(place * rows, rows), rows)].astype(BF)


def add_parts(at, parts, token, name):
    shape = parts[0].shape
    cols = shape[-1]
    rows = parts[0].size // cols
    out = jax.ShapeDtypeStruct((rows // 4, cols), BF)
    return pl.pallas_call(
        add_parts_body,
        grid=(1,),
        in_specs=[SMEM] + [whole(shape)] * 4 + [ANY],
        out_specs=[whole(out.shape)] * 4,
        out_shape=[out] * 4,
        scratch_shapes=[pltpu.VMEM((rows, cols), F32)],
        compiler_params=params(60),
        cost_estimate=cost(2),
        name=name,
    )(at, *parts, token)


def encoder_body(t_ref, w_ref, _, m_ref):
    m_ref[...] = dot(t_ref[...], w_ref[...]).astype(BF)


def encoder_memory(text, w, token):
    n, d = text.shape
    cols = w.shape[1]
    tile = 1024
    return pl.pallas_call(
        encoder_body,
        grid=(cols // tile,),
        in_specs=[whole((n, d)), pl.BlockSpec((d, tile), lambda j: (0, j)), ANY],
        out_specs=pl.BlockSpec((n, tile), lambda j: (0, j)),
        out_shape=jax.ShapeDtypeStruct((n, cols), BF),
        compiler_params=params(60),
        cost_estimate=cost(1.5),
        name="encoder_memory",
    )(text, w, token)


def last_triple_body(v_ref, _, out_ref, thin_ref):
    groups = 8
    d = out_ref.shape[1] // 3
    thin = jnp.zeros(thin_ref.shape, F32)
    for g in range(groups):
        total = v_ref[g].astype(F32)
        for k in range(1, v_ref.shape[0] // groups):
            total += v_ref[k * groups + g].astype(F32)
        for j in range(3):
            out_ref[:, j * d + g * 128 : j * d + g * 128 + 128] = total[:, 128 * j : 128 * j + 128]
        thin += total[:, 384:]
    thin_ref[...] = thin


def last_triple(v, token):
    _, rows, cols = v.shape
    shapes = [(rows, 8 * 384), (rows, 128)]
    return pl.pallas_call(
        last_triple_body,
        grid=(1,),
        in_specs=[whole(v.shape), ANY],
        out_specs=[whole(n) for n in shapes],
        out_shape=[jax.ShapeDtypeStruct(n, F32) for n in shapes],
        compiler_params=params(32),
        cost_estimate=cost(1),
        name="last_triple",
    )(v, token)


def last_mlp_body(v_ref, _, up_ref, down_ref):
    total = v_ref[0].astype(F32)
    for k in range(1, v_ref.shape[0]):
        total += v_ref[k].astype(F32)
    d = down_ref.shape[1]
    for block in range(4):
        up_ref[:, block * d : (block + 1) * d] = total[8 * block : 8 * block + 8]
    down_ref[...] = total[32:]


def last_mlp(v, token):
    d = v.shape[2]
    shapes = [(8, 4 * d), (32, d)]
    return pl.pallas_call(
        last_mlp_body,
        grid=(1,),
        in_specs=[whole(v.shape), ANY],
        out_specs=[whole(n) for n in shapes],
        out_shape=[jax.ShapeDtypeStruct(n, F32) for n in shapes],
        compiler_params=params(32),
        cost_estimate=cost(1.5),
        name="last_mlp",
    )(v, token)


RINGS = {"z": "z", "x": "x", "y": ("yl", "yh")}


def ring_place(axis):
    if axis == "y":
        return lax.axis_index("yh") * 2 + lax.axis_index("yl")
    return lax.axis_index(axis)


def ring_pairs(axis, step):
    if axis == "y":
        place = (0, 2, 1, 3)
        return [(place[i], place[(i + step) % 4]) for i in range(4)]
    return [(i, (i + step) % 4) for i in range(4)]


def shift_ring(v, axis, step):
    return lax.ppermute(v, RINGS[axis], ring_pairs(axis, step))


def first_step(parts, axis):
    return shift_ring(parts[1], axis, 1), shift_ring(parts[2], axis, 3)


def second_step(parts, got, axis, token, us, name):
    q1, q3 = add_waiting(parts[3], got[0], parts[4], got[1], token, us, name)
    return shift_ring(q1, axis, 1), shift_ring(q3, axis, 3), q1


def straight(parts, axis):
    return [parts[0]] + [shift_ring(parts[k], axis, k) for k in (1, 3, 2)]


def last_sum(parts):
    total = parts[0].astype(F32)
    for p in parts[1:]:
        total = total + p.astype(F32)
    return total


def swap_yh(v):
    return lax.ppermute(v, "yh", [(0, 1), (1, 0)])


def to_partner(v):
    return lax.ppermute(v, "c", [(0, 1), (1, 0)])


def local(
    image_rows, text_states, text_segment, item_segment, norm_gain, norm_shift, triple_weight, output_weight,
    query_weight, memory_weight, return_weight, up_weight, inner_bias, down_weight, outer_bias, cotangent,
):
    items, r, d = image_rows.shape
    t = items * r
    ff = up_weight.shape[1]
    x = image_rows.reshape(t, d)
    cot = cotangent.reshape(t, d)
    core, pz, px, py = lax.axis_index("c"), lax.axis_index("z"), lax.axis_index("x"), ring_place("y")
    place = jnp.stack([core, pz, px, py]).astype(jnp.int32)
    at_z, at_x = place[1:2], place[2:3]
    yh = lax.axis_index("yh")
    tseg = text_segment.reshape(-1, 1)

    p, h1 = triple_forward(x, norm_gain, norm_shift, triple_weight)
    cot_p = to_partner(cot)
    dg, outer = act_grad(cot, down_weight, p)
    p = lax.all_to_all(p, BLK, 0, 0).reshape(8, items, r, 384)
    memory = encoder_memory(text_states, memory_weight, dg)
    (h1,) = gate((h1,), p[0, 0, :16, :128], memory, cot_p)
    hy = swap_yh(h1)
    o = attend(p, h1, memory)
    o = lax.all_to_all(o.reshape(8, t, 128), BLK, 0, 0)
    inner, dgain2, dshift2, y1, qc, pack, gm, mail, out, dy2 = trunk(
        item_segment, place, o, x, norm_gain, norm_shift, memory, tseg, inner_bias.reshape(1, -1),
        outer_bias.reshape(1, -1), dg, cot, output_weight, query_weight, return_weight, up_weight, down_weight, hy,
    )
    mail_p, pack_p = to_partner(mail), to_partner(pack)
    b, dy1, do, dm, thin, hs = middle_back(
        item_segment, dy2, return_weight, qc, memory, tseg, query_weight, y1, norm_gain, output_weight,
        dgain2, dshift2, outer, inner, h1, hy, mail,
    )
    b_p = to_partner(b)
    do = lax.all_to_all(do, BLK, 0, 0).reshape(8, items, r, 128)
    hx1, hx3 = shift_ring(hs, "x", 1), shift_ring(hs, "x", 3)
    deep = list(mlp_grad(place, mail, mail_p, gm, cot, cot_p, b))
    deep[1], deep[2] = gate((deep[1], deep[2]), do, pack_p, b_p)
    deep_r = first_step(deep, "z")
    small = small_grad(place, pack, pack_p, b, b_p, dm, thin, text_states, memory_weight, deep[1])
    small_r = first_step(small, "y")
    (hs,) = gate((hs,), hx1, hx3, small[3])
    hx2 = shift_ring(hs, "x", 2)
    dp = attend_back(p, do, small[3])
    source = [core, px * 2 + yh]
    for k in range(4):
        sx = (px - k) % 4
        source += [sx * 2 + yh, sx * 2 + (1 - yh)]
    dp_flat = dp.reshape(8, t, 384)
    dp_home = lax.all_to_all(dp_flat, BLK, 0, 0)
    mine, theirs = triple_grad(
        jnp.stack(source).astype(jnp.int32), hs, (hx1, hx2, hx3), dp_flat, triple_weight, norm_gain, norm_shift, dp
    )
    deep_q = second_step(deep, deep_r, "z", mine, 0.02, "add_deep")
    small_q = second_step(small, small_r, "y", deep_q[2], 400, "add_small")
    part = add_two(mine, to_partner(theirs), dp_home)
    part_token = part
    part = lax.all_to_all(part.reshape(64, 8, 512), ("z", "yl", "x", "yh"), 0, 0)
    (deep_sum,) = add_ring(at_z, deep[0], *deep_r, *deep_q[:2], part_token, False, "sum_deep")
    triple_sum, norm_zero = last_triple(part, deep_sum)
    (deep_sum,) = gate((deep_sum,), norm_zero)
    small_sum = straight(add_ring(at_z, small[0], *small_r, *small_q[:2], deep_sum, True, "sum_small"), "z")
    deep_sum = lax.all_to_all(deep_sum, ("yl", "x", "yh"), 0, 0)
    input_grad = triple_back(dp_home, triple_weight, x, norm_gain, dy1, small_sum[0])
    small_sum = straight(add_parts(at_x, small_sum, input_grad, "parts_small"), "x")
    small_sum = last_sum(small_sum)
    up_sum, down_sum = last_mlp(deep_sum, norm_zero)

    return_grad, query_grad, output_grad = (small_sum[:, i * d : (i + 1) * d] for i in range(3))
    memory_grad = small_sum[:, 3 * d : 5 * d]
    thin_mine = small_sum[:, 5 * d : 5 * d + 128]
    text_grad = small_sum[:, 5 * d + 128 :].T
    gains = jnp.stack([norm_zero[:, 0], thin_mine[:, 0], thin_mine[:, 2]])
    shifts = jnp.stack([norm_zero[:, 1], thin_mine[:, 1], thin_mine[:, 3]])
    outer_mine = thin_mine[:, 4]
    inner_mine = thin_mine[:, 16:20].reshape(-1)
    return (
        out.reshape(items, r, d), input_grad.reshape(items, r, d), text_grad, gains, shifts, triple_sum, output_grad,
        query_grad, memory_grad, return_grad, up_sum, inner_mine, down_sum, outer_mine,
    )


def solution(mesh):
    fine = Mesh(mesh.devices.reshape(4, 2, 2, 4, 2), ALL)
    dp = ("z", "yl", "c")
    rows = P(dp, BLK, None)
    placed = (rows, P(), P(), P(dp)) + (P(),) * 11 + (rows,)
    outs = (
        rows, rows, P(None, ALL), P(None, ALL), P(None, ALL), P(ALL, None), P(ALL, None), P(ALL, None), P(ALL, None),
        P(ALL, None), P(ALL, None), P(ALL), P(ALL, None), P(ALL),
    )
    return jax.shard_map(local, mesh=fine, in_specs=placed, out_specs=outs, check_vma=False)
```

```python
import functools

import jax
import jax.numpy as jnp
from jax import lax
from jax.experimental import pallas as pl
from jax.experimental.pallas import tpu as pltpu
from jax.sharding import Mesh, PartitionSpec as P

DH = 64
EPS = 1e-05
SCALE = 0.125
MASKED = -1e30
BF = jnp.bfloat16
F32 = jnp.float32
MIB = 1 << 20

BLK = ("x", "yh")
ALL = ("z", "yl", "c", "x", "yh")


def dot(a, b, ca=1, cb=0):
    return lax.dot_general(a, b, (((ca,), (cb,)), ((), ())), preferred_element_type=F32)


def cost(us):
    return pl.CostEstimate(flops=1, bytes_accessed=int(us * 0.9e6), transcendentals=0)


def params(mib):
    return pltpu.CompilerParams(vmem_limit_bytes=mib * MIB)


SMEM = pl.BlockSpec(memory_space=pltpu.SMEM)
VMEM = pl.BlockSpec(memory_space=pltpu.VMEM)
HBM = pl.BlockSpec(memory_space=pltpu.HBM)
ANY = pl.BlockSpec(memory_space=pl.ANY)


def whole(shape):
    return pl.BlockSpec(shape, lambda *_: (0,) * len(shape))


def fetch(source, target, sems, k):
    rows = source.shape[0] // 4
    copies = [
        pltpu.make_async_copy(source.at[pl.ds(i * rows, rows)], target.at[pl.ds(i * rows, rows)], sems.at[k, i])
        for i in range(4)
    ]
    for copy in copies:
        copy.start()

    def wait():
        for copy in copies:
            copy.wait()

    return wait


def normalise(v):
    mean = jnp.mean(v, axis=-1, keepdims=True)
    centred = v - mean
    var = jnp.mean(centred * centred, axis=-1, keepdims=True)
    rstd = lax.rsqrt(var + EPS)
    return centred * rstd, rstd


def norm_back(dy, xhat, rstd, gain):
    dx = dy * gain
    m1 = jnp.mean(dx, axis=-1, keepdims=True)
    m2 = jnp.mean(dx * xhat, axis=-1, keepdims=True)
    back = rstd * (dx - m1 - xhat * m2)
    dgain = jnp.sum(dy * xhat, axis=0, keepdims=True)
    dshift = jnp.sum(dy, axis=0, keepdims=True)
    return back, dgain, dshift


def triple_body(x_ref, g_ref, s_ref, wq_ref, wk_ref, wv_ref, p_ref, h_ref):
    @pl.when(pl.program_id(0) == 0)
    def _():
        xhat, _ = normalise(x_ref[...].astype(F32))
        h_ref[...] = (xhat * g_ref[0:1] + s_ref[0:1]).astype(BF)

    h = h_ref[...]
    for i, w in enumerate((wq_ref, wk_ref, wv_ref)):
        r = dot(h, w[...]).astype(BF)
        for k in range(p_ref.shape[0]):
            p_ref[k, :, i * 128 : (i + 1) * 128] = r[:, k * 128 : (k + 1) * 128]


def triple_forward(x, gain, shift, w):
    t, d = x.shape
    tile = 512
    n = d // tile
    return pl.pallas_call(
        triple_body,
        grid=(n,),
        in_specs=[
            whole((t, d)),
            whole((3, d)),
            whole((3, d)),
            pl.BlockSpec((d, tile), lambda j: (0, j)),
            pl.BlockSpec((d, tile), lambda j: (0, n + j)),
            pl.BlockSpec((d, tile), lambda j: (0, 2 * n + j)),
        ],
        out_specs=[pl.BlockSpec((tile // 128, t, 384), lambda j: (j, 0, 0)), whole((t, d))],
        out_shape=[jax.ShapeDtypeStruct((d // 128, t, 384), BF), jax.ShapeDtypeStruct((t, d), BF)],
        compiler_params=params(60),
        cost_estimate=cost(6),
        name="triple_forward",
    )(x, gain, shift, w, w, w)


def head_lanes(shape, h):
    return (lax.broadcasted_iota(jnp.int32, shape, 1) // DH) == h


def masked_head(v, h):
    return jnp.where(head_lanes(v.shape, h), v, 0.0).astype(BF)


def expon_t(k, qh, qb):
    kv = 256 * (qb + 1)
    st = dot(k[:kv], qh, 1, 1)
    kpos = lax.broadcasted_iota(jnp.int32, (256, 256), 0)
    qpos = lax.broadcasted_iota(jnp.int32, (256, 256), 1)
    last = jnp.where(kpos <= qpos, st[kv - 256 :], MASKED)
    st = jnp.concatenate([st[: kv - 256], last], axis=0) if qb else last
    top = jnp.max(st, axis=0, keepdims=True)
    e = jnp.exp(st - top)
    return e, 1.0 / jnp.sum(e, axis=0, keepdims=True)


def attend_body(p_ref, _t0, _t1, o_ref):
    rows = p_ref.shape[0] * p_ref.shape[2]
    k = p_ref[:, 0, :, 128:256].reshape(rows, 128)
    v = p_ref[:, 0, :, 256:384].reshape(rows, 128)
    vt = v.T
    for qb in range(rows // 256):
        q = p_ref[2 * qb : 2 * qb + 2, 0, :, 0:128].reshape(256, 128).astype(F32) * SCALE
        kv = 256 * (qb + 1)
        parts = []
        for h in range(2):
            e, share = expon_t(k, masked_head(q, h), qb)
            parts.append(dot(vt[h * DH : (h + 1) * DH, :kv], e.astype(BF)) * share)
        o = jnp.concatenate(parts, axis=0).T.astype(BF)
        o_ref[2 * qb : 2 * qb + 2, 0] = o.reshape(2, 128, 128)


def attend(p, *tokens):
    b, items, r, _ = p.shape
    return pl.pallas_call(
        attend_body,
        grid=(items,),
        in_specs=[
            pl.BlockSpec((b, 1, r, 384), lambda i: (0, i, 0, 0)),
            ANY,
            ANY,
        ],
        out_specs=pl.BlockSpec((b, 1, r, 128), lambda i: (0, i, 0, 0)),
        out_shape=jax.ShapeDtypeStruct((b, items, r, 128), BF),
        compiler_params=params(32),
        cost_estimate=cost(10),
        name="attend",
    )(p, *tokens)


def attend_back_body(p_ref, do_ref, _, dp_ref, dk_scr, dv_scr):
    rows = p_ref.shape[0] * p_ref.shape[2]
    blocks = p_ref.shape[0]
    k = p_ref[:, 0, :, 128:256].reshape(rows, 128)
    v = p_ref[:, 0, :, 256:384].reshape(rows, 128)
    kt = k.T
    last = rows // 256 - 1
    for qb in range(last, -1, -1):
        q = p_ref[2 * qb : 2 * qb + 2, 0, :, 0:128].reshape(256, 128).astype(F32) * SCALE
        do = do_ref[2 * qb : 2 * qb + 2, 0].reshape(256, 128).astype(F32)
        kv = 256 * (qb + 1)
        parts, qs, dos, probs, grads = [], [], [], [], []
        for h in range(2):
            qh = masked_head(q, h)
            doh = masked_head(do, h)
            e, share = expon_t(k, qh, qb)
            a = e * share
            da = dot(v[:kv], doh, 1, 1)
            dots = jnp.sum(a * da, axis=0, keepdims=True)
            ds = (a * (da - dots)).astype(BF)
            parts.append(dot(kt[h * DH : (h + 1) * DH, :kv], ds))
            qs.append(qh)
            dos.append(doh)
            probs.append(a.astype(BF))
            grads.append(ds)
        dv = dot(jnp.concatenate(probs, axis=1), jnp.concatenate(dos, axis=0))
        dk = dot(jnp.concatenate(grads, axis=1), jnp.concatenate(qs, axis=0))
        if qb == last:
            dv_scr[...] = dv
            dk_scr[...] = dk
        else:
            dv_scr[:kv] += dv
            dk_scr[:kv] += dk
        dq = (jnp.concatenate(parts, axis=0) * SCALE).T.astype(BF)
        dp_ref[2 * qb : 2 * qb + 2, 0, :, 0:128] = dq.reshape(2, 128, 128)
    dp_ref[:, 0, :, 128:256] = dk_scr[...].astype(BF).reshape(blocks, -1, 128)
    dp_ref[:, 0, :, 256:384] = dv_scr[...].astype(BF).reshape(blocks, -1, 128)


def attend_back(p, do, token):
    b, items, r, _ = p.shape
    return pl.pallas_call(
        attend_back_body,
        grid=(items,),
        in_specs=[
            pl.BlockSpec((b, 1, r, 384), lambda i: (0, i, 0, 0)),
            pl.BlockSpec((b, 1, r, 128), lambda i: (0, i, 0, 0)),
            ANY,
        ],
        out_specs=pl.BlockSpec((b, 1, r, 384), lambda i: (0, i, 0, 0)),
        out_shape=jax.ShapeDtypeStruct((b, items, r, 384), BF),
        scratch_shapes=[pltpu.VMEM((b * r, 128), F32), pltpu.VMEM((b * r, 128), F32)],
        compiler_params=params(40),
        cost_estimate=cost(0.02),
        name="attend_back",
    )(p, do, token)


def gate_body(*_):
    pass


def gate(values, *tokens):
    n = len(values)
    return pl.pallas_call(
        gate_body,
        in_specs=[ANY] * (n + len(tokens)),
        out_specs=[ANY] * n,
        out_shape=[jax.ShapeDtypeStruct(v.shape, v.dtype) for v in values],
        input_output_aliases={i: i for i in range(n)},
        cost_estimate=cost(0.5),
        name="gate",
    )(*values, *tokens)


def stack_heads(v, items):
    r = v.shape[0] // items
    parts = []
    for i in range(items):
        for h in range(2):
            parts.append(masked_head(v[i * r : (i + 1) * r], h))
    return jnp.concatenate(parts, axis=0)


def unstack_heads(v, items):
    r = v.shape[0] // (2 * items)
    parts = []
    for i in range(items):
        first = v[(2 * i) * r : (2 * i + 1) * r]
        second = v[(2 * i + 1) * r : (2 * i + 2) * r]
        parts.append(jnp.where(head_lanes(first.shape, 0), first, second))
    return jnp.concatenate(parts, axis=0)


def cross_probs_t(mk, q4, allowed):
    st = jnp.where(allowed, dot(mk, q4, 1, 1), MASKED)
    top = jnp.max(st, axis=0, keepdims=True)
    e = jnp.exp(st - top)
    return e * (1.0 / jnp.sum(e, axis=0, keepdims=True))


def allowed_mask(tseg_ref, iseg_ref, items, r):
    seg = tseg_ref[...]
    return jnp.concatenate(
        [jnp.broadcast_to(seg == iseg_ref[i], (seg.shape[0], 2 * r)) for i in range(items)], axis=1
    )


def act_grad_body(r_ref, down_ref, _, dg_ref, outer_ref):
    cot = r_ref[...]
    dg_ref[...] = dot(cot, down_ref[...], 1, 1).astype(BF)

    @pl.when(pl.program_id(0) == 0)
    def _():
        outer_ref[...] = jnp.sum(cot.astype(F32), axis=0, keepdims=True)


def act_grad(cot, down, token):
    t, d = cot.shape
    ff = down.shape[0]
    tile = 2048
    return pl.pallas_call(
        act_grad_body,
        grid=(ff // tile,),
        in_specs=[whole((t, d)), pl.BlockSpec((tile, d), lambda i: (i, 0)), ANY],
        out_specs=[pl.BlockSpec((t, tile), lambda i: (0, i)), whole((1, d))],
        out_shape=[jax.ShapeDtypeStruct((t, ff), BF), jax.ShapeDtypeStruct((1, d), F32)],
        compiler_params=params(60),
        cost_estimate=cost(400),
        name="act_grad",
    )(cot, down, token)


def trunk_body(
    iseg_ref, place_ref, x_ref, g_ref, s_ref, m_ref, tseg_ref, ib_ref, ob_ref,
    o_ref, dg_hbm, r_hbm, wo_hbm, wq_hbm, wr_hbm, up_hbm, down_hbm, _,
    inner_ref, dgain_ref, dshift_ref, y1_hbm, qc_hbm, pack_hbm, gm_hbm, mail_hbm, out_hbm, dy2_hbm,
    wo_ref, wq_ref, wr_ref, up_ref, down_ref, dg_ref, r_ref,
    y1_ref, qc_ref, pack_ref, gm_ref, mail_ref, out_ref, dy2_ref, y_scr, dh_scr, in_sems, out_sems,
):
    items = iseg_ref.shape[0]
    t, d = x_ref.shape
    r = t // items
    tile = 1024
    tiles = up_ref.shape[1] // tile
    loads = [(wo_hbm, wo_ref), (wq_hbm, wq_ref), (wr_hbm, wr_ref)]
    for j in range(tiles):
        at = pl.ds(j * tile, tile)
        loads += [(up_hbm.at[:, at], up_ref.at[:, at]), (dg_hbm.at[:, at], dg_ref.at[:, at])]
        loads += [(down_hbm.at[at], down_ref.at[at])]
    loads += [(r_hbm, r_ref)]
    waits = [fetch(source, target, in_sems, k) for k, (source, target) in enumerate(loads)]
    stores = []

    def store(source, target):
        stores.append(pltpu.make_async_copy(source, target, out_sems.at[len(stores)]))
        stores[-1].start()

    o = jnp.concatenate([o_ref[j] for j in range(o_ref.shape[0])], axis=1)
    pack_ref[:, 0:d] = o
    waits[0]()
    y1 = x_ref[...].astype(F32) + dot(o, wo_ref[...])
    y1_ref[...] = y1
    store(y1_ref, y1_hbm)
    xhat, _ = normalise(y1)
    h2 = (xhat * g_ref[1:2] + s_ref[1:2]).astype(BF)
    pack_ref[:, d : 2 * d] = h2
    waits[1]()
    qc_ref[...] = dot(h2, wq_ref[...]).astype(BF)
    store(qc_ref, qc_hbm)
    allowed = allowed_mask(tseg_ref, iseg_ref, items, r)
    for p in range(d // 128):
        at = slice(p * 128, (p + 1) * 128)
        q4 = stack_heads(qc_ref[:, at].astype(F32) * SCALE, items)
        a = cross_probs_t(m_ref[:, at], q4, allowed).astype(BF)
        o4 = dot(a, m_ref[:, d + p * 128 : d + (p + 1) * 128], 0, 0)
        pack_ref[:, 2 * d + p * 128 : 2 * d + (p + 1) * 128] = unstack_heads(o4, items).astype(BF)
    waits[2]()
    y2 = y1 + dot(pack_ref[:, 2 * d : 3 * d], wr_ref[...])
    dy2_ref[...] = y2
    xhat, _ = normalise(y2)
    h3 = (xhat * g_ref[2:3] + s_ref[2:3]).astype(BF)
    store(pack_ref, pack_hbm)
    ff = up_ref.shape[1]
    mail_ref[:, ff + ff // 2 :] = h3
    store(mail_ref.at[:, pl.ds(ff + ff // 2, d)], mail_hbm.at[:, pl.ds(ff + ff // 2, d)])
    y_scr[...] = y2 + ob_ref[...]

    c0 = 0.7978845608028654
    c1 = 0.044715
    first = place_ref[0] == 0
    for j in range(tiles):
        at = slice(j * tile, (j + 1) * tile)
        waits[3 + 3 * j]()
        waits[4 + 3 * j]()
        u = dot(h3, up_ref[:, at]) + ib_ref[:, at]
        uu = u * u
        th = jnp.tanh(u * (c0 + (c0 * c1) * uu))
        half = 0.5 + 0.5 * th
        g = (u * half).astype(BF)
        slope = half + (0.5 * u) * (1.0 - th * th) * (c0 + (3.0 * c0 * c1) * uu)
        du = (slope * dg_ref[:, at].astype(F32)).astype(BF)
        mail_ref[:, at] = du
        store(mail_ref.at[:, pl.ds(j * tile, tile)], mail_hbm.at[:, pl.ds(j * tile, tile)])
        inner = jnp.sum(du.astype(F32), axis=0, keepdims=True)
        for k in range(tile // 128):
            inner_ref[8 * j + k : 8 * j + k + 1] = inner[:, 128 * k : 128 * k + 128]
        for k in range(tile // 512):
            even, odd = g[:, 512 * k : 512 * k + 256], g[:, 512 * k + 256 : 512 * k + 512]
            half_at = j * tile // 2 + 256 * k
            gm_ref[:, half_at : half_at + 256] = jnp.where(first, even, odd)
            mail_ref[:, ff + half_at : ff + half_at + 256] = jnp.where(first, odd, even)
        waits[5 + 3 * j]()
        y_scr[...] += dot(g, down_ref[at])
        back = dot(du, up_ref[:, at], 1, 1)
        dh_scr[...] = dh_scr[...] + back if j else back
    store(gm_ref, gm_hbm)
    store(mail_ref.at[:, pl.ds(ff, ff // 2)], mail_hbm.at[:, pl.ds(ff, ff // 2)])
    out_ref[...] = y_scr[...].astype(BF)
    store(out_ref, out_hbm)
    xhat, rstd = normalise(dy2_ref[...])
    back, dgain, dshift = norm_back(dh_scr[...], xhat, rstd, g_ref[2:3])
    waits[-1]()
    dy2_ref[...] = r_ref[...].astype(F32) + back
    store(dy2_ref, dy2_hbm)
    dgain_ref[...] = dgain
    dshift_ref[...] = dshift
    for copy in stores:
        copy.wait()


def trunk(iseg, place, o, x, gain, shift, m, tseg, ib, ob, dg, cot, wo, wq, wr, up, down, token):
    t, d = x.shape
    ff = up.shape[1]
    args = (iseg, place, x, gain, shift, m, tseg, ib, ob, o, dg, cot, wo, wq, wr, up, down, token)
    small = [((ff // 128, 128), F32), ((1, d), F32), ((1, d), F32)]
    large = [((t, d), F32), ((t, d), BF), ((t, 3 * d), BF), ((t, ff // 2), BF), ((t, ff + ff // 2 + d), BF),
             ((t, d), BF), ((t, d), F32)]
    weights = [(v.shape, BF) for v in (wo, wq, wr, up, down, dg, cot)]
    return pl.pallas_call(
        trunk_body,
        in_specs=[SMEM, SMEM] + [VMEM] * 8 + [HBM] * 7 + [ANY],
        out_specs=[VMEM] * 3 + [ANY] * 7,
        out_shape=[jax.ShapeDtypeStruct(*v) for v in small + large],
        scratch_shapes=[pltpu.VMEM(*v) for v in weights + large]
        + [pltpu.VMEM((t, d), F32)] * 2
        + [pltpu.SemaphoreType.DMA((17, 4)), pltpu.SemaphoreType.DMA((12,))],
        compiler_params=params(54),
        cost_estimate=cost(0.02),
        name="trunk",
    )(*args)


def middle_back_body(
    iseg_ref, tseg_ref, g_ref, dgain_ref, dshift_ref, outer_ref, inner_ref,
    dy2_hbm, wr_hbm, m_hbm, qc_hbm, wq_hbm, y1_hbm, wo_hbm, h1_hbm, hy_hbm, _,
    thin_ref, pack_hbm, dy1_hbm, do_hbm, dm_hbm, hs_hbm,
    dy2_ref, wr_ref, m_ref, qc_ref, wq_ref, y1_ref, wo_ref, h1_ref, hy_ref,
    pack_ref, dy1_ref, do_ref, dm_ref, doc_scr, in_sems, out_sems,
):
    loads = ((dy2_hbm, dy2_ref), (wr_hbm, wr_ref), (m_hbm, m_ref), (qc_hbm, qc_ref), (wq_hbm, wq_ref),
             (y1_hbm, y1_ref), (wo_hbm, wo_ref), (h1_hbm, h1_ref), (hy_hbm, hy_ref))
    wait_dy2, wait_r, wait_m, wait_qc, wait_q, wait_y1, wait_o, wait_h1, wait_hy = (
        fetch(source, target, in_sems, k) for k, (source, target) in enumerate(loads)
    )
    stores = []

    def store(source, target):
        stores.append(pltpu.make_async_copy(source, target, out_sems.at[len(stores)]))
        stores[-1].start()

    items = iseg_ref.shape[0]
    t, d = dy2_ref.shape
    r = t // items
    texts = m_ref.shape[0]
    wait_dy2()
    b2 = dy2_ref[...].astype(BF)
    pack_ref[:t, 0:d] = b2
    wait_r()
    doc_scr[...] = dot(b2, wr_ref[...], 1, 1).astype(BF)
    allowed = allowed_mask(tseg_ref, iseg_ref, items, r)
    wait_m()
    wait_qc()
    for p in range(d // 128):
        at = slice(p * 128, (p + 1) * 128)
        av = slice(d + p * 128, d + (p + 1) * 128)
        mk = m_ref[:, at]
        q4 = stack_heads(qc_ref[:, at].astype(F32) * SCALE, items)
        do4 = stack_heads(doc_scr[:, at].astype(F32), items)
        a = cross_probs_t(mk, q4, allowed)
        da = dot(m_ref[:, av], do4, 1, 1)
        dots = jnp.sum(a * da, axis=0, keepdims=True)
        ds = (a * (da - dots)).astype(BF)
        dmk, dmv = dot(ds, q4), dot(a.astype(BF), do4)
        dm_ref[:, at] = dmk
        dm_ref[:, av] = dmv
        pack_ref[t:, at] = dmk.astype(BF)
        pack_ref[t:, av] = dmv.astype(BF)
        pack_ref[:t, d + p * 128 : d + (p + 1) * 128] = (unstack_heads(dot(ds, mk, 0, 0), items) * SCALE).astype(BF)
    store(dm_ref, dm_hbm)
    store(pack_ref.at[pl.ds(0, t), pl.ds(0, 2 * d)], pack_hbm.at[pl.ds(0, t), pl.ds(0, 2 * d)])
    wait_h1()
    wait_hy()
    store(h1_ref, hs_hbm.at[0])
    store(hy_ref, hs_hbm.at[1])
    wait_y1()
    xhat, rstd = normalise(y1_ref[...])
    wait_q()
    dh2 = dot(pack_ref[:t, d : 2 * d], wq_ref[...], 1, 1)
    back, dgain, dshift = norm_back(dh2, xhat, rstd, g_ref[1:2])
    dy1 = dy2_ref[...] + back
    dy1_ref[...] = dy1
    store(dy1_ref, dy1_hbm)
    b1 = dy1.astype(BF)
    pack_ref[:t, 2 * d : 3 * d] = b1
    store(pack_ref.at[pl.ds(0, t), pl.ds(2 * d, d)], pack_hbm.at[pl.ds(0, t), pl.ds(2 * d, d)])
    thin_ref[...] = jnp.zeros_like(thin_ref)
    for k, v in enumerate((dgain, dshift, dgain_ref[...], dshift_ref[...], outer_ref[...])):
        thin_ref[k : k + 1] = v
    n = inner_ref.shape[0]
    thin_ref[16 : 16 + n, 0:128] = inner_ref[...]
    pack_ref[t:, 2 * d : 3 * d] = jnp.zeros((texts, d), BF)
    pack_ref[t : t + 16 + n, 2 * d : 3 * d] = thin_ref[...].astype(BF)
    store(pack_ref.at[pl.ds(t, texts)], pack_hbm.at[pl.ds(t, texts)])
    wait_o()
    do = dot(b1, wo_ref[...], 1, 1).astype(BF)
    for j in range(do_ref.shape[0]):
        do_ref[j] = do[:, j * 128 : (j + 1) * 128]
    store(do_ref, do_hbm)
    for copy in stores:
        copy.wait()


def middle_back(iseg, dy2, wr, qc, m, tseg, wq, y1, gain, wo, dgain, dshift, outer, inner, h1, hy, token):
    t, d = dy2.shape
    texts = m.shape[0]
    large = (dy2, wr, m, qc, wq, y1, wo, h1, hy)
    args = (iseg, tseg, gain, dgain, dshift, outer, inner) + large + (token,)
    thin = ((16 + inner.shape[0], d), F32)
    outs = [((t + texts, 3 * d), BF), ((t, d), F32), ((d // 128, t, 128), BF), ((texts, 2 * d), F32)]
    thin, pack, dy1, do, dm, hs = pl.pallas_call(
        middle_back_body,
        in_specs=[SMEM] + [VMEM] * 6 + [HBM] * 7 + [ANY] * 3,
        out_specs=[VMEM] + [ANY] * 5,
        out_shape=[jax.ShapeDtypeStruct(*v) for v in [thin] + outs + [((2, t, d), BF)]],
        scratch_shapes=[pltpu.VMEM(v.shape, v.dtype) for v in large]
        + [pltpu.VMEM(*v) for v in outs]
        + [pltpu.VMEM((t, d), BF), pltpu.SemaphoreType.DMA((9, 4)), pltpu.SemaphoreType.DMA((8,))],
        compiler_params=params(60),
        cost_estimate=cost(400),
        name="middle_back",
    )(*args)
    return pack, dy1, do, dm, thin, hs


def triple_back_body(dp_ref, wq_ref, wk_ref, wv_ref, x_ref, g_ref, dy1_ref, _, out_ref, acc):
    step = pl.program_id(0)
    n = pl.num_programs(0)

    @pl.when(step == 0)
    def _():
        acc[...] = jnp.zeros_like(acc)

    total = acc[...]
    for i, w in enumerate((wq_ref, wk_ref, wv_ref)):
        at = slice(i * 128, (i + 1) * 128)
        total += dot(jnp.concatenate([dp_ref[k, :, at] for k in range(dp_ref.shape[0])], axis=1), w[...], 1, 1)
    acc[...] = total

    @pl.when(step == n - 1)
    def _():
        xhat, rstd = normalise(x_ref[...].astype(F32))
        back, _, _ = norm_back(acc[...], xhat, rstd, g_ref[0:1])
        out_ref[...] = dy1_ref[...] + back


def triple_back(dp, w, x, gain, dy1, token):
    t, d = x.shape
    tile = 512
    n = d // tile
    return pl.pallas_call(
        triple_back_body,
        grid=(n,),
        in_specs=[
            pl.BlockSpec((tile // 128, t, 384), lambda j: (j, 0, 0)),
            pl.BlockSpec((d, tile), lambda j: (0, j)),
            pl.BlockSpec((d, tile), lambda j: (0, n + j)),
            pl.BlockSpec((d, tile), lambda j: (0, 2 * n + j)),
            whole((t, d)),
            whole((3, d)),
            whole((t, d)),
            ANY,
        ],
        out_specs=whole((t, d)),
        out_shape=jax.ShapeDtypeStruct((t, d), F32),
        scratch_shapes=[pltpu.VMEM((t, d), F32)],
        compiler_params=params(60),
        cost_estimate=cost(4.5),
        name="triple_back",
    )(dp, w, w, w, x, gain, dy1, token)


def selector(place_ref, first, rows=512, d=1024):
    n = lax.broadcasted_iota(jnp.int32, (rows, d), 0)
    at = lax.broadcasted_iota(jnp.int32, (rows, d), 1)
    third, second, ahead = (n // 8) % 4, (n // 32) % 4, n // 128
    if first == "y":
        py, pz, px = (place_ref[3] + ahead) % 4, second, third
        yl, yh = py % 2, py // 2
    else:
        pz, yl, px, yh = (place_ref[1] + ahead) % 4, (n // 64) % 2, (n // 16) % 4, (n // 8) % 2
    source = ((((pz * 2 + yl) * 2 + place_ref[0]) * 4 + px) * 2 + yh) * 8 + n % 8
    return (at == source).astype(F32).astype(BF)


def split_rows(value, c0_ref, s1_ref, s3_ref, k1_ref, k3_ref):
    n = value.shape[0] // 8
    c0_ref[...] = value[: 2 * n]
    k1_ref[...] = value[2 * n : 3 * n]
    s1_ref[:n] = value[3 * n : 4 * n]
    s1_ref[n:] = value[4 * n : 5 * n]
    s3_ref[n:] = value[5 * n : 6 * n]
    s3_ref[:n] = value[6 * n : 7 * n]
    k3_ref[...] = value[7 * n :]


def pieces(rows, cols):
    n = rows // 8
    return [jax.ShapeDtypeStruct((k, cols), BF) for k in (2 * n, 2 * n, 2 * n, n, n)]


def mlp_grad_body(
    place_ref, mail_hbm, mail_p_hbm, g_hbm, r_hbm, r_p_hbm, _,
    c0_hbm, s1_hbm, s3_hbm, k1_hbm, k3_hbm, c0, s1, s3, k1, k3, tokens, u_ref, g_ref, r_ref, sems, in_sems,
):
    t, d = r_hbm.shape
    ff = u_ref.shape[1]
    of_u, of_g, of_h = pl.ds(0, ff), pl.ds(ff, ff // 2), pl.ds(ff + ff // 2, d)
    wait_g, wait_g_p, wait_r, wait_r_p, wait_h, wait_h_p, wait_u, wait_u_p = (
        fetch(a, b, in_sems, k)
        for k, (a, b) in enumerate((
            (g_hbm, g_ref.at[:t]), (mail_p_hbm.at[:, of_g], g_ref.at[t:]), (r_hbm, r_ref.at[:t]), (r_p_hbm, r_ref.at[t:]),
            (mail_hbm.at[:, of_h], tokens.at[:t]), (mail_p_hbm.at[:, of_h], tokens.at[t:]),
            (mail_hbm.at[:, of_u], u_ref.at[:t]), (mail_p_hbm.at[:, of_u], u_ref.at[t:]),
        ))
    )
    copies = []

    def store(source, target, owners, rows):
        copies.append(
            pltpu.make_async_copy(source.at[owners, rows], target.at[owners, rows], sems.at[len(copies)])
        )
        copies[-1].start()

    half = {(0, 0): (c0, c0_hbm, 0), (0, 1): (c0, c0_hbm, 8), (1, 0): (k1, k1_hbm, 0), (1, 1): (s1, s1_hbm, 0),
            (2, 0): (s1, s1_hbm, 8), (2, 1): (s3, s3_hbm, 8), (3, 0): (s3, s3_hbm, 0), (3, 1): (k3, k3_hbm, 0)}
    sel = selector(place_ref, "z")
    for wait in (wait_g, wait_g_p, wait_r, wait_r_p):
        wait()
    right = r_ref[...]
    for (k, yl), (ref, hbm, first) in half.items():
        column = pl.multiple_of((lax.rem(place_ref[1] + k, 4) * 2 + yl) * 256, 256)
        both = g_ref[:, pl.ds(column, 256)].T
        ref[first : first + 8, 32:64] = dot(both, right).astype(BF).reshape(8, 32, d)
        store(ref, hbm, pl.ds(first, 8), pl.ds(32, 32))
    wait_h()
    wait_h_p()
    left = dot(sel, tokens[...], 1, 1).astype(BF)
    wait_u()
    wait_u_p()
    for pair in range(2):
        value = []
        for block in (2 * pair, 2 * pair + 1):
            value.append(dot(left, u_ref[:, block * d : (block + 1) * d]).reshape(64, 8, d))
        value = jnp.concatenate(value, axis=1).astype(BF)
        for (k, yl), (ref, hbm, first) in half.items():
            ref[first : first + 8, 16 * pair : 16 * pair + 16] = value[16 * k + 8 * yl : 16 * k + 8 * yl + 8]
        for ref, hbm in ((c0, c0_hbm), (s1, s1_hbm), (s3, s3_hbm), (k1, k1_hbm), (k3, k3_hbm)):
            store(ref, hbm, pl.ds(0, ref.shape[0]), pl.ds(16 * pair, 16))
    for copy in copies:
        copy.wait()


def mlp_grad(place, mail, mail_p, gm, rm, rp, token):
    t, d = rm.shape
    ff = 2 * gm.shape[1]
    shapes = [(n, 64, d) for n in (16, 16, 16, 8, 8)]
    args = (mail, mail_p, gm, rm, rp)
    return pl.pallas_call(
        mlp_grad_body,
        in_specs=[SMEM] + [ANY] * 6,
        out_specs=[ANY] * 5,
        out_shape=[jax.ShapeDtypeStruct(v, BF) for v in shapes],
        scratch_shapes=[pltpu.VMEM(v, BF) for v in shapes]
        + [pltpu.VMEM((2 * t, n), BF) for n in (d, ff, ff // 2, d)]
        + [pltpu.SemaphoreType.DMA((18,)), pltpu.SemaphoreType.DMA((8, 4))],
        compiler_params=params(60),
        cost_estimate=cost(400),
        name="mlp_grad",
    )(place, *args, token)


def small_grad_body(
    place_ref, pack_hbm, pack_p_hbm, b_hbm, b_p_hbm, dm_ref, thin_ref, text_ref, wm_hbm, _,
    c0_hbm, s1_hbm, s3_hbm, k1_hbm, k3_hbm, c0, s1, s3, k1, k3, left_scr, right_scr, extra, wm_ref, in_sems, sems,
):
    t, d = left_scr.shape[1] // 2, left_scr.shape[2]
    rows = d // 2
    outs = ((c0, c0_hbm), (s1, s1_hbm), (s3, s3_hbm), (k1, k1_hbm), (k3, k3_hbm))
    waits = []
    for i, column in enumerate((2, 1, 0)):
        at, of = pl.ds(column * d, d), pl.ds(i * d, d)
        waits.append([
            fetch(source, target, in_sems, 4 * i + k)
            for k, (source, target) in enumerate((
                (pack_hbm.at[:, at], left_scr.at[i, :t]), (pack_p_hbm.at[:, at], left_scr.at[i, t:]),
                (b_hbm.at[:t, of], right_scr.at[i, :t]), (b_p_hbm.at[:t, of], right_scr.at[i, t:]),
            ))
        ])
    wait_extra = fetch(b_p_hbm.at[t:], extra, in_sems, 12)
    wait_wm = fetch(wm_hbm, wm_ref, in_sems, 13)
    copies = []

    def put(value, first):
        columns = pl.ds(first, value.shape[1])
        split_rows(value, *(o.at[:, columns] for o, _ in outs))

    def send(k, first, columns):
        at = pl.ds(first, columns)
        for j, (o, hbm) in enumerate(outs):
            copies.append(pltpu.make_async_copy(o.at[:, at], hbm.at[:, at], sems.at[k, j]))
            copies[-1].start()

    sel = selector(place_ref, "y")
    for i in range(3):
        for wait in waits[i]:
            wait()
        left = dot(sel, left_scr[i], 1, 1).astype(BF)
        put(dot(left, right_scr[i]).astype(BF), i * d)
        send(i, i * d, d)
    wait_extra()
    dm = (dm_ref[...] + extra[:, 0 : 2 * d].astype(F32)).astype(BF)
    left = dot(sel, text_ref[...], 1, 1).astype(BF)
    put(dot(left, dm).astype(BF), 3 * d)
    send(3, 3 * d, 2 * d)
    thin = (thin_ref[...] + extra[0:48, 2 * d : 3 * d].astype(F32)).astype(BF)
    values = dot(sel, thin[:16], 1, 1)
    lane = lax.broadcasted_iota(jnp.int32, (rows, 128), 1)
    feature = lax.broadcasted_iota(jnp.int32, (rows, d), 1).astype(F32) * sel.astype(F32)
    source = jnp.sum(feature, axis=1, keepdims=True).astype(jnp.int32)
    line = (lax.broadcasted_iota(jnp.int32, (rows, 32), 1) == source // 32).astype(F32).astype(BF)
    inner = dot(line, thin[16:48, 0:128])
    inner = jnp.where(lane // 4 == source % 32, inner, 0.0).astype(BF)
    fold_from = lax.broadcasted_iota(jnp.int32, (128, 128), 0)
    fold_to = lax.broadcasted_iota(jnp.int32, (128, 128), 1)
    fold = (fold_to == 16 + fold_from % 4).astype(F32).astype(BF)
    values = jnp.concatenate([values, jnp.zeros((rows, 112), F32)], axis=1) + dot(inner, fold)
    put(values.astype(BF), 5 * d)
    wait_wm()
    texts = dot(wm_ref[...], dm, 1, 1).astype(BF)
    put(dot(sel, texts).astype(BF), 5 * d + 128)
    send(4, 5 * d, 256)
    for copy in copies:
        copy.wait()


def small_grad(place, pack, pack_p, b, b_p, dm, thin, text, wm, token):
    t = pack.shape[0]
    d = pack.shape[1] // 3
    outs = pieces(d // 2, 5 * d + 256)
    args = (place, pack, pack_p, b, b_p, dm, thin, text, wm, token)
    return pl.pallas_call(
        small_grad_body,
        in_specs=[SMEM] + [ANY] * 4 + [VMEM] * 3 + [ANY] * 2,
        out_specs=[ANY] * 5,
        out_shape=outs,
        scratch_shapes=[pltpu.VMEM(o.shape, BF) for o in outs]
        + [pltpu.VMEM((3, 2 * t, d), BF), pltpu.VMEM((3, 2 * t, d), BF)]
        + [pltpu.VMEM((b.shape[0] - t, 3 * d), BF), pltpu.VMEM(wm.shape, BF)]
        + [pltpu.SemaphoreType.DMA((14, 4)), pltpu.SemaphoreType.DMA((5, 5))],
        compiler_params=params(60),
        cost_estimate=cost(400),
        name="small_grad",
    )(*args)


def triple_grad_body(
    src_ref, hs_ref, hx1_ref, hx2_ref, hx3_ref, dp_ref, wq_ref, wk_ref, wv_ref, g_ref, s_ref, _, mine_ref, theirs_ref
):
    d = hs_ref.shape[2]
    cols = dp_ref.shape[2]
    total = jnp.zeros((cols, d), F32)
    sums = jnp.zeros((1, cols), F32)
    for k, ref in enumerate((hs_ref, hx1_ref, hx2_ref, hx3_ref)):
        for other in range(2):
            dp = dp_ref[src_ref[2 + 2 * k + other]]
            total += dot(dp.T, ref[other])
            sums += jnp.sum(dp.astype(F32), axis=0, keepdims=True)
    total = total.T
    w = jnp.concatenate([wq_ref[...], wk_ref[...], wv_ref[...]], axis=1).astype(F32)
    norm = jnp.concatenate([g_ref[0:1], s_ref[0:1], jnp.zeros((6, d), F32)], axis=0).T
    dshift = jnp.sum(w * sums, axis=1, keepdims=True)
    dgain = (jnp.sum(w * total, axis=1, keepdims=True) - norm[:, 1:2] * dshift) / norm[:, 0:1]
    lane = lax.broadcasted_iota(jnp.int32, (d, 128), 1)
    extra = jnp.where(lane == 0, dgain, 0.0) + jnp.where(lane == 1, dshift, 0.0)
    value = jnp.concatenate([total, extra], axis=1).astype(BF).reshape(8, 2, 64, 512)
    core = src_ref[0]

    @pl.when(core == 0)
    def _():
        mine_ref[...] = value[:, 0]
        theirs_ref[...] = value[:, 1]

    @pl.when(core == 1)
    def _():
        mine_ref[...] = value[:, 1]
        theirs_ref[...] = value[:, 0]


def triple_grad(src, hs, hx, dp, w, gain, shift, token):
    _, t, d = hs.shape
    cols = dp.shape[2]
    part = jax.ShapeDtypeStruct((8, 64, 512), BF)

    def columns(k):
        return pl.BlockSpec((d, 128), lambda i, src_ref: (0, k * (d // 128) + src_ref[1]))

    return pl.pallas_call(
        triple_grad_body,
        grid_spec=pltpu.PrefetchScalarGridSpec(
            num_scalar_prefetch=1,
            grid=(1,),
            in_specs=[whole(hs.shape)] * 4
            + [whole(dp.shape), columns(0), columns(1), columns(2), whole((3, d)), whole((3, d)), ANY],
            out_specs=[whole(part.shape)] * 2,
        ),
        out_shape=[part, part],
        compiler_params=params(60),
        cost_estimate=cost(0.02),
        name="triple_grad",
    )(src, hs, *hx, dp, w, w, w, gain, shift, token)


def encoder_body(t_ref, w_ref, _, m_ref):
    m_ref[...] = dot(t_ref[...], w_ref[...]).astype(BF)


def encoder_memory(text, w, token):
    n, d = text.shape
    cols = w.shape[1]
    tile = 1024
    return pl.pallas_call(
        encoder_body,
        grid=(cols // tile,),
        in_specs=[whole((n, d)), pl.BlockSpec((d, tile), lambda j: (0, j)), ANY],
        out_specs=pl.BlockSpec((n, tile), lambda j: (0, j)),
        out_shape=jax.ShapeDtypeStruct((n, cols), BF),
        compiler_params=params(32),
        cost_estimate=cost(1.5),
        name="encoder_memory",
    )(text, w, token)


def add_two_body(a_ref, b_ref, _, out_ref):
    out_ref[...] = (a_ref[...].astype(F32) + b_ref[...].astype(F32)).astype(out_ref.dtype)


def add_two(a, b, token):
    return pl.pallas_call(
        add_two_body,
        grid=(1,),
        in_specs=[whole(a.shape), whole(a.shape), ANY],
        out_specs=whole(a.shape),
        out_shape=jax.ShapeDtypeStruct(a.shape, BF),
        compiler_params=params(60),
        cost_estimate=cost(1),
        name="add_two",
    )(a, b, token)


def add_waiting_body(k1_ref, r1_ref, k3_ref, r3_ref, *refs):
    q1_ref, q3_ref = refs[-2:]
    q1_ref[...] = (k1_ref[...].astype(F32) + r1_ref[...].astype(F32)).astype(BF)
    q3_ref[...] = (k3_ref[...].astype(F32) + r3_ref[...].astype(F32)).astype(BF)


def add_waiting(k1, r1, k3, r3, token, us, name):
    half = whole(k1.shape)
    second = pl.BlockSpec(k1.shape, lambda i: (1,) + (0,) * (len(k1.shape) - 1))
    out = jax.ShapeDtypeStruct(k1.shape, BF)
    return pl.pallas_call(
        add_waiting_body,
        grid=(1,),
        in_specs=[half, second, half, second, ANY],
        out_specs=[half, half],
        out_shape=[out, out],
        compiler_params=params(60),
        cost_estimate=cost(us),
        name=name,
    )(k1, r1, k3, r3, token)


def add_ring_body(at_ref, c0_ref, r1_ref, r3_ref, q1_ref, q3_ref, _, *refs):
    n = q1_ref.shape[0]
    first = c0_ref[:n].astype(F32) + q1_ref[...].astype(F32) + r3_ref[...].astype(F32)
    second = c0_ref[n:].astype(F32) + r1_ref[...].astype(F32) + q3_ref[...].astype(F32)
    if len(refs) == 1:
        refs[0][:n] = first.astype(BF)
        refs[0][n:] = second.astype(BF)
        return
    outs, scr = refs[:4], refs[4]
    scr[0] = first
    scr[1] = second
    for k, out in enumerate(outs):
        place = lax.rem(at_ref[0] + k, 4)
        rows = out.shape[0]
        out[...] = scr[place // 2, pl.ds(pl.multiple_of(lax.rem(place, 2) * rows, rows), rows)].astype(BF)


def add_ring(at, c0, r1, r3, q1, q3, token, cut, name):
    n = q1.shape[0]
    first = pl.BlockSpec(q1.shape, lambda i: (0,) * len(q1.shape))
    shape = (n // 2, q1.shape[1]) if cut else c0.shape
    out = jax.ShapeDtypeStruct(shape, BF)
    return pl.pallas_call(
        add_ring_body,
        grid=(1,),
        in_specs=[SMEM, whole(c0.shape), first, first, first, first, ANY],
        out_specs=[whole(shape)] * (4 if cut else 1),
        out_shape=[out] * (4 if cut else 1),
        scratch_shapes=[pltpu.VMEM((2,) + q1.shape, F32)] if cut else [],
        compiler_params=params(60),
        cost_estimate=cost(2.5),
        name=name,
    )(at, c0, r1, r3, q1, q3, token)


def add_parts_body(at_ref, a_ref, b_ref, c_ref, d_ref, _, *refs):
    outs, scr = refs[:4], refs[4]
    scr[...] = (
        (a_ref[...].astype(F32) + b_ref[...].astype(F32)) + (c_ref[...].astype(F32) + d_ref[...].astype(F32))
    ).reshape(scr.shape)
    for k, out in enumerate(outs):
        place = lax.rem(at_ref[0] + k, 4)
        rows = out.shape[0]
        out[...] = scr[pl.ds(pl.multiple_of(place * rows, rows), rows)].astype(BF)


def add_parts(at, parts, token, name):
    shape = parts[0].shape
    cols = shape[-1]
    rows = parts[0].size // cols
    out = jax.ShapeDtypeStruct((rows // 4, cols), BF)
    return pl.pallas_call(
        add_parts_body,
        grid=(1,),
        in_specs=[SMEM] + [whole(shape)] * 4 + [ANY],
        out_specs=[whole(out.shape)] * 4,
        out_shape=[out] * 4,
        scratch_shapes=[pltpu.VMEM((rows, cols), F32)],
        compiler_params=params(60),
        cost_estimate=cost(2),
        name=name,
    )(at, *parts, token)


def encoder_body(t_ref, w_ref, _, m_ref):
    m_ref[...] = dot(t_ref[...], w_ref[...]).astype(BF)


def encoder_memory(text, w, token):
    n, d = text.shape
    cols = w.shape[1]
    tile = 1024
    return pl.pallas_call(
        encoder_body,
        grid=(cols // tile,),
        in_specs=[whole((n, d)), pl.BlockSpec((d, tile), lambda j: (0, j)), ANY],
        out_specs=pl.BlockSpec((n, tile), lambda j: (0, j)),
        out_shape=jax.ShapeDtypeStruct((n, cols), BF),
        compiler_params=params(60),
        cost_estimate=cost(1.5),
        name="encoder_memory",
    )(text, w, token)


def last_triple_body(v_ref, _, out_ref, thin_ref):
    groups = 8
    d = out_ref.shape[1] // 3
    thin = jnp.zeros(thin_ref.shape, F32)
    for g in range(groups):
        total = v_ref[g].astype(F32)
        for k in range(1, v_ref.shape[0] // groups):
            total += v_ref[k * groups + g].astype(F32)
        for j in range(3):
            out_ref[:, j * d + g * 128 : j * d + g * 128 + 128] = total[:, 128 * j : 128 * j + 128]
        thin += total[:, 384:]
    thin_ref[...] = thin


def last_triple(v, token):
    _, rows, cols = v.shape
    shapes = [(rows, 8 * 384), (rows, 128)]
    return pl.pallas_call(
        last_triple_body,
        grid=(1,),
        in_specs=[whole(v.shape), ANY],
        out_specs=[whole(n) for n in shapes],
        out_shape=[jax.ShapeDtypeStruct(n, F32) for n in shapes],
        compiler_params=params(32),
        cost_estimate=cost(1),
        name="last_triple",
    )(v, token)


def last_small_body(a_ref, b_ref, c_ref, d_ref, _, *outs):
    total = (a_ref[...].astype(F32) + b_ref[...].astype(F32)) + (c_ref[...].astype(F32) + d_ref[...].astype(F32))
    first = 0
    for out in outs:
        out[...] = total[:, first : first + out.shape[1]]
        first += out.shape[1]


def last_small(parts, token):
    d = 1024
    shapes = [(8, d), (8, d), (8, d), (8, 2 * d), (8, 128), (8, 128)]
    return pl.pallas_call(
        last_small_body,
        grid=(1,),
        in_specs=[whole(parts[0].shape)] * 4 + [ANY],
        out_specs=[whole(n) for n in shapes],
        out_shape=[jax.ShapeDtypeStruct(n, F32) for n in shapes],
        compiler_params=params(32),
        cost_estimate=cost(1),
        name="last_small",
    )(*parts, token)


def last_mlp_body(v_ref, _, up_ref, down_ref):
    total = v_ref[0].astype(F32)
    for k in range(1, v_ref.shape[0]):
        total += v_ref[k].astype(F32)
    d = down_ref.shape[1]
    for block in range(4):
        up_ref[:, block * d : (block + 1) * d] = total[8 * block : 8 * block + 8]
    down_ref[...] = total[32:]


def last_mlp(v, token):
    d = v.shape[2]
    shapes = [(8, 4 * d), (32, d)]
    return pl.pallas_call(
        last_mlp_body,
        grid=(1,),
        in_specs=[whole(v.shape), ANY],
        out_specs=[whole(n) for n in shapes],
        out_shape=[jax.ShapeDtypeStruct(n, F32) for n in shapes],
        compiler_params=params(32),
        cost_estimate=cost(1.5),
        name="last_mlp",
    )(v, token)


RINGS = {"z": "z", "x": "x", "y": ("yl", "yh")}


def ring_place(axis):
    if axis == "y":
        return lax.axis_index("yh") * 2 + lax.axis_index("yl")
    return lax.axis_index(axis)


def ring_pairs(axis, step):
    if axis == "y":
        place = (0, 2, 1, 3)
        return [(place[i], place[(i + step) % 4]) for i in range(4)]
    return [(i, (i + step) % 4) for i in range(4)]


def shift_ring(v, axis, step):
    return lax.ppermute(v, RINGS[axis], ring_pairs(axis, step))


def first_step(parts, axis):
    return shift_ring(parts[1], axis, 1), shift_ring(parts[2], axis, 3)


def second_step(parts, got, axis, token, us, name):
    q1, q3 = add_waiting(parts[3], got[0], parts[4], got[1], token, us, name)
    return shift_ring(q1, axis, 1), shift_ring(q3, axis, 3), q1


def straight(parts, axis):
    return [parts[0]] + [shift_ring(parts[k], axis, k) for k in (1, 3, 2)]


def last_sum(parts):
    total = parts[0].astype(F32)
    for p in parts[1:]:
        total = total + p.astype(F32)
    return total


def swap_yh(v):
    return lax.ppermute(v, "yh", [(0, 1), (1, 0)])


def to_partner(v):
    return lax.ppermute(v, "c", [(0, 1), (1, 0)])


def local(
    image_rows, text_states, text_segment, item_segment, norm_gain, norm_shift, triple_weight, output_weight,
    query_weight, memory_weight, return_weight, up_weight, inner_bias, down_weight, outer_bias, cotangent,
):
    items, r, d = image_rows.shape
    t = items * r
    ff = up_weight.shape[1]
    x = image_rows.reshape(t, d)
    cot = cotangent.reshape(t, d)
    core, pz, px, py = lax.axis_index("c"), lax.axis_index("z"), lax.axis_index("x"), ring_place("y")
    place = jnp.stack([core, pz, px, py]).astype(jnp.int32)
    at_z, at_x = place[1:2], place[2:3]
    yh = lax.axis_index("yh")
    tseg = text_segment.reshape(-1, 1)

    p, h1 = triple_forward(x, norm_gain, norm_shift, triple_weight)
    cot_p = to_partner(cot)
    dg, outer = act_grad(cot, down_weight, p)
    p = lax.all_to_all(p, BLK, 0, 0).reshape(8, items, r, 384)
    memory = encoder_memory(text_states, memory_weight, dg)
    ready = memory[:16, :128]
    h1, arrived_p = gate((h1, p[0, 0, :16, :128]), ready, cot_p[:16, :128])
    hy = swap_yh(h1)
    o = attend(p, arrived_p, ready)
    o = lax.all_to_all(o.reshape(8, t, 128), BLK, 0, 0)
    inner, dgain2, dshift2, y1, qc, pack, gm, mail, out, dy2 = trunk(
        item_segment, place, o, x, norm_gain, norm_shift, memory, tseg, inner_bias.reshape(1, -1),
        outer_bias.reshape(1, -1), dg, cot, output_weight, query_weight, return_weight, up_weight, down_weight, hy,
    )
    mail_p, pack_p = to_partner(mail), to_partner(pack)
    b, dy1, do, dm, thin, hs = middle_back(
        item_segment, dy2, return_weight, qc, memory, tseg, query_weight, y1, norm_gain, output_weight,
        dgain2, dshift2, outer, inner, h1, hy, mail,
    )
    b_p = to_partner(b)
    do = lax.all_to_all(do, BLK, 0, 0).reshape(8, items, r, 128)
    hx1, hx3 = shift_ring(hs, "x", 1), shift_ring(hs, "x", 3)
    deep = list(mlp_grad(place, mail, mail_p, gm, cot, cot_p, b))
    deep[1], deep[2] = gate((deep[1], deep[2]), do, pack_p, b_p)
    deep_r = first_step(deep, "z")
    small = small_grad(place, pack, pack_p, b, b_p, dm, thin, text_states, memory_weight, deep[1])
    small_r = first_step(small, "y")
    (hs,) = gate((hs,), hx1, hx3, small[3])
    hx2 = shift_ring(hs, "x", 2)
    dp = attend_back(p, do, small[3])
    source = [core, px * 2 + yh]
    for k in range(4):
        sx = (px - k) % 4
        source += [sx * 2 + yh, sx * 2 + (1 - yh)]
    dp_flat = dp.reshape(8, t, 384)
    dp_home = lax.all_to_all(dp_flat, BLK, 0, 0)
    mine, theirs = triple_grad(
        jnp.stack(source).astype(jnp.int32), hs, (hx1, hx2, hx3), dp_flat, triple_weight, norm_gain, norm_shift, dp
    )
    deep_q = second_step(deep, deep_r, "z", mine, 0.02, "add_deep")
    small_q = second_step(small, small_r, "y", deep_q[2], 400, "add_small")
    part = add_two(mine, to_partner(theirs), dp_home)
    part_token = part
    part = lax.all_to_all(part.reshape(64, 8, 512), ("z", "yl", "x", "yh"), 0, 0)
    (deep_sum,) = add_ring(at_z, deep[0], *deep_r, *deep_q[:2], part_token, False, "sum_deep")
    small_sum = add_ring(at_z, small[0], *small_r, *small_q[:2], deep_sum, True, "sum_small")
    triple_sum, norm_zero = last_triple(part, small_sum[0])
    small_sum = straight(small_sum, "z")
    (deep_sum,) = gate((deep_sum,), norm_zero)
    arrived = lax.all_to_all(deep_sum, ("yl", "x", "yh"), 0, 0)
    input_grad = triple_back(dp_home, triple_weight, x, norm_gain, dy1, deep_sum)
    small_sum = add_parts(at_x, small_sum, input_grad, "parts_small")
    small_sum = straight(small_sum, "x")
    return_grad, query_grad, output_grad, memory_grad, thin_mine, texts = last_small(small_sum, norm_zero)
    text_grad = texts.T
    up_sum, down_sum = last_mlp(arrived, norm_zero)
    gains = jnp.stack([norm_zero[:, 0], thin_mine[:, 0], thin_mine[:, 2]])
    shifts = jnp.stack([norm_zero[:, 1], thin_mine[:, 1], thin_mine[:, 3]])
    outer_mine = thin_mine[:, 4]
    inner_mine = thin_mine[:, 16:20].reshape(-1)
    return (
        out.reshape(items, r, d), input_grad.reshape(items, r, d), text_grad, gains, shifts, triple_sum, output_grad,
        query_grad, memory_grad, return_grad, up_sum, inner_mine, down_sum, outer_mine,
    )


def solution(mesh):
    fine = Mesh(mesh.devices.reshape(4, 2, 2, 4, 2), ALL)
    dp = ("z", "yl", "c")
    rows = P(dp, BLK, None)
    placed = (rows, P(), P(), P(dp)) + (P(),) * 11 + (rows,)
    outs = (
        rows, rows, P(None, ALL), P(None, ALL), P(None, ALL), P(ALL, None), P(ALL, None), P(ALL, None), P(ALL, None),
        P(ALL, None), P(ALL, None), P(ALL), P(ALL, None), P(ALL),
    )
    return jax.shard_map(local, mesh=fine, in_specs=placed, out_specs=outs, check_vma=False)
```

```python
import functools

import jax
import jax.numpy as jnp
from jax import lax
from jax.experimental import pallas as pl
from jax.experimental.pallas import tpu as pltpu
from jax.sharding import Mesh, PartitionSpec as P

DH = 64
EPS = 1e-05
SCALE = 0.125
MASKED = -1e30
BF = jnp.bfloat16
F32 = jnp.float32
MIB = 1 << 20

BLK = ("x", "yh")
ALL = ("z", "yl", "c", "x", "yh")


def dot(a, b, ca=1, cb=0):
    return lax.dot_general(a, b, (((ca,), (cb,)), ((), ())), preferred_element_type=F32)


def cost(us):
    return pl.CostEstimate(flops=1, bytes_accessed=int(us * 0.9e6), transcendentals=0)


def params(mib):
    return pltpu.CompilerParams(vmem_limit_bytes=mib * MIB)


SMEM = pl.BlockSpec(memory_space=pltpu.SMEM)
VMEM = pl.BlockSpec(memory_space=pltpu.VMEM)
HBM = pl.BlockSpec(memory_space=pltpu.HBM)
ANY = pl.BlockSpec(memory_space=pl.ANY)


def whole(shape):
    return pl.BlockSpec(shape, lambda *_: (0,) * len(shape))


def fetch(source, target, sems, k):
    rows = source.shape[0] // 4
    copies = [
        pltpu.make_async_copy(source.at[pl.ds(i * rows, rows)], target.at[pl.ds(i * rows, rows)], sems.at[k, i])
        for i in range(4)
    ]
    for copy in copies:
        copy.start()

    def wait():
        for copy in copies:
            copy.wait()

    return wait


def normalise(v):
    mean = jnp.mean(v, axis=-1, keepdims=True)
    centred = v - mean
    var = jnp.mean(centred * centred, axis=-1, keepdims=True)
    rstd = lax.rsqrt(var + EPS)
    return centred * rstd, rstd


def norm_back(dy, xhat, rstd, gain):
    dx = dy * gain
    m1 = jnp.mean(dx, axis=-1, keepdims=True)
    m2 = jnp.mean(dx * xhat, axis=-1, keepdims=True)
    back = rstd * (dx - m1 - xhat * m2)
    dgain = jnp.sum(dy * xhat, axis=0, keepdims=True)
    dshift = jnp.sum(dy, axis=0, keepdims=True)
    return back, dgain, dshift


def triple_body(x_ref, g_ref, s_ref, wq_ref, wk_ref, wv_ref, p_ref, h_ref):
    @pl.when(pl.program_id(0) == 0)
    def _():
        xhat, _ = normalise(x_ref[...].astype(F32))
        h_ref[...] = (xhat * g_ref[0:1] + s_ref[0:1]).astype(BF)

    h = h_ref[...]
    for i, w in enumerate((wq_ref, wk_ref, wv_ref)):
        r = dot(h, w[...]).astype(BF)
        for k in range(p_ref.shape[0]):
            p_ref[k, :, i * 128 : (i + 1) * 128] = r[:, k * 128 : (k + 1) * 128]


def triple_forward(x, gain, shift, w):
    t, d = x.shape
    tile = 512
    n = d // tile
    return pl.pallas_call(
        triple_body,
        grid=(n,),
        in_specs=[
            whole((t, d)),
            whole((3, d)),
            whole((3, d)),
            pl.BlockSpec((d, tile), lambda j: (0, j)),
            pl.BlockSpec((d, tile), lambda j: (0, n + j)),
            pl.BlockSpec((d, tile), lambda j: (0, 2 * n + j)),
        ],
        out_specs=[pl.BlockSpec((tile // 128, t, 384), lambda j: (j, 0, 0)), whole((t, d))],
        out_shape=[jax.ShapeDtypeStruct((d // 128, t, 384), BF), jax.ShapeDtypeStruct((t, d), BF)],
        compiler_params=params(60),
        cost_estimate=cost(6),
        name="triple_forward",
    )(x, gain, shift, w, w, w)


def head_lanes(shape, h):
    return (lax.broadcasted_iota(jnp.int32, shape, 1) // DH) == h


def masked_head(v, h):
    return jnp.where(head_lanes(v.shape, h), v, 0.0).astype(BF)


def expon_t(k, qh, qb):
    kv = 256 * (qb + 1)
    st = dot(k[:kv], qh, 1, 1)
    kpos = lax.broadcasted_iota(jnp.int32, (256, 256), 0)
    qpos = lax.broadcasted_iota(jnp.int32, (256, 256), 1)
    last = jnp.where(kpos <= qpos, st[kv - 256 :], MASKED)
    st = jnp.concatenate([st[: kv - 256], last], axis=0) if qb else last
    top = jnp.max(st, axis=0, keepdims=True)
    e = jnp.exp(st - top)
    return e, 1.0 / jnp.sum(e, axis=0, keepdims=True)


def attend_body(p_ref, _t0, _t1, o_ref):
    rows = p_ref.shape[0] * p_ref.shape[2]
    k = p_ref[:, 0, :, 128:256].reshape(rows, 128)
    v = p_ref[:, 0, :, 256:384].reshape(rows, 128)
    vt = v.T
    for qb in range(rows // 256):
        q = p_ref[2 * qb : 2 * qb + 2, 0, :, 0:128].reshape(256, 128).astype(F32) * SCALE
        kv = 256 * (qb + 1)
        parts = []
        for h in range(2):
            e, share = expon_t(k, masked_head(q, h), qb)
            parts.append(dot(vt[h * DH : (h + 1) * DH, :kv], e.astype(BF)) * share)
        o = jnp.concatenate(parts, axis=0).T.astype(BF)
        o_ref[2 * qb : 2 * qb + 2, 0] = o.reshape(2, 128, 128)


def attend(p, *tokens):
    b, items, r, _ = p.shape
    return pl.pallas_call(
        attend_body,
        grid=(items,),
        in_specs=[
            pl.BlockSpec((b, 1, r, 384), lambda i: (0, i, 0, 0)),
            ANY,
            ANY,
        ],
        out_specs=pl.BlockSpec((b, 1, r, 128), lambda i: (0, i, 0, 0)),
        out_shape=jax.ShapeDtypeStruct((b, items, r, 128), BF),
        compiler_params=params(32),
        cost_estimate=cost(10),
        name="attend",
    )(p, *tokens)


def attend_back_body(p_ref, do_ref, _, dp_ref, dk_scr, dv_scr):
    rows = p_ref.shape[0] * p_ref.shape[2]
    blocks = p_ref.shape[0]
    k = p_ref[:, 0, :, 128:256].reshape(rows, 128)
    v = p_ref[:, 0, :, 256:384].reshape(rows, 128)
    kt = k.T
    last = rows // 256 - 1
    for qb in range(last, -1, -1):
        q = p_ref[2 * qb : 2 * qb + 2, 0, :, 0:128].reshape(256, 128).astype(F32) * SCALE
        do = do_ref[2 * qb : 2 * qb + 2, 0].reshape(256, 128).astype(F32)
        kv = 256 * (qb + 1)
        parts, qs, dos, probs, grads = [], [], [], [], []
        for h in range(2):
            qh = masked_head(q, h)
            doh = masked_head(do, h)
            e, share = expon_t(k, qh, qb)
            a = e * share
            da = dot(v[:kv], doh, 1, 1)
            dots = jnp.sum(a * da, axis=0, keepdims=True)
            ds = (a * (da - dots)).astype(BF)
            parts.append(dot(kt[h * DH : (h + 1) * DH, :kv], ds))
            qs.append(qh)
            dos.append(doh)
            probs.append(a.astype(BF))
            grads.append(ds)
        dv = dot(jnp.concatenate(probs, axis=1), jnp.concatenate(dos, axis=0))
        dk = dot(jnp.concatenate(grads, axis=1), jnp.concatenate(qs, axis=0))
        if qb == last:
            dv_scr[...] = dv
            dk_scr[...] = dk
        else:
            dv_scr[:kv] += dv
            dk_scr[:kv] += dk
        dq = (jnp.concatenate(parts, axis=0) * SCALE).T.astype(BF)
        dp_ref[2 * qb : 2 * qb + 2, 0, :, 0:128] = dq.reshape(2, 128, 128)
    dp_ref[:, 0, :, 128:256] = dk_scr[...].astype(BF).reshape(blocks, -1, 128)
    dp_ref[:, 0, :, 256:384] = dv_scr[...].astype(BF).reshape(blocks, -1, 128)


def attend_back(p, do, token):
    b, items, r, _ = p.shape
    return pl.pallas_call(
        attend_back_body,
        grid=(items,),
        in_specs=[
            pl.BlockSpec((b, 1, r, 384), lambda i: (0, i, 0, 0)),
            pl.BlockSpec((b, 1, r, 128), lambda i: (0, i, 0, 0)),
            ANY,
        ],
        out_specs=pl.BlockSpec((b, 1, r, 384), lambda i: (0, i, 0, 0)),
        out_shape=jax.ShapeDtypeStruct((b, items, r, 384), BF),
        scratch_shapes=[pltpu.VMEM((b * r, 128), F32), pltpu.VMEM((b * r, 128), F32)],
        compiler_params=params(40),
        cost_estimate=cost(0.02),
        name="attend_back",
    )(p, do, token)


def gate_body(*_):
    pass


def gate(values, *tokens):
    n = len(values)
    return pl.pallas_call(
        gate_body,
        in_specs=[ANY] * (n + len(tokens)),
        out_specs=[ANY] * n,
        out_shape=[jax.ShapeDtypeStruct(v.shape, v.dtype) for v in values],
        input_output_aliases={i: i for i in range(n)},
        cost_estimate=cost(0.5),
        name="gate",
    )(*values, *tokens)


def stack_heads(v, items):
    r = v.shape[0] // items
    parts = []
    for i in range(items):
        for h in range(2):
            parts.append(masked_head(v[i * r : (i + 1) * r], h))
    return jnp.concatenate(parts, axis=0)


def unstack_heads(v, items):
    r = v.shape[0] // (2 * items)
    parts = []
    for i in range(items):
        first = v[(2 * i) * r : (2 * i + 1) * r]
        second = v[(2 * i + 1) * r : (2 * i + 2) * r]
        parts.append(jnp.where(head_lanes(first.shape, 0), first, second))
    return jnp.concatenate(parts, axis=0)


def cross_probs_t(mk, q4, allowed):
    st = jnp.where(allowed, dot(mk, q4, 1, 1), MASKED)
    top = jnp.max(st, axis=0, keepdims=True)
    e = jnp.exp(st - top)
    return e * (1.0 / jnp.sum(e, axis=0, keepdims=True))


def allowed_mask(tseg_ref, iseg_ref, items, r):
    seg = tseg_ref[...]
    return jnp.concatenate(
        [jnp.broadcast_to(seg == iseg_ref[i], (seg.shape[0], 2 * r)) for i in range(items)], axis=1
    )


def act_grad_body(r_ref, down_ref, _, dg_ref, outer_ref):
    cot = r_ref[...]
    dg_ref[...] = dot(cot, down_ref[...], 1, 1).astype(BF)

    @pl.when(pl.program_id(0) == 0)
    def _():
        outer_ref[...] = jnp.sum(cot.astype(F32), axis=0, keepdims=True)


def act_grad(cot, down, token):
    t, d = cot.shape
    ff = down.shape[0]
    tile = 2048
    return pl.pallas_call(
        act_grad_body,
        grid=(ff // tile,),
        in_specs=[whole((t, d)), pl.BlockSpec((tile, d), lambda i: (i, 0)), ANY],
        out_specs=[pl.BlockSpec((t, tile), lambda i: (0, i)), whole((1, d))],
        out_shape=[jax.ShapeDtypeStruct((t, ff), BF), jax.ShapeDtypeStruct((1, d), F32)],
        compiler_params=params(60),
        cost_estimate=cost(400),
        name="act_grad",
    )(cot, down, token)


def trunk_body(
    iseg_ref, place_ref, x_ref, g_ref, s_ref, m_ref, tseg_ref, ib_ref, ob_ref,
    o_ref, dg_hbm, r_hbm, wo_hbm, wq_hbm, wr_hbm, up_hbm, down_hbm, _,
    inner_ref, dgain_ref, dshift_ref, y1_hbm, qc_hbm, pack_hbm, gm_hbm, mail_hbm, out_hbm, dy2_hbm,
    wo_ref, wq_ref, wr_ref, up_ref, down_ref, dg_ref, r_ref,
    y1_ref, qc_ref, pack_ref, gm_ref, mail_ref, out_ref, dy2_ref, y_scr, dh_scr, xhat_scr, in_sems, out_sems,
):
    items = iseg_ref.shape[0]
    t, d = x_ref.shape
    r = t // items
    tile = 2048
    tiles = up_ref.shape[1] // tile
    loads = [(wo_hbm, wo_ref), (wq_hbm, wq_ref), (wr_hbm, wr_ref)]
    for j in range(tiles):
        at = pl.ds(j * tile, tile)
        loads += [(up_hbm.at[:, at], up_ref.at[:, at]), (dg_hbm.at[:, at], dg_ref.at[:, at])]
        loads += [(down_hbm.at[at], down_ref.at[at])]
    loads += [(r_hbm, r_ref)]
    waits = [fetch(source, target, in_sems, k) for k, (source, target) in enumerate(loads)]
    stores = []

    def store(source, target):
        stores.append(pltpu.make_async_copy(source, target, out_sems.at[len(stores)]))
        stores[-1].start()

    o = jnp.concatenate([o_ref[j] for j in range(o_ref.shape[0])], axis=1)
    pack_ref[:, 0:d] = o
    waits[0]()
    y1 = x_ref[...].astype(F32) + dot(o, wo_ref[...])
    y1_ref[...] = y1
    store(y1_ref, y1_hbm)
    xhat, _ = normalise(y1)
    h2 = (xhat * g_ref[1:2] + s_ref[1:2]).astype(BF)
    pack_ref[:, d : 2 * d] = h2
    waits[1]()
    qc_ref[...] = dot(h2, wq_ref[...]).astype(BF)
    store(qc_ref, qc_hbm)
    allowed = allowed_mask(tseg_ref, iseg_ref, items, r)
    for p in range(d // 128):
        at = slice(p * 128, (p + 1) * 128)
        q4 = stack_heads(qc_ref[:, at].astype(F32) * SCALE, items)
        a = cross_probs_t(m_ref[:, at], q4, allowed).astype(BF)
        o4 = dot(a, m_ref[:, d + p * 128 : d + (p + 1) * 128], 0, 0)
        pack_ref[:, 2 * d + p * 128 : 2 * d + (p + 1) * 128] = unstack_heads(o4, items).astype(BF)
    waits[2]()
    y2 = y1 + dot(pack_ref[:, 2 * d : 3 * d], wr_ref[...])
    xhat, rstd = normalise(y2)
    xhat_scr[...] = xhat
    h3 = (xhat * g_ref[2:3] + s_ref[2:3]).astype(BF)
    store(pack_ref, pack_hbm)
    ff = up_ref.shape[1]
    mail_ref[:, ff + ff // 2 :] = h3
    store(mail_ref.at[:, pl.ds(ff + ff // 2, d)], mail_hbm.at[:, pl.ds(ff + ff // 2, d)])
    y_scr[...] = y2 + ob_ref[...]

    c0 = 0.7978845608028654
    c1 = 0.044715
    first = place_ref[0] == 0
    for j in range(tiles):
        at = slice(j * tile, (j + 1) * tile)
        waits[3 + 3 * j]()
        waits[4 + 3 * j]()
        u = dot(h3, up_ref[:, at]) + ib_ref[:, at]
        uu = u * u
        th = jnp.tanh(u * (c0 + (c0 * c1) * uu))
        half = 0.5 + 0.5 * th
        g = (u * half).astype(BF)
        slope = half + (0.5 * u) * (1.0 - th * th) * (c0 + (3.0 * c0 * c1) * uu)
        du = (slope * dg_ref[:, at].astype(F32)).astype(BF)
        mail_ref[:, at] = du
        store(mail_ref.at[:, pl.ds(j * tile, tile)], mail_hbm.at[:, pl.ds(j * tile, tile)])
        inner = jnp.sum(du.astype(F32), axis=0, keepdims=True)
        for k in range(tile // 128):
            inner_ref[16 * j + k : 16 * j + k + 1] = inner[:, 128 * k : 128 * k + 128]
        for k in range(tile // 512):
            even, odd = g[:, 512 * k : 512 * k + 256], g[:, 512 * k + 256 : 512 * k + 512]
            half_at = j * tile // 2 + 256 * k
            gm_ref[:, half_at : half_at + 256] = jnp.where(first, even, odd)
            mail_ref[:, ff + half_at : ff + half_at + 256] = jnp.where(first, odd, even)
        waits[5 + 3 * j]()
        y_scr[...] += dot(g, down_ref[at])
        back = dot(du, up_ref[:, at], 1, 1)
        dh_scr[...] = dh_scr[...] + back if j else back
    store(gm_ref, gm_hbm)
    store(mail_ref.at[:, pl.ds(ff, ff // 2)], mail_hbm.at[:, pl.ds(ff, ff // 2)])
    out_ref[...] = y_scr[...].astype(BF)
    store(out_ref, out_hbm)
    back, dgain, dshift = norm_back(dh_scr[...], xhat_scr[...], rstd, g_ref[2:3])
    waits[-1]()
    dy2_ref[...] = r_ref[...].astype(F32) + back
    store(dy2_ref, dy2_hbm)
    dgain_ref[...] = dgain
    dshift_ref[...] = dshift
    for copy in stores:
        copy.wait()


def trunk(iseg, place, o, x, gain, shift, m, tseg, ib, ob, dg, cot, wo, wq, wr, up, down, token):
    t, d = x.shape
    ff = up.shape[1]
    args = (iseg, place, x, gain, shift, m, tseg, ib, ob, o, dg, cot, wo, wq, wr, up, down, token)
    small = [((ff // 128, 128), F32), ((1, d), F32), ((1, d), F32)]
    large = [((t, d), F32), ((t, d), BF), ((t, 3 * d), BF), ((t, ff // 2), BF), ((t, ff + ff // 2 + d), BF),
             ((t, d), BF), ((t, d), F32)]
    weights = [(v.shape, BF) for v in (wo, wq, wr, up, down, dg, cot)]
    return pl.pallas_call(
        trunk_body,
        in_specs=[SMEM, SMEM] + [VMEM] * 8 + [HBM] * 7 + [ANY],
        out_specs=[VMEM] * 3 + [ANY] * 7,
        out_shape=[jax.ShapeDtypeStruct(*v) for v in small + large],
        scratch_shapes=[pltpu.VMEM(*v) for v in weights + large]
        + [pltpu.VMEM((t, d), F32)] * 3
        + [pltpu.SemaphoreType.DMA((17, 4)), pltpu.SemaphoreType.DMA((12,))],
        compiler_params=params(54),
        cost_estimate=cost(0.02),
        name="trunk",
    )(*args)


def middle_back_body(
    iseg_ref, tseg_ref, g_ref, dgain_ref, dshift_ref, outer_ref, inner_ref,
    dy2_hbm, wr_hbm, m_hbm, qc_hbm, wq_hbm, y1_hbm, wo_hbm, h1_hbm, hy_hbm, _,
    thin_ref, pack_hbm, dy1_hbm, do_hbm, dm_hbm, hs_hbm,
    dy2_ref, wr_ref, m_ref, qc_ref, wq_ref, y1_ref, wo_ref, h1_ref, hy_ref,
    pack_ref, dy1_ref, do_ref, dm_ref, doc_scr, in_sems, out_sems,
):
    loads = ((dy2_hbm, dy2_ref), (wr_hbm, wr_ref), (m_hbm, m_ref), (qc_hbm, qc_ref), (wq_hbm, wq_ref),
             (y1_hbm, y1_ref), (wo_hbm, wo_ref), (h1_hbm, h1_ref), (hy_hbm, hy_ref))
    wait_dy2, wait_r, wait_m, wait_qc, wait_q, wait_y1, wait_o, wait_h1, wait_hy = (
        fetch(source, target, in_sems, k) for k, (source, target) in enumerate(loads)
    )
    stores = []

    def store(source, target):
        stores.append(pltpu.make_async_copy(source, target, out_sems.at[len(stores)]))
        stores[-1].start()

    items = iseg_ref.shape[0]
    t, d = dy2_ref.shape
    r = t // items
    texts = m_ref.shape[0]
    wait_dy2()
    b2 = dy2_ref[...].astype(BF)
    pack_ref[:t, 0:d] = b2
    wait_r()
    doc_scr[...] = dot(b2, wr_ref[...], 1, 1).astype(BF)
    allowed = allowed_mask(tseg_ref, iseg_ref, items, r)
    wait_m()
    wait_qc()
    for p in range(d // 128):
        at = slice(p * 128, (p + 1) * 128)
        av = slice(d + p * 128, d + (p + 1) * 128)
        mk = m_ref[:, at]
        q4 = stack_heads(qc_ref[:, at].astype(F32) * SCALE, items)
        do4 = stack_heads(doc_scr[:, at].astype(F32), items)
        a = cross_probs_t(mk, q4, allowed)
        da = dot(m_ref[:, av], do4, 1, 1)
        dots = jnp.sum(a * da, axis=0, keepdims=True)
        ds = (a * (da - dots)).astype(BF)
        dmk, dmv = dot(ds, q4), dot(a.astype(BF), do4)
        dm_ref[:, at] = dmk
        dm_ref[:, av] = dmv
        pack_ref[t:, at] = dmk.astype(BF)
        pack_ref[t:, av] = dmv.astype(BF)
        pack_ref[:t, d + p * 128 : d + (p + 1) * 128] = (unstack_heads(dot(ds, mk, 0, 0), items) * SCALE).astype(BF)
    store(dm_ref, dm_hbm)
    store(pack_ref.at[pl.ds(0, t), pl.ds(0, 2 * d)], pack_hbm.at[pl.ds(0, t), pl.ds(0, 2 * d)])
    wait_h1()
    wait_hy()
    store(h1_ref, hs_hbm.at[0])
    store(hy_ref, hs_hbm.at[1])
    wait_y1()
    xhat, rstd = normalise(y1_ref[...])
    wait_q()
    dh2 = dot(pack_ref[:t, d : 2 * d], wq_ref[...], 1, 1)
    back, dgain, dshift = norm_back(dh2, xhat, rstd, g_ref[1:2])
    dy1 = dy2_ref[...] + back
    dy1_ref[...] = dy1
    store(dy1_ref, dy1_hbm)
    b1 = dy1.astype(BF)
    pack_ref[:t, 2 * d : 3 * d] = b1
    store(pack_ref.at[pl.ds(0, t), pl.ds(2 * d, d)], pack_hbm.at[pl.ds(0, t), pl.ds(2 * d, d)])
    thin_ref[...] = jnp.zeros_like(thin_ref)
    for k, v in enumerate((dgain, dshift, dgain_ref[...], dshift_ref[...], outer_ref[...])):
        thin_ref[k : k + 1] = v
    n = inner_ref.shape[0]
    thin_ref[16 : 16 + n, 0:128] = inner_ref[...]
    pack_ref[t:, 2 * d : 3 * d] = jnp.zeros((texts, d), BF)
    pack_ref[t : t + 16 + n, 2 * d : 3 * d] = thin_ref[...].astype(BF)
    store(pack_ref.at[pl.ds(t, texts)], pack_hbm.at[pl.ds(t, texts)])
    wait_o()
    do = dot(b1, wo_ref[...], 1, 1).astype(BF)
    for j in range(do_ref.shape[0]):
        do_ref[j] = do[:, j * 128 : (j + 1) * 128]
    store(do_ref, do_hbm)
    for copy in stores:
        copy.wait()


def middle_back(iseg, dy2, wr, qc, m, tseg, wq, y1, gain, wo, dgain, dshift, outer, inner, h1, hy, token):
    t, d = dy2.shape
    texts = m.shape[0]
    large = (dy2, wr, m, qc, wq, y1, wo, h1, hy)
    args = (iseg, tseg, gain, dgain, dshift, outer, inner) + large + (token,)
    thin = ((16 + inner.shape[0], d), F32)
    outs = [((t + texts, 3 * d), BF), ((t, d), F32), ((d // 128, t, 128), BF), ((texts, 2 * d), F32)]
    thin, pack, dy1, do, dm, hs = pl.pallas_call(
        middle_back_body,
        in_specs=[SMEM] + [VMEM] * 6 + [HBM] * 7 + [ANY] * 3,
        out_specs=[VMEM] + [ANY] * 5,
        out_shape=[jax.ShapeDtypeStruct(*v) for v in [thin] + outs + [((2, t, d), BF)]],
        scratch_shapes=[pltpu.VMEM(v.shape, v.dtype) for v in large]
        + [pltpu.VMEM(*v) for v in outs]
        + [pltpu.VMEM((t, d), BF), pltpu.SemaphoreType.DMA((9, 4)), pltpu.SemaphoreType.DMA((8,))],
        compiler_params=params(60),
        cost_estimate=cost(400),
        name="middle_back",
    )(*args)
    return pack, dy1, do, dm, thin, hs


def triple_back_body(dp_ref, wq_ref, wk_ref, wv_ref, x_ref, g_ref, dy1_ref, _, out_ref, acc):
    step = pl.program_id(0)
    n = pl.num_programs(0)

    @pl.when(step == 0)
    def _():
        acc[...] = jnp.zeros_like(acc)

    total = acc[...]
    for i, w in enumerate((wq_ref, wk_ref, wv_ref)):
        at = slice(i * 128, (i + 1) * 128)
        total += dot(jnp.concatenate([dp_ref[k, :, at] for k in range(dp_ref.shape[0])], axis=1), w[...], 1, 1)
    acc[...] = total

    @pl.when(step == n - 1)
    def _():
        xhat, rstd = normalise(x_ref[...].astype(F32))
        back, _, _ = norm_back(acc[...], xhat, rstd, g_ref[0:1])
        out_ref[...] = dy1_ref[...] + back


def triple_back(dp, w, x, gain, dy1, token):
    t, d = x.shape
    tile = 512
    n = d // tile
    return pl.pallas_call(
        triple_back_body,
        grid=(n,),
        in_specs=[
            pl.BlockSpec((tile // 128, t, 384), lambda j: (j, 0, 0)),
            pl.BlockSpec((d, tile), lambda j: (0, j)),
            pl.BlockSpec((d, tile), lambda j: (0, n + j)),
            pl.BlockSpec((d, tile), lambda j: (0, 2 * n + j)),
            whole((t, d)),
            whole((3, d)),
            whole((t, d)),
            ANY,
        ],
        out_specs=whole((t, d)),
        out_shape=jax.ShapeDtypeStruct((t, d), F32),
        scratch_shapes=[pltpu.VMEM((t, d), F32)],
        compiler_params=params(60),
        cost_estimate=cost(4.5),
        name="triple_back",
    )(dp, w, w, w, x, gain, dy1, token)


def selector(place_ref, first, rows=512, d=1024):
    n = lax.broadcasted_iota(jnp.int32, (rows, d), 0)
    at = lax.broadcasted_iota(jnp.int32, (rows, d), 1)
    third, second, ahead = (n // 8) % 4, (n // 32) % 4, n // 128
    if first == "y":
        py, pz, px = (place_ref[3] + ahead) % 4, second, third
        yl, yh = py % 2, py // 2
    else:
        pz, yl, px, yh = (place_ref[1] + ahead) % 4, (n // 64) % 2, (n // 16) % 4, (n // 8) % 2
    source = ((((pz * 2 + yl) * 2 + place_ref[0]) * 4 + px) * 2 + yh) * 8 + n % 8
    return (at == source).astype(F32).astype(BF)


def split_rows(value, c0_ref, s1_ref, s3_ref, k1_ref, k3_ref):
    n = value.shape[0] // 8
    c0_ref[...] = value[: 2 * n]
    k1_ref[...] = value[2 * n : 3 * n]
    s1_ref[:n] = value[3 * n : 4 * n]
    s1_ref[n:] = value[4 * n : 5 * n]
    s3_ref[n:] = value[5 * n : 6 * n]
    s3_ref[:n] = value[6 * n : 7 * n]
    k3_ref[...] = value[7 * n :]


def pieces(rows, cols):
    n = rows // 8
    return [jax.ShapeDtypeStruct((k, cols), BF) for k in (2 * n, 2 * n, 2 * n, n, n)]


def mlp_grad_body(
    place_ref, mail_hbm, mail_p_hbm, g_hbm, r_hbm, r_p_hbm, _,
    c0_hbm, s1_hbm, s3_hbm, k1_hbm, k3_hbm, c0, s1, s3, k1, k3, tokens, u_ref, g_ref, r_ref, sems, in_sems,
):
    t, d = r_hbm.shape
    ff = u_ref.shape[1]
    of_u, of_g, of_h = pl.ds(0, ff), pl.ds(ff, ff // 2), pl.ds(ff + ff // 2, d)
    wait_g, wait_g_p, wait_r, wait_r_p, wait_h, wait_h_p, wait_u, wait_u_p = (
        fetch(a, b, in_sems, k)
        for k, (a, b) in enumerate((
            (g_hbm, g_ref.at[:t]), (mail_p_hbm.at[:, of_g], g_ref.at[t:]), (r_hbm, r_ref.at[:t]), (r_p_hbm, r_ref.at[t:]),
            (mail_hbm.at[:, of_h], tokens.at[:t]), (mail_p_hbm.at[:, of_h], tokens.at[t:]),
            (mail_hbm.at[:, of_u], u_ref.at[:t]), (mail_p_hbm.at[:, of_u], u_ref.at[t:]),
        ))
    )
    copies = []

    def store(source, target, owners, rows):
        copies.append(
            pltpu.make_async_copy(source.at[owners, rows], target.at[owners, rows], sems.at[len(copies)])
        )
        copies[-1].start()

    half = {(0, 0): (c0, c0_hbm, 0), (0, 1): (c0, c0_hbm, 8), (1, 0): (k1, k1_hbm, 0), (1, 1): (s1, s1_hbm, 0),
            (2, 0): (s1, s1_hbm, 8), (2, 1): (s3, s3_hbm, 8), (3, 0): (s3, s3_hbm, 0), (3, 1): (k3, k3_hbm, 0)}
    sel = selector(place_ref, "z")
    for wait in (wait_g, wait_g_p, wait_r, wait_r_p):
        wait()
    right = r_ref[...]
    for (k, yl), (ref, hbm, first) in half.items():
        column = pl.multiple_of((lax.rem(place_ref[1] + k, 4) * 2 + yl) * 256, 256)
        both = g_ref[:, pl.ds(column, 256)].T
        ref[first : first + 8, 32:64] = dot(both, right).astype(BF).reshape(8, 32, d)
        store(ref, hbm, pl.ds(first, 8), pl.ds(32, 32))
    wait_h()
    wait_h_p()
    left = dot(sel, tokens[...], 1, 1).astype(BF)
    wait_u()
    wait_u_p()
    for pair in range(2):
        value = []
        for block in (2 * pair, 2 * pair + 1):
            value.append(dot(left, u_ref[:, block * d : (block + 1) * d]).reshape(64, 8, d))
        value = jnp.concatenate(value, axis=1).astype(BF)
        for (k, yl), (ref, hbm, first) in half.items():
            ref[first : first + 8, 16 * pair : 16 * pair + 16] = value[16 * k + 8 * yl : 16 * k + 8 * yl + 8]
        for ref, hbm in ((c0, c0_hbm), (s1, s1_hbm), (s3, s3_hbm), (k1, k1_hbm), (k3, k3_hbm)):
            store(ref, hbm, pl.ds(0, ref.shape[0]), pl.ds(16 * pair, 16))
    for copy in copies:
        copy.wait()


def mlp_grad(place, mail, mail_p, gm, rm, rp, token):
    t, d = rm.shape
    ff = 2 * gm.shape[1]
    shapes = [(n, 64, d) for n in (16, 16, 16, 8, 8)]
    args = (mail, mail_p, gm, rm, rp)
    return pl.pallas_call(
        mlp_grad_body,
        in_specs=[SMEM] + [ANY] * 6,
        out_specs=[ANY] * 5,
        out_shape=[jax.ShapeDtypeStruct(v, BF) for v in shapes],
        scratch_shapes=[pltpu.VMEM(v, BF) for v in shapes]
        + [pltpu.VMEM((2 * t, n), BF) for n in (d, ff, ff // 2, d)]
        + [pltpu.SemaphoreType.DMA((18,)), pltpu.SemaphoreType.DMA((8, 4))],
        compiler_params=params(60),
        cost_estimate=cost(400),
        name="mlp_grad",
    )(place, *args, token)


def small_grad_body(
    place_ref, pack_hbm, pack_p_hbm, b_hbm, b_p_hbm, dm_ref, thin_ref, text_ref, wm_hbm, _,
    c0_hbm, s1_hbm, s3_hbm, k1_hbm, k3_hbm, c0, s1, s3, k1, k3, left_scr, right_scr, extra, wm_ref, in_sems, sems,
):
    t, d = left_scr.shape[1] // 2, left_scr.shape[2]
    rows = d // 2
    outs = ((c0, c0_hbm), (s1, s1_hbm), (s3, s3_hbm), (k1, k1_hbm), (k3, k3_hbm))
    waits = []
    for i, column in enumerate((2, 1, 0)):
        at, of = pl.ds(column * d, d), pl.ds(i * d, d)
        waits.append([
            fetch(source, target, in_sems, 4 * i + k)
            for k, (source, target) in enumerate((
                (pack_hbm.at[:, at], left_scr.at[i, :t]), (pack_p_hbm.at[:, at], left_scr.at[i, t:]),
                (b_hbm.at[:t, of], right_scr.at[i, :t]), (b_p_hbm.at[:t, of], right_scr.at[i, t:]),
            ))
        ])
    wait_extra = fetch(b_p_hbm.at[t:], extra, in_sems, 12)
    wait_wm = fetch(wm_hbm, wm_ref, in_sems, 13)
    copies = []

    def put(value, first):
        columns = pl.ds(first, value.shape[1])
        split_rows(value, *(o.at[:, columns] for o, _ in outs))

    def send(k, first, columns):
        at = pl.ds(first, columns)
        for j, (o, hbm) in enumerate(outs):
            copies.append(pltpu.make_async_copy(o.at[:, at], hbm.at[:, at], sems.at[k, j]))
            copies[-1].start()

    sel = selector(place_ref, "y")
    for i in range(3):
        for wait in waits[i]:
            wait()
        left = dot(sel, left_scr[i], 1, 1).astype(BF)
        put(dot(left, right_scr[i]).astype(BF), i * d)
        send(i, i * d, d)
    wait_extra()
    dm = (dm_ref[...] + extra[:, 0 : 2 * d].astype(F32)).astype(BF)
    left = dot(sel, text_ref[...], 1, 1).astype(BF)
    put(dot(left, dm).astype(BF), 3 * d)
    send(3, 3 * d, 2 * d)
    thin = (thin_ref[...] + extra[0:48, 2 * d : 3 * d].astype(F32)).astype(BF)
    values = dot(sel, thin[:16], 1, 1)
    lane = lax.broadcasted_iota(jnp.int32, (rows, 128), 1)
    feature = lax.broadcasted_iota(jnp.int32, (rows, d), 1).astype(F32) * sel.astype(F32)
    source = jnp.sum(feature, axis=1, keepdims=True).astype(jnp.int32)
    line = (lax.broadcasted_iota(jnp.int32, (rows, 32), 1) == source // 32).astype(F32).astype(BF)
    inner = dot(line, thin[16:48, 0:128])
    inner = jnp.where(lane // 4 == source % 32, inner, 0.0).astype(BF)
    fold_from = lax.broadcasted_iota(jnp.int32, (128, 128), 0)
    fold_to = lax.broadcasted_iota(jnp.int32, (128, 128), 1)
    fold = (fold_to == 16 + fold_from % 4).astype(F32).astype(BF)
    values = jnp.concatenate([values, jnp.zeros((rows, 112), F32)], axis=1) + dot(inner, fold)
    put(values.astype(BF), 5 * d)
    wait_wm()
    texts = dot(wm_ref[...], dm, 1, 1).astype(BF)
    put(dot(sel, texts).astype(BF), 5 * d + 128)
    send(4, 5 * d, 256)
    for copy in copies:
        copy.wait()


def small_grad(place, pack, pack_p, b, b_p, dm, thin, text, wm, token):
    t = pack.shape[0]
    d = pack.shape[1] // 3
    outs = pieces(d // 2, 5 * d + 256)
    args = (place, pack, pack_p, b, b_p, dm, thin, text, wm, token)
    return pl.pallas_call(
        small_grad_body,
        in_specs=[SMEM] + [ANY] * 4 + [VMEM] * 3 + [ANY] * 2,
        out_specs=[ANY] * 5,
        out_shape=outs,
        scratch_shapes=[pltpu.VMEM(o.shape, BF) for o in outs]
        + [pltpu.VMEM((3, 2 * t, d), BF), pltpu.VMEM((3, 2 * t, d), BF)]
        + [pltpu.VMEM((b.shape[0] - t, 3 * d), BF), pltpu.VMEM(wm.shape, BF)]
        + [pltpu.SemaphoreType.DMA((14, 4)), pltpu.SemaphoreType.DMA((5, 5))],
        compiler_params=params(60),
        cost_estimate=cost(400),
        name="small_grad",
    )(*args)


def triple_grad_body(
    src_ref, hs_ref, hx1_ref, hx2_ref, hx3_ref, dp_ref, wq_ref, wk_ref, wv_ref, g_ref, s_ref, _, mine_ref, theirs_ref
):
    d = hs_ref.shape[2]
    cols = dp_ref.shape[2]
    total = jnp.zeros((cols, d), F32)
    sums = jnp.zeros((1, cols), F32)
    for k, ref in enumerate((hs_ref, hx1_ref, hx2_ref, hx3_ref)):
        for other in range(2):
            dp = dp_ref[src_ref[2 + 2 * k + other]]
            total += dot(dp.T, ref[other])
            sums += jnp.sum(dp.astype(F32), axis=0, keepdims=True)
    total = total.T
    w = jnp.concatenate([wq_ref[...], wk_ref[...], wv_ref[...]], axis=1).astype(F32)
    norm = jnp.concatenate([g_ref[0:1], s_ref[0:1], jnp.zeros((6, d), F32)], axis=0).T
    dshift = jnp.sum(w * sums, axis=1, keepdims=True)
    dgain = (jnp.sum(w * total, axis=1, keepdims=True) - norm[:, 1:2] * dshift) / norm[:, 0:1]
    lane = lax.broadcasted_iota(jnp.int32, (d, 128), 1)
    extra = jnp.where(lane == 0, dgain, 0.0) + jnp.where(lane == 1, dshift, 0.0)
    value = jnp.concatenate([total, extra], axis=1).astype(BF).reshape(8, 2, 64, 512)
    core = src_ref[0]

    @pl.when(core == 0)
    def _():
        mine_ref[...] = value[:, 0]
        theirs_ref[...] = value[:, 1]

    @pl.when(core == 1)
    def _():
        mine_ref[...] = value[:, 1]
        theirs_ref[...] = value[:, 0]


def triple_grad(src, hs, hx, dp, w, gain, shift, token):
    _, t, d = hs.shape
    cols = dp.shape[2]
    part = jax.ShapeDtypeStruct((8, 64, 512), BF)

    def columns(k):
        return pl.BlockSpec((d, 128), lambda i, src_ref: (0, k * (d // 128) + src_ref[1]))

    return pl.pallas_call(
        triple_grad_body,
        grid_spec=pltpu.PrefetchScalarGridSpec(
            num_scalar_prefetch=1,
            grid=(1,),
            in_specs=[whole(hs.shape)] * 4
            + [whole(dp.shape), columns(0), columns(1), columns(2), whole((3, d)), whole((3, d)), ANY],
            out_specs=[whole(part.shape)] * 2,
        ),
        out_shape=[part, part],
        compiler_params=params(60),
        cost_estimate=cost(0.02),
        name="triple_grad",
    )(src, hs, *hx, dp, w, w, w, gain, shift, token)


def encoder_body(t_ref, w_ref, _, m_ref):
    m_ref[...] = dot(t_ref[...], w_ref[...]).astype(BF)


def encoder_memory(text, w, token):
    n, d = text.shape
    cols = w.shape[1]
    tile = 1024
    return pl.pallas_call(
        encoder_body,
        grid=(cols // tile,),
        in_specs=[whole((n, d)), pl.BlockSpec((d, tile), lambda j: (0, j)), ANY],
        out_specs=pl.BlockSpec((n, tile), lambda j: (0, j)),
        out_shape=jax.ShapeDtypeStruct((n, cols), BF),
        compiler_params=params(32),
        cost_estimate=cost(1.5),
        name="encoder_memory",
    )(text, w, token)


def add_two_body(a_ref, b_ref, _, out_ref):
    out_ref[...] = (a_ref[...].astype(F32) + b_ref[...].astype(F32)).astype(out_ref.dtype)


def add_two(a, b, token):
    return pl.pallas_call(
        add_two_body,
        grid=(1,),
        in_specs=[whole(a.shape), whole(a.shape), ANY],
        out_specs=whole(a.shape),
        out_shape=jax.ShapeDtypeStruct(a.shape, BF),
        compiler_params=params(60),
        cost_estimate=cost(1),
        name="add_two",
    )(a, b, token)


def add_slices_body(plan, chunk, n_in, *refs):
    inputs, outs, (scr, out_scr, in_sems, out_sems) = refs[:n_in], refs[n_in + 1 : -4], refs[-4:]
    loads = []
    for i, (_, _, terms) in enumerate(plan):
        for j, (which, first) in enumerate(terms):
            loads.append(
                pltpu.make_async_copy(inputs[which].at[pl.ds(first, chunk)], scr.at[i, j], in_sems.at[i, j])
            )
            loads[-1].start()
    stores = []
    at = 0
    for i, (which, first, terms) in enumerate(plan):
        for load in loads[at : at + len(terms)]:
            load.wait()
        at += len(terms)
        total = scr[i, 0].astype(F32)
        for j in range(1, len(terms)):
            total += scr[i, j].astype(F32)
        out_scr[i] = total.astype(BF)
        stores.append(pltpu.make_async_copy(out_scr.at[i], outs[which].at[pl.ds(first, chunk)], out_sems.at[i]))
        stores[-1].start()
    for copy in stores:
        copy.wait()


def add_slices(inputs, outs, plan, chunk, token, us, name):
    block = (chunk,) + tuple(inputs[0].shape[1:])
    terms = len(plan[0][2])
    return pl.pallas_call(
        functools.partial(add_slices_body, plan, chunk, len(inputs)),
        in_specs=[ANY] * (len(inputs) + 1),
        out_specs=[ANY] * len(outs),
        out_shape=[jax.ShapeDtypeStruct(v, BF) for v in outs],
        scratch_shapes=[
            pltpu.VMEM((len(plan), terms) + block, BF),
            pltpu.VMEM((len(plan),) + block, BF),
            pltpu.SemaphoreType.DMA((len(plan), terms)),
            pltpu.SemaphoreType.DMA((len(plan),)),
        ],
        compiler_params=params(60),
        cost_estimate=cost(us),
        name=name,
    )(*inputs, token)


def add_waiting(k1, r1, k3, r3, token, us, name):
    n = k1.shape[0]
    chunk = n // 4
    plan = []
    for first in range(0, n, chunk):
        plan += [(0, first, ((0, first), (1, n + first))), (1, first, ((2, first), (3, n + first)))]
    return add_slices((k1, r1, k3, r3), (k1.shape, k1.shape), tuple(plan), chunk, token, us, name)


def add_deep(c0, r1, r3, q1, q3, token):
    n = q1.shape[0]
    chunk = n // 4
    plan = []
    for first in range(0, n, chunk):
        plan += [(0, first, ((0, first), (3, first), (2, first))), (0, n + first, ((0, n + first), (1, first), (4, first)))]
    return add_slices((c0, r1, r3, q1, q3), (c0.shape,), tuple(plan), chunk, token, 2.5, "sum_deep")


def add_ring_body(at_ref, c0_ref, r1_ref, r3_ref, q1_ref, q3_ref, _, *refs):
    n = q1_ref.shape[0]
    first = c0_ref[:n].astype(F32) + q1_ref[...].astype(F32) + r3_ref[...].astype(F32)
    second = c0_ref[n:].astype(F32) + r1_ref[...].astype(F32) + q3_ref[...].astype(F32)
    if len(refs) == 1:
        refs[0][:n] = first.astype(BF)
        refs[0][n:] = second.astype(BF)
        return
    outs, scr = refs[:4], refs[4]
    scr[0] = first
    scr[1] = second
    for k, out in enumerate(outs):
        place = lax.rem(at_ref[0] + k, 4)
        rows = out.shape[0]
        out[...] = scr[place // 2, pl.ds(pl.multiple_of(lax.rem(place, 2) * rows, rows), rows)].astype(BF)


def add_ring(at, c0, r1, r3, q1, q3, token, cut, name):
    n = q1.shape[0]
    first = pl.BlockSpec(q1.shape, lambda i: (0,) * len(q1.shape))
    shape = (n // 2, q1.shape[1]) if cut else c0.shape
    out = jax.ShapeDtypeStruct(shape, BF)
    return pl.pallas_call(
        add_ring_body,
        grid=(1,),
        in_specs=[SMEM, whole(c0.shape), first, first, first, first, ANY],
        out_specs=[whole(shape)] * (4 if cut else 1),
        out_shape=[out] * (4 if cut else 1),
        scratch_shapes=[pltpu.VMEM((2,) + q1.shape, F32)] if cut else [],
        compiler_params=params(60),
        cost_estimate=cost(2.5),
        name=name,
    )(at, c0, r1, r3, q1, q3, token)


def add_parts_body(at_ref, a_ref, b_ref, c_ref, d_ref, _, *refs):
    outs, scr = refs[:4], refs[4]
    scr[...] = (
        (a_ref[...].astype(F32) + b_ref[...].astype(F32)) + (c_ref[...].astype(F32) + d_ref[...].astype(F32))
    ).reshape(scr.shape)
    for k, out in enumerate(outs):
        place = lax.rem(at_ref[0] + k, 4)
        rows = out.shape[0]
        out[...] = scr[pl.ds(pl.multiple_of(place * rows, rows), rows)].astype(BF)


def add_parts(at, parts, token, name):
    shape = parts[0].shape
    cols = shape[-1]
    rows = parts[0].size // cols
    out = jax.ShapeDtypeStruct((rows // 4, cols), BF)
    return pl.pallas_call(
        add_parts_body,
        grid=(1,),
        in_specs=[SMEM] + [whole(shape)] * 4 + [ANY],
        out_specs=[whole(out.shape)] * 4,
        out_shape=[out] * 4,
        scratch_shapes=[pltpu.VMEM((rows, cols), F32)],
        compiler_params=params(60),
        cost_estimate=cost(2),
        name=name,
    )(at, *parts, token)


def encoder_body(t_ref, w_ref, _, m_ref):
    m_ref[...] = dot(t_ref[...], w_ref[...]).astype(BF)


def encoder_memory(text, w, token):
    n, d = text.shape
    cols = w.shape[1]
    tile = 1024
    return pl.pallas_call(
        encoder_body,
        grid=(cols // tile,),
        in_specs=[whole((n, d)), pl.BlockSpec((d, tile), lambda j: (0, j)), ANY],
        out_specs=pl.BlockSpec((n, tile), lambda j: (0, j)),
        out_shape=jax.ShapeDtypeStruct((n, cols), BF),
        compiler_params=params(60),
        cost_estimate=cost(1.5),
        name="encoder_memory",
    )(text, w, token)


def last_triple_body(v_ref, _, out_ref, thin_ref):
    groups = 8
    d = out_ref.shape[1] // 3
    thin = jnp.zeros(thin_ref.shape, F32)
    for g in range(groups):
        total = v_ref[g].astype(F32)
        for k in range(1, v_ref.shape[0] // groups):
            total += v_ref[k * groups + g].astype(F32)
        for j in range(3):
            out_ref[:, j * d + g * 128 : j * d + g * 128 + 128] = total[:, 128 * j : 128 * j + 128]
        thin += total[:, 384:]
    thin_ref[...] = thin


def last_triple(v, token):
    _, rows, cols = v.shape
    shapes = [(rows, 8 * 384), (rows, 128)]
    return pl.pallas_call(
        last_triple_body,
        grid=(1,),
        in_specs=[whole(v.shape), ANY],
        out_specs=[whole(n) for n in shapes],
        out_shape=[jax.ShapeDtypeStruct(n, F32) for n in shapes],
        compiler_params=params(32),
        cost_estimate=cost(1),
        name="last_triple",
    )(v, token)


def last_small_body(
    a_ref, b_ref, c_ref, d_ref, zero_ref, return_ref, query_ref, output_ref, memory_ref, text_ref, gain_ref, shift_ref,
    outer_ref, inner_ref,
):
    total = (a_ref[...].astype(F32) + b_ref[...].astype(F32)) + (c_ref[...].astype(F32) + d_ref[...].astype(F32))
    first = 0
    for out in (return_ref, query_ref, output_ref, memory_ref):
        out[...] = total[:, first : first + out.shape[1]]
        first += out.shape[1]
    thin = total[:, first : first + 128]
    text_ref[...] = total[:, first + 128 :].T
    rows, zero = thin.T, zero_ref[...].T
    gain_ref[...] = jnp.concatenate([zero[0:1], rows[0:1], rows[2:3]], axis=0)
    shift_ref[...] = jnp.concatenate([zero[1:2], rows[1:2], rows[3:4]], axis=0)
    outer_ref[...] = rows[4:5]
    inner_ref[...] = thin[:, 16:20]


def last_small(parts, zero):
    d = 1024
    shapes = [(8, d), (8, d), (8, d), (8, 2 * d), (128, 8), (3, 8), (3, 8), (1, 8), (8, 4)]
    return pl.pallas_call(
        last_small_body,
        grid=(1,),
        in_specs=[whole(parts[0].shape)] * 4 + [whole(zero.shape)],
        out_specs=[whole(n) for n in shapes],
        out_shape=[jax.ShapeDtypeStruct(n, F32) for n in shapes],
        compiler_params=params(32),
        cost_estimate=cost(1),
        name="last_small",
    )(*parts, zero)


def last_mlp_body(v_ref, _, up_ref, down_ref):
    total = v_ref[0].astype(F32)
    for k in range(1, v_ref.shape[0]):
        total += v_ref[k].astype(F32)
    d = down_ref.shape[1]
    for block in range(4):
        up_ref[:, block * d : (block + 1) * d] = total[8 * block : 8 * block + 8]
    down_ref[...] = total[32:]


def last_mlp(v, token):
    d = v.shape[2]
    shapes = [(8, 4 * d), (32, d)]
    return pl.pallas_call(
        last_mlp_body,
        grid=(1,),
        in_specs=[whole(v.shape), ANY],
        out_specs=[whole(n) for n in shapes],
        out_shape=[jax.ShapeDtypeStruct(n, F32) for n in shapes],
        compiler_params=params(32),
        cost_estimate=cost(1.5),
        name="last_mlp",
    )(v, token)


RINGS = {"z": "z", "x": "x", "y": ("yl", "yh")}


def ring_place(axis):
    if axis == "y":
        return lax.axis_index("yh") * 2 + lax.axis_index("yl")
    return lax.axis_index(axis)


def ring_pairs(axis, step):
    if axis == "y":
        place = (0, 2, 1, 3)
        return [(place[i], place[(i + step) % 4]) for i in range(4)]
    return [(i, (i + step) % 4) for i in range(4)]


def shift_ring(v, axis, step):
    return lax.ppermute(v, RINGS[axis], ring_pairs(axis, step))


def first_step(parts, axis):
    return shift_ring(parts[1], axis, 1), shift_ring(parts[2], axis, 3)


def second_step(parts, got, axis, token, us, name):
    q1, q3 = add_waiting(parts[3], got[0], parts[4], got[1], token, us, name)
    return shift_ring(q1, axis, 1), shift_ring(q3, axis, 3), q1


def straight(parts, axis):
    return [parts[0]] + [shift_ring(parts[k], axis, k) for k in (1, 3, 2)]


def last_sum(parts):
    total = parts[0].astype(F32)
    for p in parts[1:]:
        total = total + p.astype(F32)
    return total


def swap_yh(v):
    return lax.ppermute(v, "yh", [(0, 1), (1, 0)])


def to_partner(v):
    return lax.ppermute(v, "c", [(0, 1), (1, 0)])


def local(
    image_rows, text_states, text_segment, item_segment, norm_gain, norm_shift, triple_weight, output_weight,
    query_weight, memory_weight, return_weight, up_weight, inner_bias, down_weight, outer_bias, cotangent,
):
    items, r, d = image_rows.shape
    t = items * r
    ff = up_weight.shape[1]
    x = image_rows.reshape(t, d)
    cot = cotangent.reshape(t, d)
    core, pz, px, py = lax.axis_index("c"), lax.axis_index("z"), lax.axis_index("x"), ring_place("y")
    place = jnp.stack([core, pz, px, py]).astype(jnp.int32)
    at_z, at_x = place[1:2], place[2:3]
    yh = lax.axis_index("yh")
    tseg = text_segment.reshape(-1, 1)

    p, h1 = triple_forward(x, norm_gain, norm_shift, triple_weight)
    cot_p = to_partner(cot)
    dg, outer = act_grad(cot, down_weight, p)
    p = lax.all_to_all(p, BLK, 0, 0).reshape(8, items, r, 384)
    memory = encoder_memory(text_states, memory_weight, dg)
    ready = memory[:16, :128]
    h1, arrived_p = gate((h1, p[0, 0, :16, :128]), ready, cot_p[:16, :128])
    hy = swap_yh(h1)
    o = attend(p, arrived_p, ready)
    o = lax.all_to_all(o.reshape(8, t, 128), BLK, 0, 0)
    inner, dgain2, dshift2, y1, qc, pack, gm, mail, out, dy2 = trunk(
        item_segment, place, o, x, norm_gain, norm_shift, memory, tseg, inner_bias.reshape(1, -1),
        outer_bias.reshape(1, -1), dg, cot, output_weight, query_weight, return_weight, up_weight, down_weight, hy,
    )
    mail_p, pack_p = to_partner(mail), to_partner(pack)
    b, dy1, do, dm, thin, hs = middle_back(
        item_segment, dy2, return_weight, qc, memory, tseg, query_weight, y1, norm_gain, output_weight,
        dgain2, dshift2, outer, inner, h1, hy, mail,
    )
    b_p = to_partner(b)
    do = lax.all_to_all(do, BLK, 0, 0).reshape(8, items, r, 128)
    hx1, hx3 = shift_ring(hs, "x", 1), shift_ring(hs, "x", 3)
    deep = list(mlp_grad(place, mail, mail_p, gm, cot, cot_p, b))
    deep[1], deep[2] = gate((deep[1], deep[2]), do, pack_p, b_p)
    deep_r = first_step(deep, "z")
    small = small_grad(place, pack, pack_p, b, b_p, dm, thin, text_states, memory_weight, deep[1])
    small_r = first_step(small, "y")
    (hs,) = gate((hs,), hx1, hx3, small[3])
    hx2 = shift_ring(hs, "x", 2)
    dp = attend_back(p, do, small[3])
    source = [core, px * 2 + yh]
    for k in range(4):
        sx = (px - k) % 4
        source += [sx * 2 + yh, sx * 2 + (1 - yh)]
    dp_flat = dp.reshape(8, t, 384)
    dp_home = lax.all_to_all(dp_flat, BLK, 0, 0)
    mine, theirs = triple_grad(
        jnp.stack(source).astype(jnp.int32), hs, (hx1, hx2, hx3), dp_flat, triple_weight, norm_gain, norm_shift, dp
    )
    deep_q = second_step(deep, deep_r, "z", mine, 0.02, "add_deep")
    small_q = second_step(small, small_r, "y", deep_q[2], 400, "add_small")
    part = add_two(mine, to_partner(theirs), dp_home)
    part_token = part
    part = lax.all_to_all(part.reshape(64, 8, 512), ("z", "yl", "x", "yh"), 0, 0)
    (deep_sum,) = add_deep(deep[0], *deep_r, *deep_q[:2], part_token)
    small_sum = add_ring(at_z, small[0], *small_r, *small_q[:2], deep_sum, True, "sum_small")
    triple_sum, norm_zero = last_triple(part, small_sum[0])
    small_sum = straight(small_sum, "z")
    (deep_sum,) = gate((deep_sum,), norm_zero)
    arrived = lax.all_to_all(deep_sum, ("yl", "x", "yh"), 0, 0)
    input_grad = triple_back(dp_home, triple_weight, x, norm_gain, dy1, deep_sum)
    small_sum = add_parts(at_x, small_sum, input_grad, "parts_small")
    small_sum = straight(small_sum, "x")
    return_grad, query_grad, output_grad, memory_grad, text_grad, gains, shifts, outer_mine, inner_mine = last_small(
        small_sum, norm_zero
    )
    up_sum, down_sum = last_mlp(arrived, norm_zero)
    return (
        out.reshape(items, r, d), input_grad.reshape(items, r, d), text_grad, gains, shifts, triple_sum, output_grad,
        query_grad, memory_grad, return_grad, up_sum, inner_mine.reshape(-1), down_sum, outer_mine.reshape(-1),
    )


def solution(mesh):
    fine = Mesh(mesh.devices.reshape(4, 2, 2, 4, 2), ALL)
    dp = ("z", "yl", "c")
    rows = P(dp, BLK, None)
    placed = (rows, P(), P(), P(dp)) + (P(),) * 11 + (rows,)
    outs = (
        rows, rows, P(None, ALL), P(None, ALL), P(None, ALL), P(ALL, None), P(ALL, None), P(ALL, None), P(ALL, None),
        P(ALL, None), P(ALL, None), P(ALL), P(ALL, None), P(ALL),
    )
    return jax.shard_map(local, mesh=fine, in_specs=placed, out_specs=outs, check_vma=False)
```

```python
import functools

import jax
import jax.numpy as jnp
from jax import lax
from jax.experimental import pallas as pl
from jax.experimental.pallas import tpu as pltpu
from jax.sharding import Mesh, PartitionSpec as P

DH = 64
EPS = 1e-05
SCALE = 0.125
MASKED = -1e30
BF = jnp.bfloat16
F32 = jnp.float32
MIB = 1 << 20

BLK = ("x", "yh")
ALL = ("z", "yl", "c", "x", "yh")


def dot(a, b, ca=1, cb=0):
    return lax.dot_general(a, b, (((ca,), (cb,)), ((), ())), preferred_element_type=F32)


def cost(us):
    return pl.CostEstimate(flops=1, bytes_accessed=int(us * 0.9e6), transcendentals=0)


def params(mib):
    return pltpu.CompilerParams(vmem_limit_bytes=mib * MIB)


SMEM = pl.BlockSpec(memory_space=pltpu.SMEM)
VMEM = pl.BlockSpec(memory_space=pltpu.VMEM)
HBM = pl.BlockSpec(memory_space=pltpu.HBM)
ANY = pl.BlockSpec(memory_space=pl.ANY)


def whole(shape):
    return pl.BlockSpec(shape, lambda *_: (0,) * len(shape))


def fetch(source, target, sems, k):
    rows = source.shape[0] // 4
    copies = [
        pltpu.make_async_copy(source.at[pl.ds(i * rows, rows)], target.at[pl.ds(i * rows, rows)], sems.at[k, i])
        for i in range(4)
    ]
    for copy in copies:
        copy.start()

    def wait():
        for copy in copies:
            copy.wait()

    return wait


def normalise(v):
    mean = jnp.mean(v, axis=-1, keepdims=True)
    centred = v - mean
    var = jnp.mean(centred * centred, axis=-1, keepdims=True)
    rstd = lax.rsqrt(var + EPS)
    return centred * rstd, rstd


def norm_back(dy, xhat, rstd, gain):
    dx = dy * gain
    m1 = jnp.mean(dx, axis=-1, keepdims=True)
    m2 = jnp.mean(dx * xhat, axis=-1, keepdims=True)
    back = rstd * (dx - m1 - xhat * m2)
    dgain = jnp.sum(dy * xhat, axis=0, keepdims=True)
    dshift = jnp.sum(dy, axis=0, keepdims=True)
    return back, dgain, dshift


def triple_body(x_ref, g_ref, s_ref, wq_ref, wk_ref, wv_ref, p_ref, h_ref):
    @pl.when(pl.program_id(0) == 0)
    def _():
        xhat, _ = normalise(x_ref[...].astype(F32))
        h_ref[...] = (xhat * g_ref[0:1] + s_ref[0:1]).astype(BF)

    h = h_ref[...]
    for i, w in enumerate((wq_ref, wk_ref, wv_ref)):
        r = dot(h, w[...]).astype(BF)
        for k in range(p_ref.shape[0]):
            p_ref[k, :, i * 128 : (i + 1) * 128] = r[:, k * 128 : (k + 1) * 128]


def triple_forward(x, gain, shift, w):
    t, d = x.shape
    tile = 512
    n = d // tile
    return pl.pallas_call(
        triple_body,
        grid=(n,),
        in_specs=[
            whole((t, d)),
            whole((3, d)),
            whole((3, d)),
            pl.BlockSpec((d, tile), lambda j: (0, j)),
            pl.BlockSpec((d, tile), lambda j: (0, n + j)),
            pl.BlockSpec((d, tile), lambda j: (0, 2 * n + j)),
        ],
        out_specs=[pl.BlockSpec((tile // 128, t, 384), lambda j: (j, 0, 0)), whole((t, d))],
        out_shape=[jax.ShapeDtypeStruct((d // 128, t, 384), BF), jax.ShapeDtypeStruct((t, d), BF)],
        compiler_params=params(60),
        cost_estimate=cost(6),
        name="triple_forward",
    )(x, gain, shift, w, w, w)


def head_lanes(shape, h):
    return (lax.broadcasted_iota(jnp.int32, shape, 1) // DH) == h


def masked_head(v, h):
    return jnp.where(head_lanes(v.shape, h), v, 0.0).astype(BF)


def expon_t(k, qh, qb):
    kv = 256 * (qb + 1)
    st = dot(k[:kv], qh, 1, 1)
    kpos = lax.broadcasted_iota(jnp.int32, (256, 256), 0)
    qpos = lax.broadcasted_iota(jnp.int32, (256, 256), 1)
    last = jnp.where(kpos <= qpos, st[kv - 256 :], MASKED)
    st = jnp.concatenate([st[: kv - 256], last], axis=0) if qb else last
    top = jnp.max(st, axis=0, keepdims=True)
    e = jnp.exp(st - top)
    return e, 1.0 / jnp.sum(e, axis=0, keepdims=True)


def attend_body(p_ref, _, o_ref):
    rows = p_ref.shape[0] * p_ref.shape[2]
    k = p_ref[:, 0, :, 128:256].reshape(rows, 128)
    v = p_ref[:, 0, :, 256:384].reshape(rows, 128)
    vt = v.T
    for qb in range(rows // 256):
        q = p_ref[2 * qb : 2 * qb + 2, 0, :, 0:128].reshape(256, 128).astype(F32) * SCALE
        kv = 256 * (qb + 1)
        parts = []
        for h in range(2):
            e, share = expon_t(k, masked_head(q, h), qb)
            parts.append(dot(vt[h * DH : (h + 1) * DH, :kv], e.astype(BF)) * share)
        o = jnp.concatenate(parts, axis=0).T.astype(BF)
        o_ref[2 * qb : 2 * qb + 2, 0] = o.reshape(2, 128, 128)


def attend(p, token):
    b, items, r, _ = p.shape
    return pl.pallas_call(
        attend_body,
        grid=(items,),
        in_specs=[
            pl.BlockSpec((b, 1, r, 384), lambda i: (0, i, 0, 0)),
            ANY,
        ],
        out_specs=pl.BlockSpec((b, 1, r, 128), lambda i: (0, i, 0, 0)),
        out_shape=jax.ShapeDtypeStruct((b, items, r, 128), BF),
        compiler_params=params(32),
        cost_estimate=cost(10),
        name="attend",
    )(p, token)


def attend_back_body(p_ref, do_ref, _, dp_ref, dk_scr, dv_scr):
    rows = p_ref.shape[0] * p_ref.shape[2]
    blocks = p_ref.shape[0]
    k = p_ref[:, 0, :, 128:256].reshape(rows, 128)
    v = p_ref[:, 0, :, 256:384].reshape(rows, 128)
    kt = k.T
    last = rows // 256 - 1
    for qb in range(last, -1, -1):
        q = p_ref[2 * qb : 2 * qb + 2, 0, :, 0:128].reshape(256, 128).astype(F32) * SCALE
        do = do_ref[2 * qb : 2 * qb + 2, 0].reshape(256, 128).astype(F32)
        kv = 256 * (qb + 1)
        parts, qs, dos, probs, grads = [], [], [], [], []
        for h in range(2):
            qh = masked_head(q, h)
            doh = masked_head(do, h)
            e, share = expon_t(k, qh, qb)
            a = e * share
            da = dot(v[:kv], doh, 1, 1)
            dots = jnp.sum(a * da, axis=0, keepdims=True)
            ds = (a * (da - dots)).astype(BF)
            parts.append(dot(kt[h * DH : (h + 1) * DH, :kv], ds))
            qs.append(qh)
            dos.append(doh)
            probs.append(a.astype(BF))
            grads.append(ds)
        dv = dot(jnp.concatenate(probs, axis=1), jnp.concatenate(dos, axis=0))
        dk = dot(jnp.concatenate(grads, axis=1), jnp.concatenate(qs, axis=0))
        if qb == last:
            dv_scr[...] = dv
            dk_scr[...] = dk
        else:
            dv_scr[:kv] += dv
            dk_scr[:kv] += dk
        dq = (jnp.concatenate(parts, axis=0) * SCALE).T.astype(BF)
        dp_ref[2 * qb : 2 * qb + 2, 0, :, 0:128] = dq.reshape(2, 128, 128)
    dp_ref[:, 0, :, 128:256] = dk_scr[...].astype(BF).reshape(blocks, -1, 128)
    dp_ref[:, 0, :, 256:384] = dv_scr[...].astype(BF).reshape(blocks, -1, 128)


def attend_back(p, do, token):
    b, items, r, _ = p.shape
    return pl.pallas_call(
        attend_back_body,
        grid=(items,),
        in_specs=[
            pl.BlockSpec((b, 1, r, 384), lambda i: (0, i, 0, 0)),
            pl.BlockSpec((b, 1, r, 128), lambda i: (0, i, 0, 0)),
            ANY,
        ],
        out_specs=pl.BlockSpec((b, 1, r, 384), lambda i: (0, i, 0, 0)),
        out_shape=jax.ShapeDtypeStruct((b, items, r, 384), BF),
        scratch_shapes=[pltpu.VMEM((b * r, 128), F32), pltpu.VMEM((b * r, 128), F32)],
        compiler_params=params(40),
        cost_estimate=cost(0.02),
        name="attend_back",
    )(p, do, token)


def gate_body(*_):
    pass


def gate(values, *tokens):
    n = len(values)
    return pl.pallas_call(
        gate_body,
        in_specs=[ANY] * (n + len(tokens)),
        out_specs=[ANY] * n,
        out_shape=[jax.ShapeDtypeStruct(v.shape, v.dtype) for v in values],
        input_output_aliases={i: i for i in range(n)},
        cost_estimate=cost(0.5),
        name="gate",
    )(*values, *tokens)


def stack_heads(v, items):
    r = v.shape[0] // items
    parts = []
    for i in range(items):
        for h in range(2):
            parts.append(masked_head(v[i * r : (i + 1) * r], h))
    return jnp.concatenate(parts, axis=0)


def unstack_heads(v, items):
    r = v.shape[0] // (2 * items)
    parts = []
    for i in range(items):
        first = v[(2 * i) * r : (2 * i + 1) * r]
        second = v[(2 * i + 1) * r : (2 * i + 2) * r]
        parts.append(jnp.where(head_lanes(first.shape, 0), first, second))
    return jnp.concatenate(parts, axis=0)


def cross_probs_t(mk, q4, allowed):
    st = jnp.where(allowed, dot(mk, q4, 1, 1), MASKED)
    top = jnp.max(st, axis=0, keepdims=True)
    e = jnp.exp(st - top)
    return e * (1.0 / jnp.sum(e, axis=0, keepdims=True))


def allowed_mask(tseg_ref, iseg_ref, items, r):
    seg = tseg_ref[...]
    return jnp.concatenate(
        [jnp.broadcast_to(seg == iseg_ref[i], (seg.shape[0], 2 * r)) for i in range(items)], axis=1
    )


def act_grad_body(r_ref, down_ref, _, dg_ref, outer_ref):
    cot = r_ref[...]
    dg_ref[...] = dot(cot, down_ref[...], 1, 1).astype(BF)

    @pl.when(pl.program_id(0) == 0)
    def _():
        outer_ref[...] = jnp.sum(cot.astype(F32), axis=0, keepdims=True)


def act_grad(cot, down, token):
    t, d = cot.shape
    ff = down.shape[0]
    tile = 2048
    return pl.pallas_call(
        act_grad_body,
        grid=(ff // tile,),
        in_specs=[whole((t, d)), pl.BlockSpec((tile, d), lambda i: (i, 0)), ANY],
        out_specs=[pl.BlockSpec((t, tile), lambda i: (0, i)), whole((1, d))],
        out_shape=[jax.ShapeDtypeStruct((t, ff), BF), jax.ShapeDtypeStruct((1, d), F32)],
        compiler_params=params(60),
        cost_estimate=cost(400),
        name="act_grad",
    )(cot, down, token)


def trunk_body(
    iseg_ref, place_ref, x_ref, g_ref, s_ref, m_ref, tseg_ref, ib_ref, ob_ref,
    o_ref, dg_hbm, r_hbm, wo_hbm, wq_hbm, wr_hbm, up_hbm, down_hbm, _,
    inner_ref, dgain_ref, dshift_ref, y1_hbm, qc_hbm, pack_hbm, gm_hbm, mail_hbm, out_hbm, dy2_hbm,
    wo_ref, wq_ref, wr_ref, up_ref, down_ref, dg_ref, r_ref,
    y1_ref, qc_ref, pack_ref, gm_ref, mail_ref, out_ref, dy2_ref, y_scr, dh_scr, xhat_scr, in_sems, out_sems,
):
    items = iseg_ref.shape[0]
    t, d = x_ref.shape
    r = t // items
    tile = 2048
    tiles = up_ref.shape[1] // tile
    loads = [(wo_hbm, wo_ref), (wq_hbm, wq_ref), (wr_hbm, wr_ref)]
    for j in range(tiles):
        at = pl.ds(j * tile, tile)
        loads += [(up_hbm.at[:, at], up_ref.at[:, at]), (dg_hbm.at[:, at], dg_ref.at[:, at])]
        loads += [(down_hbm.at[at], down_ref.at[at])]
    loads += [(r_hbm, r_ref)]
    waits = [fetch(source, target, in_sems, k) for k, (source, target) in enumerate(loads)]
    stores = []

    def store(source, target):
        stores.append(pltpu.make_async_copy(source, target, out_sems.at[len(stores)]))
        stores[-1].start()

    o = jnp.concatenate([o_ref[j] for j in range(o_ref.shape[0])], axis=1)
    pack_ref[:, 0:d] = o
    waits[0]()
    y1 = x_ref[...].astype(F32) + dot(o, wo_ref[...])
    y1_ref[...] = y1
    store(y1_ref, y1_hbm)
    xhat, _ = normalise(y1)
    h2 = (xhat * g_ref[1:2] + s_ref[1:2]).astype(BF)
    pack_ref[:, d : 2 * d] = h2
    waits[1]()
    qc_ref[...] = dot(h2, wq_ref[...]).astype(BF)
    store(qc_ref, qc_hbm)
    allowed = allowed_mask(tseg_ref, iseg_ref, items, r)
    for p in range(d // 128):
        at = slice(p * 128, (p + 1) * 128)
        q4 = stack_heads(qc_ref[:, at].astype(F32) * SCALE, items)
        a = cross_probs_t(m_ref[:, at], q4, allowed).astype(BF)
        o4 = dot(a, m_ref[:, d + p * 128 : d + (p + 1) * 128], 0, 0)
        pack_ref[:, 2 * d + p * 128 : 2 * d + (p + 1) * 128] = unstack_heads(o4, items).astype(BF)
    waits[2]()
    y2 = y1 + dot(pack_ref[:, 2 * d : 3 * d], wr_ref[...])
    xhat, rstd = normalise(y2)
    xhat_scr[...] = xhat
    h3 = (xhat * g_ref[2:3] + s_ref[2:3]).astype(BF)
    store(pack_ref, pack_hbm)
    ff = up_ref.shape[1]
    mail_ref[:, ff + ff // 2 :] = h3
    store(mail_ref.at[:, pl.ds(ff + ff // 2, d)], mail_hbm.at[:, pl.ds(ff + ff // 2, d)])
    y_scr[...] = y2 + ob_ref[...]

    c0 = 0.7978845608028654
    c1 = 0.044715
    first = place_ref[0] == 0
    for j in range(tiles):
        at = slice(j * tile, (j + 1) * tile)
        waits[3 + 3 * j]()
        waits[4 + 3 * j]()
        u = dot(h3, up_ref[:, at]) + ib_ref[:, at]
        uu = u * u
        th = jnp.tanh(u * (c0 + (c0 * c1) * uu))
        half = 0.5 + 0.5 * th
        g = (u * half).astype(BF)
        slope = half + (0.5 * u) * (1.0 - th * th) * (c0 + (3.0 * c0 * c1) * uu)
        du = (slope * dg_ref[:, at].astype(F32)).astype(BF)
        mail_ref[:, at] = du
        store(mail_ref.at[:, pl.ds(j * tile, tile)], mail_hbm.at[:, pl.ds(j * tile, tile)])
        inner = jnp.sum(du.astype(F32), axis=0, keepdims=True)
        for k in range(tile // 128):
            inner_ref[16 * j + k : 16 * j + k + 1] = inner[:, 128 * k : 128 * k + 128]
        for k in range(tile // 512):
            even, odd = g[:, 512 * k : 512 * k + 256], g[:, 512 * k + 256 : 512 * k + 512]
            half_at = j * tile // 2 + 256 * k
            gm_ref[:, half_at : half_at + 256] = jnp.where(first, even, odd)
            mail_ref[:, ff + half_at : ff + half_at + 256] = jnp.where(first, odd, even)
        waits[5 + 3 * j]()
        y_scr[...] += dot(g, down_ref[at])
        back = dot(du, up_ref[:, at], 1, 1)
        dh_scr[...] = dh_scr[...] + back if j else back
    store(gm_ref, gm_hbm)
    store(mail_ref.at[:, pl.ds(ff, ff // 2)], mail_hbm.at[:, pl.ds(ff, ff // 2)])
    out_ref[...] = y_scr[...].astype(BF)
    store(out_ref, out_hbm)
    back, dgain, dshift = norm_back(dh_scr[...], xhat_scr[...], rstd, g_ref[2:3])
    waits[-1]()
    dy2_ref[...] = r_ref[...].astype(F32) + back
    store(dy2_ref, dy2_hbm)
    dgain_ref[...] = dgain
    dshift_ref[...] = dshift
    for copy in stores:
        copy.wait()


def trunk(iseg, place, o, x, gain, shift, m, tseg, ib, ob, dg, cot, wo, wq, wr, up, down, token):
    t, d = x.shape
    ff = up.shape[1]
    args = (iseg, place, x, gain, shift, m, tseg, ib, ob, o, dg, cot, wo, wq, wr, up, down, token)
    small = [((ff // 128, 128), F32), ((1, d), F32), ((1, d), F32)]
    large = [((t, d), F32), ((t, d), BF), ((t, 3 * d), BF), ((t, ff // 2), BF), ((t, ff + ff // 2 + d), BF),
             ((t, d), BF), ((t, d), F32)]
    weights = [(v.shape, BF) for v in (wo, wq, wr, up, down, dg, cot)]
    return pl.pallas_call(
        trunk_body,
        in_specs=[SMEM, SMEM] + [VMEM] * 8 + [HBM] * 7 + [ANY],
        out_specs=[VMEM] * 3 + [ANY] * 7,
        out_shape=[jax.ShapeDtypeStruct(*v) for v in small + large],
        scratch_shapes=[pltpu.VMEM(*v) for v in weights + large]
        + [pltpu.VMEM((t, d), F32)] * 3
        + [pltpu.SemaphoreType.DMA((17, 4)), pltpu.SemaphoreType.DMA((12,))],
        compiler_params=params(54),
        cost_estimate=cost(0.02),
        name="trunk",
    )(*args)


def middle_back_body(
    iseg_ref, tseg_ref, g_ref, dgain_ref, dshift_ref, outer_ref, inner_ref,
    dy2_hbm, wr_hbm, m_hbm, qc_hbm, wq_hbm, y1_hbm, wo_hbm, h1_hbm, hy_hbm, _,
    thin_ref, pack_hbm, dy1_hbm, do_hbm, dm_hbm, hs_hbm,
    dy2_ref, wr_ref, m_ref, qc_ref, wq_ref, y1_ref, wo_ref, h1_ref, hy_ref,
    pack_ref, dy1_ref, do_ref, dm_ref, doc_scr, in_sems, out_sems,
):
    loads = ((dy2_hbm, dy2_ref), (wr_hbm, wr_ref), (m_hbm, m_ref), (qc_hbm, qc_ref), (wq_hbm, wq_ref),
             (y1_hbm, y1_ref), (wo_hbm, wo_ref), (h1_hbm, h1_ref), (hy_hbm, hy_ref))
    wait_dy2, wait_r, wait_m, wait_qc, wait_q, wait_y1, wait_o, wait_h1, wait_hy = (
        fetch(source, target, in_sems, k) for k, (source, target) in enumerate(loads)
    )
    stores = []

    def store(source, target):
        stores.append(pltpu.make_async_copy(source, target, out_sems.at[len(stores)]))
        stores[-1].start()

    items = iseg_ref.shape[0]
    t, d = dy2_ref.shape
    r = t // items
    texts = m_ref.shape[0]
    wait_dy2()
    b2 = dy2_ref[...].astype(BF)
    pack_ref[:t, 0:d] = b2
    wait_r()
    doc_scr[...] = dot(b2, wr_ref[...], 1, 1).astype(BF)
    allowed = allowed_mask(tseg_ref, iseg_ref, items, r)
    wait_m()
    wait_qc()
    for p in range(d // 128):
        at = slice(p * 128, (p + 1) * 128)
        av = slice(d + p * 128, d + (p + 1) * 128)
        mk = m_ref[:, at]
        q4 = stack_heads(qc_ref[:, at].astype(F32) * SCALE, items)
        do4 = stack_heads(doc_scr[:, at].astype(F32), items)
        a = cross_probs_t(mk, q4, allowed)
        da = dot(m_ref[:, av], do4, 1, 1)
        dots = jnp.sum(a * da, axis=0, keepdims=True)
        ds = (a * (da - dots)).astype(BF)
        dmk, dmv = dot(ds, q4), dot(a.astype(BF), do4)
        dm_ref[:, at] = dmk
        dm_ref[:, av] = dmv
        pack_ref[t:, at] = dmk.astype(BF)
        pack_ref[t:, av] = dmv.astype(BF)
        pack_ref[:t, d + p * 128 : d + (p + 1) * 128] = (unstack_heads(dot(ds, mk, 0, 0), items) * SCALE).astype(BF)
    store(dm_ref, dm_hbm)
    store(pack_ref.at[pl.ds(0, t), pl.ds(0, 2 * d)], pack_hbm.at[pl.ds(0, t), pl.ds(0, 2 * d)])
    wait_h1()
    wait_hy()
    store(h1_ref, hs_hbm.at[0])
    store(hy_ref, hs_hbm.at[1])
    wait_y1()
    xhat, rstd = normalise(y1_ref[...])
    wait_q()
    dh2 = dot(pack_ref[:t, d : 2 * d], wq_ref[...], 1, 1)
    back, dgain, dshift = norm_back(dh2, xhat, rstd, g_ref[1:2])
    dy1 = dy2_ref[...] + back
    dy1_ref[...] = dy1
    store(dy1_ref, dy1_hbm)
    b1 = dy1.astype(BF)
    pack_ref[:t, 2 * d : 3 * d] = b1
    store(pack_ref.at[pl.ds(0, t), pl.ds(2 * d, d)], pack_hbm.at[pl.ds(0, t), pl.ds(2 * d, d)])
    thin_ref[...] = jnp.zeros_like(thin_ref)
    for k, v in enumerate((dgain, dshift, dgain_ref[...], dshift_ref[...], outer_ref[...])):
        thin_ref[k : k + 1] = v
    n = inner_ref.shape[0]
    thin_ref[16 : 16 + n, 0:128] = inner_ref[...]
    pack_ref[t:, 2 * d : 3 * d] = jnp.zeros((texts, d), BF)
    pack_ref[t : t + 16 + n, 2 * d : 3 * d] = thin_ref[...].astype(BF)
    store(pack_ref.at[pl.ds(t, texts)], pack_hbm.at[pl.ds(t, texts)])
    wait_o()
    do = dot(b1, wo_ref[...], 1, 1).astype(BF)
    for j in range(do_ref.shape[0]):
        do_ref[j] = do[:, j * 128 : (j + 1) * 128]
    store(do_ref, do_hbm)
    for copy in stores:
        copy.wait()


def middle_back(iseg, dy2, wr, qc, m, tseg, wq, y1, gain, wo, dgain, dshift, outer, inner, h1, hy, token):
    t, d = dy2.shape
    texts = m.shape[0]
    large = (dy2, wr, m, qc, wq, y1, wo, h1, hy)
    args = (iseg, tseg, gain, dgain, dshift, outer, inner) + large + (token,)
    thin = ((16 + inner.shape[0], d), F32)
    outs = [((t + texts, 3 * d), BF), ((t, d), F32), ((d // 128, t, 128), BF), ((texts, 2 * d), F32)]
    thin, pack, dy1, do, dm, hs = pl.pallas_call(
        middle_back_body,
        in_specs=[SMEM] + [VMEM] * 6 + [HBM] * 7 + [ANY] * 3,
        out_specs=[VMEM] + [ANY] * 5,
        out_shape=[jax.ShapeDtypeStruct(*v) for v in [thin] + outs + [((2, t, d), BF)]],
        scratch_shapes=[pltpu.VMEM(v.shape, v.dtype) for v in large]
        + [pltpu.VMEM(*v) for v in outs]
        + [pltpu.VMEM((t, d), BF), pltpu.SemaphoreType.DMA((9, 4)), pltpu.SemaphoreType.DMA((8,))],
        compiler_params=params(60),
        cost_estimate=cost(400),
        name="middle_back",
    )(*args)
    return pack, dy1, do, dm, thin, hs


def triple_back_body(dp_ref, wq_ref, wk_ref, wv_ref, x_ref, g_ref, dy1_ref, _, out_ref, acc):
    step = pl.program_id(0)
    n = pl.num_programs(0)

    @pl.when(step == 0)
    def _():
        acc[...] = jnp.zeros_like(acc)

    total = acc[...]
    for i, w in enumerate((wq_ref, wk_ref, wv_ref)):
        at = slice(i * 128, (i + 1) * 128)
        total += dot(jnp.concatenate([dp_ref[k, :, at] for k in range(dp_ref.shape[0])], axis=1), w[...], 1, 1)
    acc[...] = total

    @pl.when(step == n - 1)
    def _():
        xhat, rstd = normalise(x_ref[...].astype(F32))
        back, _, _ = norm_back(acc[...], xhat, rstd, g_ref[0:1])
        out_ref[...] = dy1_ref[...] + back


def triple_back(dp, w, x, gain, dy1, token):
    t, d = x.shape
    tile = 512
    n = d // tile
    return pl.pallas_call(
        triple_back_body,
        grid=(n,),
        in_specs=[
            pl.BlockSpec((tile // 128, t, 384), lambda j: (j, 0, 0)),
            pl.BlockSpec((d, tile), lambda j: (0, j)),
            pl.BlockSpec((d, tile), lambda j: (0, n + j)),
            pl.BlockSpec((d, tile), lambda j: (0, 2 * n + j)),
            whole((t, d)),
            whole((3, d)),
            whole((t, d)),
            ANY,
        ],
        out_specs=whole((t, d)),
        out_shape=jax.ShapeDtypeStruct((t, d), F32),
        scratch_shapes=[pltpu.VMEM((t, d), F32)],
        compiler_params=params(60),
        cost_estimate=cost(4.5),
        name="triple_back",
    )(dp, w, w, w, x, gain, dy1, token)


def selector(place_ref, first, rows=512, d=1024):
    n = lax.broadcasted_iota(jnp.int32, (rows, d), 0)
    at = lax.broadcasted_iota(jnp.int32, (rows, d), 1)
    third, second, ahead = (n // 8) % 4, (n // 32) % 4, n // 128
    if first == "y":
        py, pz, px = (place_ref[3] + ahead) % 4, second, third
        yl, yh = py % 2, py // 2
    else:
        pz, yl, px, yh = (place_ref[1] + ahead) % 4, (n // 64) % 2, (n // 16) % 4, (n // 8) % 2
    source = ((((pz * 2 + yl) * 2 + place_ref[0]) * 4 + px) * 2 + yh) * 8 + n % 8
    return (at == source).astype(F32).astype(BF)


def split_rows(value, c0_ref, s1_ref, s3_ref, k1_ref, k3_ref):
    n = value.shape[0] // 8
    c0_ref[...] = value[: 2 * n]
    k1_ref[...] = value[2 * n : 3 * n]
    s1_ref[:n] = value[3 * n : 4 * n]
    s1_ref[n:] = value[4 * n : 5 * n]
    s3_ref[n:] = value[5 * n : 6 * n]
    s3_ref[:n] = value[6 * n : 7 * n]
    k3_ref[...] = value[7 * n :]


def pieces(rows, cols):
    n = rows // 8
    return [jax.ShapeDtypeStruct((k, cols), BF) for k in (2 * n, 2 * n, 2 * n, n, n)]


def mlp_grad_body(
    place_ref, mail_hbm, mail_p_hbm, g_hbm, r_hbm, r_p_hbm, _,
    c0_hbm, s1_hbm, s3_hbm, k1_hbm, k3_hbm, c0, s1, s3, k1, k3, tokens, u_ref, g_ref, r_ref, sems, in_sems,
):
    t, d = r_hbm.shape
    ff = u_ref.shape[1]
    of_u, of_g, of_h = pl.ds(0, ff), pl.ds(ff, ff // 2), pl.ds(ff + ff // 2, d)
    wait_g, wait_g_p, wait_r, wait_r_p, wait_h, wait_h_p, wait_u, wait_u_p = (
        fetch(a, b, in_sems, k)
        for k, (a, b) in enumerate((
            (g_hbm, g_ref.at[:t]), (mail_p_hbm.at[:, of_g], g_ref.at[t:]), (r_hbm, r_ref.at[:t]), (r_p_hbm, r_ref.at[t:]),
            (mail_hbm.at[:, of_h], tokens.at[:t]), (mail_p_hbm.at[:, of_h], tokens.at[t:]),
            (mail_hbm.at[:, of_u], u_ref.at[:t]), (mail_p_hbm.at[:, of_u], u_ref.at[t:]),
        ))
    )
    copies = []

    def store(source, target, owners, rows):
        copies.append(
            pltpu.make_async_copy(source.at[owners, rows], target.at[owners, rows], sems.at[len(copies)])
        )
        copies[-1].start()

    half = {(0, 0): (c0, c0_hbm, 0), (0, 1): (c0, c0_hbm, 8), (1, 0): (k1, k1_hbm, 0), (1, 1): (s1, s1_hbm, 0),
            (2, 0): (s1, s1_hbm, 8), (2, 1): (s3, s3_hbm, 8), (3, 0): (s3, s3_hbm, 0), (3, 1): (k3, k3_hbm, 0)}
    sel = selector(place_ref, "z")
    for wait in (wait_g, wait_g_p, wait_r, wait_r_p):
        wait()
    right = r_ref[...]
    for (k, yl), (ref, hbm, first) in half.items():
        column = pl.multiple_of((lax.rem(place_ref[1] + k, 4) * 2 + yl) * 256, 256)
        both = g_ref[:, pl.ds(column, 256)].T
        ref[first : first + 8, 32:64] = dot(both, right).astype(BF).reshape(8, 32, d)
        store(ref, hbm, pl.ds(first, 8), pl.ds(32, 32))
    wait_h()
    wait_h_p()
    left = dot(sel, tokens[...], 1, 1).astype(BF)
    wait_u()
    wait_u_p()
    for pair in range(2):
        value = []
        for block in (2 * pair, 2 * pair + 1):
            value.append(dot(left, u_ref[:, block * d : (block + 1) * d]).reshape(64, 8, d))
        value = jnp.concatenate(value, axis=1).astype(BF)
        for (k, yl), (ref, hbm, first) in half.items():
            ref[first : first + 8, 16 * pair : 16 * pair + 16] = value[16 * k + 8 * yl : 16 * k + 8 * yl + 8]
        for ref, hbm in ((c0, c0_hbm), (s1, s1_hbm), (s3, s3_hbm), (k1, k1_hbm), (k3, k3_hbm)):
            store(ref, hbm, pl.ds(0, ref.shape[0]), pl.ds(16 * pair, 16))
    for copy in copies:
        copy.wait()


def mlp_grad(place, mail, mail_p, gm, rm, rp, token):
    t, d = rm.shape
    ff = 2 * gm.shape[1]
    shapes = [(n, 64, d) for n in (16, 16, 16, 8, 8)]
    args = (mail, mail_p, gm, rm, rp)
    return pl.pallas_call(
        mlp_grad_body,
        in_specs=[SMEM] + [ANY] * 6,
        out_specs=[ANY] * 5,
        out_shape=[jax.ShapeDtypeStruct(v, BF) for v in shapes],
        scratch_shapes=[pltpu.VMEM(v, BF) for v in shapes]
        + [pltpu.VMEM((2 * t, n), BF) for n in (d, ff, ff // 2, d)]
        + [pltpu.SemaphoreType.DMA((18,)), pltpu.SemaphoreType.DMA((8, 4))],
        compiler_params=params(60),
        cost_estimate=cost(400),
        name="mlp_grad",
    )(place, *args, token)


def small_grad_body(
    place_ref, pack_hbm, pack_p_hbm, b_hbm, b_p_hbm, dm_ref, thin_ref, text_ref, wm_hbm, _,
    c0_hbm, s1_hbm, s3_hbm, k1_hbm, k3_hbm, c0, s1, s3, k1, k3, left_scr, right_scr, extra, wm_ref, in_sems, sems,
):
    t, d = left_scr.shape[1] // 2, left_scr.shape[2]
    rows = d // 2
    outs = ((c0, c0_hbm), (s1, s1_hbm), (s3, s3_hbm), (k1, k1_hbm), (k3, k3_hbm))
    waits = []
    for i, column in enumerate((2, 1, 0)):
        at, of = pl.ds(column * d, d), pl.ds(i * d, d)
        waits.append([
            fetch(source, target, in_sems, 4 * i + k)
            for k, (source, target) in enumerate((
                (pack_hbm.at[:, at], left_scr.at[i, :t]), (pack_p_hbm.at[:, at], left_scr.at[i, t:]),
                (b_hbm.at[:t, of], right_scr.at[i, :t]), (b_p_hbm.at[:t, of], right_scr.at[i, t:]),
            ))
        ])
    wait_extra = fetch(b_p_hbm.at[t:], extra, in_sems, 12)
    wait_wm = fetch(wm_hbm, wm_ref, in_sems, 13)
    copies = []

    def put(value, first):
        columns = pl.ds(first, value.shape[1])
        split_rows(value, *(o.at[:, columns] for o, _ in outs))

    def send(k, first, columns):
        at = pl.ds(first, columns)
        for j, (o, hbm) in enumerate(outs):
            copies.append(pltpu.make_async_copy(o.at[:, at], hbm.at[:, at], sems.at[k, j]))
            copies[-1].start()

    sel = selector(place_ref, "y")
    for i in range(3):
        for wait in waits[i]:
            wait()
        left = dot(sel, left_scr[i], 1, 1).astype(BF)
        put(dot(left, right_scr[i]).astype(BF), i * d)
        send(i, i * d, d)
    wait_extra()
    dm = (dm_ref[...] + extra[:, 0 : 2 * d].astype(F32)).astype(BF)
    left = dot(sel, text_ref[...], 1, 1).astype(BF)
    put(dot(left, dm).astype(BF), 3 * d)
    send(3, 3 * d, 2 * d)
    thin = (thin_ref[...] + extra[0:48, 2 * d : 3 * d].astype(F32)).astype(BF)
    values = dot(sel, thin[:16], 1, 1)
    lane = lax.broadcasted_iota(jnp.int32, (rows, 128), 1)
    feature = lax.broadcasted_iota(jnp.int32, (rows, d), 1).astype(F32) * sel.astype(F32)
    source = jnp.sum(feature, axis=1, keepdims=True).astype(jnp.int32)
    line = (lax.broadcasted_iota(jnp.int32, (rows, 32), 1) == source // 32).astype(F32).astype(BF)
    inner = dot(line, thin[16:48, 0:128])
    inner = jnp.where(lane // 4 == source % 32, inner, 0.0).astype(BF)
    fold_from = lax.broadcasted_iota(jnp.int32, (128, 128), 0)
    fold_to = lax.broadcasted_iota(jnp.int32, (128, 128), 1)
    fold = (fold_to == 16 + fold_from % 4).astype(F32).astype(BF)
    values = jnp.concatenate([values, jnp.zeros((rows, 112), F32)], axis=1) + dot(inner, fold)
    put(values.astype(BF), 5 * d)
    wait_wm()
    texts = dot(wm_ref[...], dm, 1, 1).astype(BF)
    put(dot(sel, texts).astype(BF), 5 * d + 128)
    send(4, 5 * d, 256)
    for copy in copies:
        copy.wait()


def small_grad(place, pack, pack_p, b, b_p, dm, thin, text, wm, token):
    t = pack.shape[0]
    d = pack.shape[1] // 3
    outs = pieces(d // 2, 5 * d + 256)
    args = (place, pack, pack_p, b, b_p, dm, thin, text, wm, token)
    return pl.pallas_call(
        small_grad_body,
        in_specs=[SMEM] + [ANY] * 4 + [VMEM] * 3 + [ANY] * 2,
        out_specs=[ANY] * 5,
        out_shape=outs,
        scratch_shapes=[pltpu.VMEM(o.shape, BF) for o in outs]
        + [pltpu.VMEM((3, 2 * t, d), BF), pltpu.VMEM((3, 2 * t, d), BF)]
        + [pltpu.VMEM((b.shape[0] - t, 3 * d), BF), pltpu.VMEM(wm.shape, BF)]
        + [pltpu.SemaphoreType.DMA((14, 4)), pltpu.SemaphoreType.DMA((5, 5))],
        compiler_params=params(60),
        cost_estimate=cost(400),
        name="small_grad",
    )(*args)


def triple_grad_body(
    src_ref, hs_ref, hx1_ref, hx2_ref, hx3_ref, dp_ref, wq_ref, wk_ref, wv_ref, g_ref, s_ref, _, mine_ref, theirs_ref
):
    d = hs_ref.shape[2]
    cols = dp_ref.shape[2]
    total = jnp.zeros((cols, d), F32)
    sums = jnp.zeros((1, cols), F32)
    for k, ref in enumerate((hs_ref, hx1_ref, hx2_ref, hx3_ref)):
        for other in range(2):
            dp = dp_ref[src_ref[2 + 2 * k + other]]
            total += dot(dp.T, ref[other])
            sums += jnp.sum(dp.astype(F32), axis=0, keepdims=True)
    total = total.T
    w = jnp.concatenate([wq_ref[...], wk_ref[...], wv_ref[...]], axis=1).astype(F32)
    norm = jnp.concatenate([g_ref[0:1], s_ref[0:1], jnp.zeros((6, d), F32)], axis=0).T
    dshift = jnp.sum(w * sums, axis=1, keepdims=True)
    dgain = (jnp.sum(w * total, axis=1, keepdims=True) - norm[:, 1:2] * dshift) / norm[:, 0:1]
    lane = lax.broadcasted_iota(jnp.int32, (d, 128), 1)
    extra = jnp.where(lane == 0, dgain, 0.0) + jnp.where(lane == 1, dshift, 0.0)
    value = jnp.concatenate([total, extra], axis=1).astype(BF).reshape(8, 2, 64, 512)
    core = src_ref[0]

    @pl.when(core == 0)
    def _():
        mine_ref[...] = value[:, 0]
        theirs_ref[...] = value[:, 1]

    @pl.when(core == 1)
    def _():
        mine_ref[...] = value[:, 1]
        theirs_ref[...] = value[:, 0]


def triple_grad(src, hs, hx, dp, w, gain, shift, token):
    _, t, d = hs.shape
    cols = dp.shape[2]
    part = jax.ShapeDtypeStruct((8, 64, 512), BF)

    def columns(k):
        return pl.BlockSpec((d, 128), lambda i, src_ref: (0, k * (d // 128) + src_ref[1]))

    return pl.pallas_call(
        triple_grad_body,
        grid_spec=pltpu.PrefetchScalarGridSpec(
            num_scalar_prefetch=1,
            grid=(1,),
            in_specs=[whole(hs.shape)] * 4
            + [whole(dp.shape), columns(0), columns(1), columns(2), whole((3, d)), whole((3, d)), ANY],
            out_specs=[whole(part.shape)] * 2,
        ),
        out_shape=[part, part],
        compiler_params=params(60),
        cost_estimate=cost(0.02),
        name="triple_grad",
    )(src, hs, *hx, dp, w, w, w, gain, shift, token)


def encoder_body(t_ref, w_ref, _, m_ref):
    m_ref[...] = dot(t_ref[...], w_ref[...]).astype(BF)


def encoder_memory(text, w, token):
    n, d = text.shape
    cols = w.shape[1]
    tile = 1024
    return pl.pallas_call(
        encoder_body,
        grid=(cols // tile,),
        in_specs=[whole((n, d)), pl.BlockSpec((d, tile), lambda j: (0, j)), ANY],
        out_specs=pl.BlockSpec((n, tile), lambda j: (0, j)),
        out_shape=jax.ShapeDtypeStruct((n, cols), BF),
        compiler_params=params(32),
        cost_estimate=cost(1.5),
        name="encoder_memory",
    )(text, w, token)


def add_two_body(a_ref, b_ref, _, out_ref):
    out_ref[...] = (a_ref[...].astype(F32) + b_ref[...].astype(F32)).astype(out_ref.dtype)


def add_two(a, b, token):
    return pl.pallas_call(
        add_two_body,
        grid=(1,),
        in_specs=[whole(a.shape), whole(a.shape), ANY],
        out_specs=whole(a.shape),
        out_shape=jax.ShapeDtypeStruct(a.shape, BF),
        compiler_params=params(60),
        cost_estimate=cost(1),
        name="add_two",
    )(a, b, token)


def add_slices_body(plan, chunk, n_in, *refs):
    inputs, outs, (scr, out_scr, in_sems, out_sems) = refs[:n_in], refs[n_in + 1 : -4], refs[-4:]
    loads = []
    for i, (_, _, terms) in enumerate(plan):
        for j, (which, first) in enumerate(terms):
            loads.append(
                pltpu.make_async_copy(inputs[which].at[pl.ds(first, chunk)], scr.at[i, j], in_sems.at[i, j])
            )
            loads[-1].start()
    stores = []
    at = 0
    for i, (which, first, terms) in enumerate(plan):
        for load in loads[at : at + len(terms)]:
            load.wait()
        at += len(terms)
        total = scr[i, 0].astype(F32)
        for j in range(1, len(terms)):
            total += scr[i, j].astype(F32)
        out_scr[i] = total.astype(BF)
        stores.append(pltpu.make_async_copy(out_scr.at[i], outs[which].at[pl.ds(first, chunk)], out_sems.at[i]))
        stores[-1].start()
    for copy in stores:
        copy.wait()


def add_slices(inputs, outs, plan, chunk, token, us, name):
    block = (chunk,) + tuple(inputs[0].shape[1:])
    terms = len(plan[0][2])
    return pl.pallas_call(
        functools.partial(add_slices_body, plan, chunk, len(inputs)),
        in_specs=[ANY] * (len(inputs) + 1),
        out_specs=[ANY] * len(outs),
        out_shape=[jax.ShapeDtypeStruct(v, BF) for v in outs],
        scratch_shapes=[
            pltpu.VMEM((len(plan), terms) + block, BF),
            pltpu.VMEM((len(plan),) + block, BF),
            pltpu.SemaphoreType.DMA((len(plan), terms)),
            pltpu.SemaphoreType.DMA((len(plan),)),
        ],
        compiler_params=params(60),
        cost_estimate=cost(us),
        name=name,
    )(*inputs, token)


def add_waiting(k1, r1, k3, r3, token, us, name):
    n = k1.shape[0]
    chunk = n // 4
    plan = []
    for first in range(0, n, chunk):
        plan += [(0, first, ((0, first), (1, n + first))), (1, first, ((2, first), (3, n + first)))]
    return add_slices((k1, r1, k3, r3), (k1.shape, k1.shape), tuple(plan), chunk, token, us, name)


def add_deep(c0, r1, r3, q1, q3, token):
    n = q1.shape[0]
    chunk = n // 4
    plan = []
    for first in range(0, n, chunk):
        plan += [(0, first, ((0, first), (3, first), (2, first))), (0, n + first, ((0, n + first), (1, first), (4, first)))]
    return add_slices((c0, r1, r3, q1, q3), (c0.shape,), tuple(plan), chunk, token, 2.5, "sum_deep")


def add_ring_body(at_ref, c0_ref, r1_ref, r3_ref, q1_ref, q3_ref, _, *refs):
    n = q1_ref.shape[0]
    first = c0_ref[:n].astype(F32) + q1_ref[...].astype(F32) + r3_ref[...].astype(F32)
    second = c0_ref[n:].astype(F32) + r1_ref[...].astype(F32) + q3_ref[...].astype(F32)
    if len(refs) == 1:
        refs[0][:n] = first.astype(BF)
        refs[0][n:] = second.astype(BF)
        return
    outs, scr = refs[:4], refs[4]
    scr[0] = first
    scr[1] = second
    for k, out in enumerate(outs):
        place = lax.rem(at_ref[0] + k, 4)
        rows = out.shape[0]
        out[...] = scr[place // 2, pl.ds(pl.multiple_of(lax.rem(place, 2) * rows, rows), rows)].astype(BF)


def add_ring(at, c0, r1, r3, q1, q3, token, cut, name):
    n = q1.shape[0]
    first = pl.BlockSpec(q1.shape, lambda i: (0,) * len(q1.shape))
    shape = (n // 2, q1.shape[1]) if cut else c0.shape
    out = jax.ShapeDtypeStruct(shape, BF)
    return pl.pallas_call(
        add_ring_body,
        grid=(1,),
        in_specs=[SMEM, whole(c0.shape), first, first, first, first, ANY],
        out_specs=[whole(shape)] * (4 if cut else 1),
        out_shape=[out] * (4 if cut else 1),
        scratch_shapes=[pltpu.VMEM((2,) + q1.shape, F32)] if cut else [],
        compiler_params=params(60),
        cost_estimate=cost(2.5),
        name=name,
    )(at, c0, r1, r3, q1, q3, token)


def add_parts_body(at_ref, a_ref, b_ref, c_ref, d_ref, _, *refs):
    outs, scr = refs[:4], refs[4]
    scr[...] = (
        (a_ref[...].astype(F32) + b_ref[...].astype(F32)) + (c_ref[...].astype(F32) + d_ref[...].astype(F32))
    ).reshape(scr.shape)
    for k, out in enumerate(outs):
        place = lax.rem(at_ref[0] + k, 4)
        rows = out.shape[0]
        out[...] = scr[pl.ds(pl.multiple_of(place * rows, rows), rows)].astype(BF)


def add_parts(at, parts, token, name):
    shape = parts[0].shape
    cols = shape[-1]
    rows = parts[0].size // cols
    out = jax.ShapeDtypeStruct((rows // 4, cols), BF)
    return pl.pallas_call(
        add_parts_body,
        grid=(1,),
        in_specs=[SMEM] + [whole(shape)] * 4 + [ANY],
        out_specs=[whole(out.shape)] * 4,
        out_shape=[out] * 4,
        scratch_shapes=[pltpu.VMEM((rows, cols), F32)],
        compiler_params=params(60),
        cost_estimate=cost(2),
        name=name,
    )(at, *parts, token)


def encoder_body(t_ref, w_ref, _, m_ref):
    m_ref[...] = dot(t_ref[...], w_ref[...]).astype(BF)


def encoder_memory(text, w, token):
    n, d = text.shape
    cols = w.shape[1]
    tile = 1024
    return pl.pallas_call(
        encoder_body,
        grid=(cols // tile,),
        in_specs=[whole((n, d)), pl.BlockSpec((d, tile), lambda j: (0, j)), ANY],
        out_specs=pl.BlockSpec((n, tile), lambda j: (0, j)),
        out_shape=jax.ShapeDtypeStruct((n, cols), BF),
        compiler_params=params(60),
        cost_estimate=cost(1.5),
        name="encoder_memory",
    )(text, w, token)


def last_triple_body(v_ref, _, out_ref, thin_ref):
    groups = 8
    d = out_ref.shape[1] // 3
    thin = jnp.zeros(thin_ref.shape, F32)
    for g in range(groups):
        total = v_ref[g].astype(F32)
        for k in range(1, v_ref.shape[0] // groups):
            total += v_ref[k * groups + g].astype(F32)
        for j in range(3):
            out_ref[:, j * d + g * 128 : j * d + g * 128 + 128] = total[:, 128 * j : 128 * j + 128]
        thin += total[:, 384:]
    thin_ref[...] = thin


def last_triple(v, token):
    _, rows, cols = v.shape
    shapes = [(rows, 8 * 384), (rows, 128)]
    return pl.pallas_call(
        last_triple_body,
        grid=(1,),
        in_specs=[whole(v.shape), ANY],
        out_specs=[whole(n) for n in shapes],
        out_shape=[jax.ShapeDtypeStruct(n, F32) for n in shapes],
        compiler_params=params(32),
        cost_estimate=cost(1),
        name="last_triple",
    )(v, token)


def last_small_body(
    a_ref, b_ref, c_ref, d_ref, zero_ref, return_ref, query_ref, output_ref, memory_ref, text_ref, gain_ref, shift_ref,
    outer_ref, inner_ref,
):
    total = (a_ref[...].astype(F32) + b_ref[...].astype(F32)) + (c_ref[...].astype(F32) + d_ref[...].astype(F32))
    first = 0
    for out in (return_ref, query_ref, output_ref, memory_ref):
        out[...] = total[:, first : first + out.shape[1]]
        first += out.shape[1]
    thin = total[:, first : first + 128]
    text_ref[...] = total[:, first + 128 :]
    rows, zero = thin.T, zero_ref[...].T
    gain_ref[...] = jnp.concatenate([zero[0:1], rows[0:1], rows[2:3]], axis=0)
    shift_ref[...] = jnp.concatenate([zero[1:2], rows[1:2], rows[3:4]], axis=0)
    outer_ref[...] = rows[4]
    of = lax.broadcasted_iota(jnp.int32, (8, 32), 0) == lax.broadcasted_iota(jnp.int32, (8, 32), 1) // 4
    lane = lax.broadcasted_iota(jnp.int32, (8, 32), 1) % 4
    spread = jnp.zeros((8, 32), F32)
    for j in range(4):
        spread += jnp.where(lane == j, thin[:, 16 + j : 17 + j], 0.0)
    inner_ref[...] = jnp.sum(jnp.where(of, spread, 0.0), axis=0)


def last_small(parts, zero):
    d = 1024
    shapes = [(8, d), (8, d), (8, d), (8, 2 * d), (8, 128), (3, 8), (3, 8), (8,), (32,)]
    return pl.pallas_call(
        last_small_body,
        grid=(1,),
        in_specs=[whole(parts[0].shape)] * 4 + [whole(zero.shape)],
        out_specs=[whole(n) for n in shapes],
        out_shape=[jax.ShapeDtypeStruct(n, F32) for n in shapes],
        compiler_params=params(32),
        cost_estimate=cost(1),
        name="last_small",
    )(*parts, zero)


def last_mlp_body(v_ref, _, up_ref, down_ref):
    total = v_ref[0].astype(F32)
    for k in range(1, v_ref.shape[0]):
        total += v_ref[k].astype(F32)
    d = down_ref.shape[1]
    for block in range(4):
        up_ref[:, block * d : (block + 1) * d] = total[8 * block : 8 * block + 8]
    down_ref[...] = total[32:]


def last_mlp(v, token):
    d = v.shape[2]
    shapes = [(8, 4 * d), (32, d)]
    return pl.pallas_call(
        last_mlp_body,
        grid=(1,),
        in_specs=[whole(v.shape), ANY],
        out_specs=[whole(n) for n in shapes],
        out_shape=[jax.ShapeDtypeStruct(n, F32) for n in shapes],
        compiler_params=params(32),
        cost_estimate=cost(1.5),
        name="last_mlp",
    )(v, token)


RINGS = {"z": "z", "x": "x", "y": ("yl", "yh")}


def ring_place(axis):
    if axis == "y":
        return lax.axis_index("yh") * 2 + lax.axis_index("yl")
    return lax.axis_index(axis)


def ring_pairs(axis, step):
    if axis == "y":
        place = (0, 2, 1, 3)
        return [(place[i], place[(i + step) % 4]) for i in range(4)]
    return [(i, (i + step) % 4) for i in range(4)]


def shift_ring(v, axis, step):
    return lax.ppermute(v, RINGS[axis], ring_pairs(axis, step))


def first_step(parts, axis):
    return shift_ring(parts[1], axis, 1), shift_ring(parts[2], axis, 3)


def second_step(parts, got, axis, token, us, name):
    q1, q3 = add_waiting(parts[3], got[0], parts[4], got[1], token, us, name)
    return shift_ring(q1, axis, 1), shift_ring(q3, axis, 3), q1


def straight(parts, axis):
    return [parts[0]] + [shift_ring(parts[k], axis, k) for k in (1, 3, 2)]


def last_sum(parts):
    total = parts[0].astype(F32)
    for p in parts[1:]:
        total = total + p.astype(F32)
    return total


def swap_yh(v):
    return lax.ppermute(v, "yh", [(0, 1), (1, 0)])


def to_partner(v):
    return lax.ppermute(v, "c", [(0, 1), (1, 0)])


def local(
    image_rows, text_states, text_segment, item_segment, norm_gain, norm_shift, triple_weight, output_weight,
    query_weight, memory_weight, return_weight, up_weight, inner_bias, down_weight, outer_bias, cotangent,
):
    items, r, d = image_rows.shape
    t = items * r
    ff = up_weight.shape[1]
    x = image_rows.reshape(t, d)
    cot = cotangent.reshape(t, d)
    core, pz, px, py = lax.axis_index("c"), lax.axis_index("z"), lax.axis_index("x"), ring_place("y")
    place = jnp.stack([core, pz, px, py]).astype(jnp.int32)
    at_z, at_x = place[1:2], place[2:3]
    yh = lax.axis_index("yh")
    tseg = text_segment.reshape(-1, 1)

    p, h1 = triple_forward(x, norm_gain, norm_shift, triple_weight)
    cot_p = to_partner(cot)
    dg, outer = act_grad(cot, down_weight, p)
    p = lax.all_to_all(p, BLK, 0, 0).reshape(8, items, r, 384)
    memory = encoder_memory(text_states, memory_weight, dg)
    h1, arrived_p = gate((h1, p[0, 0, :16, :128]), outer, cot_p[:16, :128])
    hy = swap_yh(h1)
    o = attend(p, arrived_p)
    o = lax.all_to_all(o.reshape(8, t, 128), BLK, 0, 0)
    inner, dgain2, dshift2, y1, qc, pack, gm, mail, out, dy2 = trunk(
        item_segment, place, o, x, norm_gain, norm_shift, memory, tseg, inner_bias.reshape(1, -1),
        outer_bias.reshape(1, -1), dg, cot, output_weight, query_weight, return_weight, up_weight, down_weight, hy,
    )
    mail_p, pack_p = to_partner(mail), to_partner(pack)
    b, dy1, do, dm, thin, hs = middle_back(
        item_segment, dy2, return_weight, qc, memory, tseg, query_weight, y1, norm_gain, output_weight,
        dgain2, dshift2, outer, inner, h1, hy, mail,
    )
    b_p = to_partner(b)
    do = lax.all_to_all(do, BLK, 0, 0).reshape(8, items, r, 128)
    hx1, hx3 = shift_ring(hs, "x", 1), shift_ring(hs, "x", 3)
    deep = list(mlp_grad(place, mail, mail_p, gm, cot, cot_p, b))
    deep[1], deep[2] = gate((deep[1], deep[2]), do, pack_p, b_p)
    deep_r = first_step(deep, "z")
    small = small_grad(place, pack, pack_p, b, b_p, dm, thin, text_states, memory_weight, deep[1])
    small_r = first_step(small, "y")
    (hs,) = gate((hs,), hx1, hx3, small[3])
    hx2 = shift_ring(hs, "x", 2)
    dp = attend_back(p, do, small[3])
    source = [core, px * 2 + yh]
    for k in range(4):
        sx = (px - k) % 4
        source += [sx * 2 + yh, sx * 2 + (1 - yh)]
    dp_flat = dp.reshape(8, t, 384)
    dp_home = lax.all_to_all(dp_flat, BLK, 0, 0)
    mine, theirs = triple_grad(
        jnp.stack(source).astype(jnp.int32), hs, (hx1, hx2, hx3), dp_flat, triple_weight, norm_gain, norm_shift, dp
    )
    deep_q = second_step(deep, deep_r, "z", mine, 0.02, "add_deep")
    small_q = second_step(small, small_r, "y", deep_q[2], 400, "add_small")
    part = add_two(mine, to_partner(theirs), dp_home)
    part_token = part
    part = lax.all_to_all(part.reshape(64, 8, 512), ("z", "yl", "x", "yh"), 0, 0)
    (deep_sum,) = add_deep(deep[0], *deep_r, *deep_q[:2], part_token)
    small_sum = add_ring(at_z, small[0], *small_r, *small_q[:2], deep_sum, True, "sum_small")
    triple_sum, norm_zero = last_triple(part, small_sum[0])
    small_sum = straight(small_sum, "z")
    (deep_sum,) = gate((deep_sum,), norm_zero)
    arrived = lax.all_to_all(deep_sum, ("yl", "x", "yh"), 0, 0)
    input_grad = triple_back(dp_home, triple_weight, x, norm_gain, dy1, deep_sum)
    small_sum = add_parts(at_x, small_sum, input_grad, "parts_small")
    small_sum = straight(small_sum, "x")
    return_grad, query_grad, output_grad, memory_grad, texts, gains, shifts, outer_mine, inner_mine = last_small(
        small_sum, norm_zero
    )
    up_sum, down_sum = last_mlp(arrived, norm_zero)
    return (
        out.reshape(items, r, d), input_grad.reshape(items, r, d), texts.T, gains, shifts, triple_sum, output_grad,
        query_grad, memory_grad, return_grad, up_sum, inner_mine, down_sum, outer_mine,
    )


def solution(mesh):
    fine = Mesh(mesh.devices.reshape(4, 2, 2, 4, 2), ALL)
    dp = ("z", "yl", "c")
    rows = P(dp, BLK, None)
    placed = (rows, P(), P(), P(dp)) + (P(),) * 11 + (rows,)
    outs = (
        rows, rows, P(None, ALL), P(None, ALL), P(None, ALL), P(ALL, None), P(ALL, None), P(ALL, None), P(ALL, None),
        P(ALL, None), P(ALL, None), P(ALL), P(ALL, None), P(ALL),
    )
    return jax.shard_map(local, mesh=fine, in_specs=placed, out_specs=outs, check_vma=False)
```
